32 devices in a mesh: clip: 16 (over z, y, x), frame: 2 (over core).
Axes of the slice: x: 2, y: 2, z: 4, core: 2. Of those that a mesh axis runs over, the one named last changes fastest.
Arguments:
- clip_tokens: bfloat16 [16, 8, 196, 768], P('clip', 'frame'), may hold values from -6 to 6
- clip_class: bfloat16 [16, 768], P('clip'), may hold values from -6 to 6
- output_grad: bfloat16 [16, 8, 196, 768], P('clip', 'frame'), may hold values from -6 to 6
- class_grad: bfloat16 [16, 768], P('clip'), may hold values from -6 to 6
- clip_count: int32 [16], P('clip'), may hold values from 1 to 1, as said below
- time_qkv: bfloat16 [768, 2304], P(('clip', 'frame')), may hold values from -0.21875 to 0.21875
- time_proj: bfloat16 [768, 768], P(('clip', 'frame')), may hold values from -0.625 to 0.625
- time_vec: bfloat16 [5, 768], P(None, ('clip', 'frame'))
- space_qkv: bfloat16 [768, 2304], P(('clip', 'frame')), may hold values from -0.21875 to 0.21875
- space_proj: bfloat16 [768, 768], P(('clip', 'frame')), may hold values from -1.25 to 1.25
- space_vec: bfloat16 [5, 768], P(None, ('clip', 'frame'))
- mlp_up: bfloat16 [768, 3072], P(('clip', 'frame')), may hold values from -0.21875 to 0.21875
- mlp_down: bfloat16 [3072, 768], P(('clip', 'frame')), may hold values from -0.109375 to 0.109375
- mlp_vec: bfloat16 [3, 768], P(None, ('clip', 'frame'))
- mlp_bias: bfloat16 [3072], P(('clip', 'frame')), may hold values from -3 to 3
Outputs:
- block_out: bfloat16 [16, 8, 196, 768], P('clip', 'frame')
- class_out: bfloat16 [16, 768], P('clip')
- token_grad: float32 [16, 8, 196, 768], P('clip', 'frame')
- class_in_grad: float32 [16, 768], P('clip')
- grad_time_qkv: float32 [768, 2304], P(('clip', 'frame'))
- grad_time_proj: float32 [768, 768], P(('clip', 'frame'))
- grad_time_vec: float32 [5, 768], P(None, ('clip', 'frame'))
- grad_space_qkv: float32 [768, 2304], P(('clip', 'frame'))
- grad_space_proj: float32 [768, 768], P(('clip', 'frame'))
- grad_space_vec: float32 [5, 768], P(None, ('clip', 'frame'))
- grad_mlp_up: float32 [768, 3072], P(('clip', 'frame'))
- grad_mlp_down: float32 [3072, 768], P(('clip', 'frame'))
- grad_mlp_vec: float32 [3, 768], P(None, ('clip', 'frame'))
- grad_mlp_bias: float32 [3072], P(('clip', 'frame'))
The draws below stay inside these ranges and needn't reach their ends.
Inputs may be any that keep to these rules, and one draw needn't show every extreme that they name: Clip slot s of index i of clip is live when s < clip_count[i]; with one slot per index, every clip_count is 1 and every slot is live.
All inputs are finite; a program needn't handle non-finite values.
Results may differ from the reference program's by a relative error of at most 0.015.
Values may be sent and summed in bfloat16 or wider, within the bound.
No kernel may reach another device: no remote copies, remote signals or barrier semaphores. Data moves between devices by JAX's collectives and lax.ppermute only.
A program may use at most 192 MiB of HBM per device.

```python
import jax
import jax.numpy as jnp
from jax import lax

D = 768
HEADS = 12
HEAD_DIM = 64
FF = 3072
FRAMES = 8
PLACES = 196
CLIP_DEV = 1
CLIPS = 16


def vector_rows(key, count, width):
    gain_key = jax.random.fold_in(key, 11)
    shift_key = jax.random.fold_in(key, 12)
    gains = 1.0 + 0.3 * jax.random.uniform(gain_key, (1, width), jnp.float32, -1.0, 1.0)
    shifts = 0.4 * jax.random.normal(shift_key, (count - 1, width), jnp.float32)
    return jnp.concatenate([gains, shifts], axis=0).astype(jnp.bfloat16)


def draw_time_vec(key, part):
    return vector_rows(jax.random.fold_in(key, 101), 5, D)


def draw_space_vec(key, part):
    return vector_rows(jax.random.fold_in(key, 202), 5, D)


def draw_mlp_vec(key, part):
    return vector_rows(jax.random.fold_in(key, 303), 3, D)


def draw_clip_count(key, part):
    groups = CLIPS // CLIP_DEV
    counts = jax.random.randint(jax.random.fold_in(key, 1), (groups,), 1, CLIP_DEV + 1)
    fullest = jax.random.randint(jax.random.fold_in(key, 2), (), 0, groups)
    offset = jax.random.randint(jax.random.fold_in(key, 3), (), 1, groups)
    emptiest = (fullest + offset) % groups
    counts = counts.at[fullest].set(CLIP_DEV).at[emptiest].set(1)
    return counts.astype(jnp.int32)


def block_scale(key, dims, pieces, least, top_value):
    gain = 1.0
    for dim, blocks in pieces:
        steps = jax.random.uniform(jax.random.fold_in(jax.random.fold_in(key, 6), dim), (blocks,), jnp.float32, least / len(pieces), top_value / len(pieces))
        gain = gain * jnp.repeat(jnp.exp(steps), dims[dim] // blocks).reshape((-1,) + (1,) * (len(dims) - 1 - dim))
    return gain


def bell_draw(rng, dims, scale, most, split=(), kind=jnp.bfloat16):
    entries = jax.random.normal(rng, dims, jnp.float32) * scale
    if len(split) > 0:
        entries = block_scale(rng, dims, split, -0.22, 0.18) * entries
    return jnp.clip(entries, min=-most, max=most).astype(kind)


def setup_inputs(seed: int = 0) -> dict:
    splits = jax.random.split(jax.random.key(seed), 16)
    clip_tokens = bell_draw(splits[0], (CLIPS, FRAMES, PLACES, D), 1.0, 6.0, ((0, 16), (1, 2)))
    clip_class = bell_draw(splits[1], (CLIPS, D), 1.0, 6.0, ((0, 16),))
    output_grad = bell_draw(splits[2], (CLIPS, FRAMES, PLACES, D), 1.0, 6.0, ((0, 16), (1, 2)))
    class_grad = bell_draw(splits[3], (CLIPS, D), 1.0, 6.0, ((0, 16),))
    clip_count = draw_clip_count(jax.random.fold_in(splits[15], 71), 0)
    time_qkv = bell_draw(splits[5], (D, 3 * D), D ** -0.5, 0.21875, ((0, 32),))
    time_proj = bell_draw(splits[6], (D, D), (D // 8) ** -0.5, 0.625, ((0, 32),))
    time_vec = draw_time_vec(jax.random.fold_in(splits[15], 71), 0)
    space_qkv = bell_draw(splits[8], (D, 3 * D), D ** -0.5, 0.21875, ((0, 32),))
    space_proj = bell_draw(splits[9], (D, D), (D // 32) ** -0.5, 1.25, ((0, 32),))
    space_vec = draw_space_vec(jax.random.fold_in(splits[15], 71), 0)
    mlp_up = bell_draw(splits[11], (D, FF), D ** -0.5, 0.21875, ((0, 32),))
    mlp_down = bell_draw(splits[12], (FF, D), FF ** -0.5, 0.109375, ((0, 32),))
    mlp_vec = draw_mlp_vec(jax.random.fold_in(splits[15], 71), 0)
    mlp_bias = bell_draw(splits[14], (FF,), 0.5, 3.0, ((0, 32),))
    return {"clip_tokens": clip_tokens, "clip_class": clip_class, "output_grad": output_grad, "class_grad": class_grad, "clip_count": clip_count, "time_qkv": time_qkv, "time_proj": time_proj, "time_vec": time_vec, "space_qkv": space_qkv, "space_proj": space_proj, "space_vec": space_vec, "mlp_up": mlp_up, "mlp_down": mlp_down, "mlp_vec": mlp_vec, "mlp_bias": mlp_bias}


@jax.custom_vjp
def low(v):
    return lax.optimization_barrier(v.astype(jnp.bfloat16)).astype(jnp.float32)

@jax.custom_vjp
def low_back(v):
    return v

def low_keep(v):
    return (low(v), None)

def low_pass(kept, grad):
    return (grad,)

def back_keep(v):
    return (v, None)

def back_low(kept, grad):
    return (low(grad),)
low.defvjp(low_keep, low_pass)
low_back.defvjp(back_keep, back_low)
EPSILON = 1e-06
HIGHEST = lax.Precision.HIGHEST

def layer_norm(values, scales, shifts):
    average = lax.optimization_barrier(jnp.mean(values, axis=-1, keepdims=True))
    centred = values - average
    spread = lax.optimization_barrier(jnp.mean(centred * centred, axis=-1, keepdims=True))
    return centred * lax.rsqrt(spread + EPSILON) * scales + shifts

def project(values, matrix):
    return jnp.einsum('...d,de->...e', values, matrix, precision=HIGHEST)

def attend(queries, key_rows, values):
    scores = jnp.einsum('...qhe,...khe->...hqk', queries, key_rows, precision=HIGHEST)
    scores = low_back(scores * HEAD_DIM ** (-0.5))
    softmax_weights = low(jax.nn.softmax(scores, axis=-1))
    return jnp.einsum('...hqk,...khe->...qhe', softmax_weights, values, precision=HIGHEST)

def attention_branch(tokens, matrix_in, matrix_out, vectors, over_frames):
    normed = low(layer_norm(tokens, vectors[0], vectors[1]))
    mixed_rows = project(normed, matrix_in)
    queries = low(low_back(mixed_rows[..., :D] + vectors[2]))
    key_rows = low(low_back(mixed_rows[..., D:2 * D]))
    values = low(low_back(mixed_rows[..., 2 * D:] + vectors[3]))
    head_shape = tokens.shape[:-1] + (HEADS, HEAD_DIM)
    queries = queries.reshape(head_shape)
    key_rows = key_rows.reshape(head_shape)
    values = values.reshape(head_shape)
    if over_frames:
        queries = jnp.swapaxes(queries, 0, 1)
        key_rows = jnp.swapaxes(key_rows, 0, 1)
        values = jnp.swapaxes(values, 0, 1)
    attended = attend(queries, key_rows, values)
    if over_frames:
        attended = jnp.swapaxes(attended, 0, 1)
    attended = low(low_back(attended.reshape(tokens.shape)))
    return low_back(project(attended, matrix_out) + vectors[4])

def feed_forward(tokens, matrix_up, matrix_down, vectors, up_bias):
    normed = low(layer_norm(tokens, vectors[0], vectors[1]))
    before = low_back(project(normed, matrix_up) + up_bias)
    hidden = low(jax.nn.gelu(before, approximate=False))
    return low_back(project(hidden, matrix_down) + vectors[2])

def clip_pass(tokens, class_token, params):
    time_qkv, time_proj, time_vec, space_qkv, space_proj, space_vec, mlp_up, mlp_down, mlp_vec, mlp_bias = params
    after_time = tokens + attention_branch(tokens, time_qkv, time_proj, time_vec, True)
    class_rows = jnp.broadcast_to(class_token[None, None, :], (FRAMES, 1, D))
    joined = jnp.concatenate([class_rows, after_time], axis=1)
    spatial = attention_branch(joined, space_qkv, space_proj, space_vec, False)
    places = after_time + spatial[:, 1:]
    class_mid = class_token + lax.optimization_barrier(jnp.sum(spatial[:, 0], axis=0)) * FRAMES ** (-0.5)
    outputs = places + feed_forward(places, mlp_up, mlp_down, mlp_vec, mlp_bias)
    class_result = class_mid + feed_forward(class_mid, mlp_up, mlp_down, mlp_vec, mlp_bias)
    return (outputs, class_result)

def reference(clip_tokens, clip_class, output_grad, class_grad, clip_count, time_qkv, time_proj, time_vec, space_qkv, space_proj, space_vec, mlp_up, mlp_down, mlp_vec, mlp_bias):
    weights = tuple((member.astype(jnp.float32) for member in (time_qkv, time_proj, time_vec, space_qkv, space_proj, space_vec, mlp_up, mlp_down, mlp_vec, mlp_bias)))
    slots = jnp.arange(CLIPS, dtype=jnp.int32)
    alive = (slots % CLIP_DEV < clip_count[slots // CLIP_DEV]).astype(jnp.float32)

    def whole(tokens, classes, params):
        checked = jax.checkpoint(clip_pass)

        def step(running, inputs_pair):
            return (running, checked(inputs_pair[0], inputs_pair[1], params))
        running, (outputs, class_result) = lax.scan(step, jnp.zeros((), jnp.float32), (tokens, classes))
        return (outputs * alive[:, None, None, None], class_result * alive[:, None])
    (outputs, class_result), pullback = jax.vjp(whole, clip_tokens.astype(jnp.float32), clip_class.astype(jnp.float32), weights)
    token_grad, class_in_grad, weight_grads = pullback((output_grad.astype(jnp.float32), class_grad.astype(jnp.float32)))
    return (outputs.astype(jnp.bfloat16), class_result.astype(jnp.bfloat16), token_grad, class_in_grad, weight_grads[0], weight_grads[1], weight_grads[2], weight_grads[3], weight_grads[4], weight_grads[5], weight_grads[6], weight_grads[7], weight_grads[8], weight_grads[9])
```

```python
import functools

import jax
import jax.numpy as jnp
from jax import lax
from jax.experimental import pallas as pl
from jax.experimental.pallas import tpu as pltpu
from jax.sharding import PartitionSpec as P

HEAD_DIM = 64
EPSILON = 1e-06
FLOAT = jnp.float32
BRAIN = jnp.bfloat16
LANES = 128
BLOCKS = 16
VMEM_BYTES = 56 * 1024 * 1024


def nn(left, right):
    return lax.dot_general(left, right, (((1,), (0,)), ((), ())), preferred_element_type=FLOAT)


def nt(left, right):
    return lax.dot_general(left, right, (((1,), (1,)), ((), ())), preferred_element_type=FLOAT)


def tn(left, right):
    return lax.dot_general(left, right, (((0,), (0,)), ((), ())), preferred_element_type=FLOAT)


def unit_of(values):
    average = jnp.mean(values, axis=-1, keepdims=True)
    centred = values - average
    spread = jnp.mean(centred * centred, axis=-1, keepdims=True)
    inverse = lax.rsqrt(spread + EPSILON)
    return centred * inverse, inverse


def norm_back(unit, inverse, gain, upstream):
    scaled = upstream * gain
    inner = jnp.mean(scaled, axis=-1, keepdims=True)
    along = jnp.mean(scaled * unit, axis=-1, keepdims=True)
    return inverse * (scaled - inner - unit * along)


def column_sum(values):
    return jnp.sum(values, axis=0, keepdims=True)


def row_index(shape):
    return lax.broadcasted_iota(jnp.int32, shape, 0)


def head_map(width):
    lane = lax.broadcasted_iota(jnp.int32, (width, LANES), 0) // HEAD_DIM
    head = lax.broadcasted_iota(jnp.int32, (width, LANES), 1)
    return (lane == head).astype(FLOAT).astype(BRAIN)


def head_spread(width):
    head = lax.broadcasted_iota(jnp.int32, (LANES, width), 0)
    lane = lax.broadcasted_iota(jnp.int32, (LANES, width), 1) // HEAD_DIM
    return (lane == head).astype(FLOAT).astype(BRAIN)


def load_columns(core, mine, other, held, sems):
    half = held.shape[1] // 2
    first = pltpu.make_async_copy(
        mine.at[:, :half], held.at[:, pl.ds(pl.multiple_of(core * half, LANES), half)], sems.at[0]
    )
    second = pltpu.make_async_copy(
        other.at[:, :half], held.at[:, pl.ds(pl.multiple_of((1 - core) * half, LANES), half)], sems.at[1]
    )
    first.start()
    second.start()
    return first, second


def load_mlp(core, mine, other, up, down, sems):
    cut = up.shape[2]
    copies = []
    for k, (source, slot) in enumerate(((mine, core), (other, 1 - core))):
        for t in (0, 1):
            copies.append(
                pltpu.make_async_copy(source.at[:, t * cut : (t + 1) * cut], up.at[2 * slot + t], sems.at[3 * k + t])
            )
        copies.append(pltpu.make_async_copy(source.at[:, 2 * cut :], down.at[:, slot], sems.at[3 * k + 2]))
    for copy in copies:
        copy.start()
    return copies


def wait_all(*copies):
    for group in copies:
        for copy in group:
            copy.wait()


def time_mix_kernel(own, info, tokens, vectors, w_mine, w_other, q_out, k_out, v_out, low_out, held, sems):
    step = pl.program_id(0)
    width = tokens.shape[-1]

    @pl.when(step == 0)
    def _():
        wait_all(load_columns(info[0], w_mine, w_other, held, sems))

    unit, _ = unit_of(tokens[0].astype(FLOAT))
    low = (unit * vectors[0:1] + vectors[1:2]).astype(BRAIN)
    k_out[0] = nn(low, held[:, width : 2 * width]).astype(BRAIN)
    v_out[0] = (nn(low, held[:, 2 * width :]) + vectors[3:4]).astype(BRAIN)

    @pl.when(step < own)
    def _():
        queries = (nn(low, held[:, :width]) + vectors[2:3]).astype(BRAIN)
        q_out[0] = queries * jnp.asarray(HEAD_DIM ** (-0.5), BRAIN)
        low_out[0] = low


def attention_kernel(
    places_here, info, tokens, vectors, q_in, k_in, v_in, begin, sw_mine, sw_other,
    prob_out, att_out, after_out, low_out, mixed_out, sprob_out, satt_out, places_out, class_out,
    held, sems,
):
    step = pl.program_id(0)
    frames = k_in.shape[0]
    rows, width = tokens.shape[1:]
    core = info[0]

    @pl.when(step == 0)
    def _():
        wait_all(load_columns(core, sw_mine, sw_other, held, sems))

    mapping = head_map(width)
    spread = head_spread(width)
    queries = q_in[0]
    scores = [nn(queries * k_in[g], mapping) for g in range(frames)]
    top = functools.reduce(jnp.maximum, scores)
    powers = [jnp.exp(s - top) for s in scores]
    scale = 1.0 / sum(powers)
    total = jnp.zeros((rows, width), FLOAT)
    for g in range(frames):
        prob = (powers[g] * scale).astype(BRAIN)
        prob_out[0, g] = prob
        total = total + nn(prob, spread) * v_in[g].astype(FLOAT)
    attended = total.astype(BRAIN)
    att_out[0] = attended
    place = row_index((rows, 1)) < places_here
    base = tokens[0].astype(FLOAT)
    after = jnp.where(place, base + (nn(attended, held[:, 4 * width :]) + vectors[4:5]), base)
    after_out[0] = after
    unit, _ = unit_of(after)
    low = (unit * vectors[5:6] + vectors[6:7]).astype(BRAIN)
    low_out[0] = low
    mixed_out[0, :, :width] = (
        (nn(low, held[:, :width]) + vectors[7:8]).astype(BRAIN) * jnp.asarray(HEAD_DIM ** (-0.5), BRAIN)
    )
    mixed_out[0, :, width : 2 * width] = nn(low, held[:, width : 2 * width]).astype(BRAIN)
    mixed_out[0, :, 2 * width :] = (nn(low, held[:, 2 * width : 3 * width]) + vectors[8:9]).astype(BRAIN)
    lane = lax.broadcasted_iota(jnp.int32, (1, LANES), 1)
    masks = [(lane // HEAD_DIM == e).astype(FLOAT).astype(BRAIN) for e in (0, 1)]
    key_ok = lax.broadcasted_iota(jnp.int32, (1, rows), 1) <= places_here
    for pair in range(width // LANES):
        at = pair * LANES
        q2 = mixed_out[0, :, at : at + LANES]
        k2 = mixed_out[0, :, width + at : width + at + LANES]
        v2 = mixed_out[0, :, 2 * width + at : 2 * width + at + LANES]
        result = []
        for e in (0, 1):
            logits = jnp.where(key_ok, nt(q2 * masks[e], k2), -1e30)
            power = jnp.exp(logits - jnp.max(logits, axis=-1, keepdims=True))
            prob = (power * (1.0 / jnp.sum(power, axis=-1, keepdims=True))).astype(BRAIN)
            sprob_out[0, 2 * pair + e] = prob
            result.append(nn(prob, v2))
        satt_out[0, :, at : at + LANES] = jnp.where(lane < HEAD_DIM, result[0], result[1]).astype(BRAIN)
    spatial = nn(satt_out[0], held[:, 3 * width : 4 * width]) + vectors[9:10]
    places_out[0] = jnp.where(place, after, 0.0) + spatial

    @pl.when(step == 0)
    def _():
        class_out[...] = begin[...]

    class_row = column_sum(jnp.where(row_index((rows, 1)) == places_here, spatial, 0.0))
    class_out[0:1] = class_out[0:1] + class_row


def gelu_parts(values):
    half = 0.5 + 0.5 * lax.erf(values * (0.5 ** 0.5))
    density = jnp.exp(values * values * (-0.5)) * (0.5 / 3.141592653589793) ** 0.5
    return values * half, half + values * density


def mlp_kernel(
    places_here, all_frames, info, alive, places, grads, class_row, class_own, class_far, vectors, bias,
    w_mine, w_other,
    out, low_out, hidden_out, feed_out, before_out, rows_out, sums, slopes, up, down, sems,
):
    step = pl.program_id(0)
    rows, width = places.shape[1:]
    core = info[0]

    @pl.when(step == 0)
    def _():
        sums[...] = jnp.zeros_like(sums)
        wait_all(load_mlp(core, w_mine, w_other, up, down, sems))

    class_mid = class_row[0:1] + (class_own[0:1] + class_far[0:1]) * all_frames ** (-0.5)
    class_at = row_index((rows, 1)) == places_here
    is_class = class_at & (step == pl.num_programs(0) - 1)
    kept = jnp.logical_not(class_at & (info[1] == 0))
    values = jnp.where(is_class, class_mid, places[0])
    unit, inverse = unit_of(values)
    low = (unit * vectors[10:11] + vectors[11:12]).astype(BRAIN)
    low_out[0] = low
    feed = jnp.zeros((rows, width), FLOAT)
    chunks = hidden_out.shape[-1] // width
    per = down.shape[0] // chunks
    for j in range(chunks):
        before = nn(low, up[j].reshape(width, width)) + bias[j : j + 1]
        hidden, slope = gelu_parts(before)
        hidden = hidden.astype(BRAIN)
        hidden_out[0, :, j * width : (j + 1) * width] = hidden
        slopes[j] = slope
        feed = feed + nn(hidden, down[j * per : (j + 1) * per].reshape(width, width))
    out[0] = ((values + (feed + vectors[12:13])) * alive[0]).astype(BRAIN)

    row_grad = grads[0].astype(FLOAT) * alive[0]
    feed_grad = row_grad.astype(BRAIN)
    feed_kept = jnp.where(kept, row_grad, 0.0).astype(BRAIN)
    feed_out[0] = feed_kept
    sums[2:3] = sums[2:3] + column_sum(feed_kept.astype(FLOAT))
    upstream = jnp.zeros((rows, width), FLOAT)
    for j in range(chunks):
        hidden_grad = nt(feed_grad, down[j * per : (j + 1) * per].reshape(width, width))
        before_grad = (hidden_grad * slopes[j]).astype(BRAIN)
        before_kept = jnp.where(kept, before_grad.astype(FLOAT), 0.0)
        before_out[0, :, j * width : (j + 1) * width] = before_kept.astype(BRAIN)
        sums[3 + j : 4 + j] = sums[3 + j : 4 + j] + column_sum(before_kept)
        upstream = upstream + nt(before_grad, up[j].reshape(width, width))
    rows_out[0] = row_grad + norm_back(unit, inverse, vectors[10:11], upstream)
    upstream = jnp.where(kept, upstream, 0.0)
    sums[0:1] = sums[0:1] + column_sum(upstream * unit)
    sums[1:2] = sums[1:2] + column_sum(upstream)


def space_back_kernel(
    places_here, all_frames, info, rows_grad, class_grad, after, mixed, sprob, vectors, begin,
    sw_mine, sw_other,
    branch_out, mixed_out, after_out, time_out, att_out, sums, held, sems,
):
    step = pl.program_id(0)
    rows, width = after.shape[1:]
    core = info[0]

    @pl.when(step == 0)
    def _():
        sums[...] = begin[...]
        wait_all(load_columns(core, sw_mine, sw_other, held, sems))

    index = row_index((rows, 1))
    place = index < places_here
    class_at = index == places_here
    offset = places_here % 16
    share = class_grad[0, offset : offset + 1] * all_frames ** (-0.5)
    direct = jnp.where(place, rows_grad[0], 0.0)
    branch = jnp.where(class_at, share, direct).astype(BRAIN)
    branch_out[0] = branch
    sums[4:5] = sums[4:5] + column_sum(branch.astype(FLOAT))
    att_grad = nt(branch, held[:, 3 * width : 4 * width]).astype(BRAIN)
    lane = lax.broadcasted_iota(jnp.int32, (1, LANES), 1)
    masks = [(lane // HEAD_DIM == e).astype(FLOAT).astype(BRAIN) for e in (0, 1)]
    for pair in range(width // LANES):
        at = pair * LANES
        a2 = att_grad[:, at : at + LANES]
        q2 = mixed[0, :, at : at + LANES]
        k2 = mixed[0, :, width + at : width + at + LANES]
        v2 = mixed[0, :, 2 * width + at : 2 * width + at + LANES]
        queries, key_rows, value_rows = [], [], []
        for e in (0, 1):
            prob = sprob[0, 2 * pair + e]
            wide = prob.astype(FLOAT)
            prob_grad = nt(a2 * masks[e], v2)
            weighted = wide * prob_grad
            rowdot = jnp.sum(weighted, axis=-1, keepdims=True)
            score = (weighted - wide * rowdot).astype(BRAIN)
            queries.append(nn(score, k2))
            key_rows.append(tn(score, q2))
            value_rows.append(tn(prob, a2))
        left = lane < HEAD_DIM
        q_grad = (jnp.where(left, queries[0], queries[1]) * HEAD_DIM ** (-0.5)).astype(BRAIN)
        v_grad = jnp.where(left, value_rows[0], value_rows[1]).astype(BRAIN)
        mixed_out[0, :, at : at + LANES] = q_grad
        mixed_out[0, :, width + at : width + at + LANES] = jnp.where(left, key_rows[0], key_rows[1]).astype(BRAIN)
        mixed_out[0, :, 2 * width + at : 2 * width + at + LANES] = v_grad
    sums[2:3] = sums[2:3] + column_sum(mixed_out[0, :, :width].astype(FLOAT))
    sums[3:4] = sums[3:4] + column_sum(mixed_out[0, :, 2 * width :].astype(FLOAT))
    upstream = nt(mixed_out[0], held[:, : 3 * width])
    unit, inverse = unit_of(after[0])
    inner = norm_back(unit, inverse, vectors[5:6], upstream)
    sums[0:1] = sums[0:1] + column_sum(upstream * unit)
    sums[1:2] = sums[1:2] + column_sum(upstream)
    sums[6:7] = sums[6:7] + column_sum(jnp.where(class_at, inner, 0.0))
    after_grad = jnp.where(place, direct + inner, 0.0)
    after_out[0] = after_grad
    low = after_grad.astype(BRAIN)
    time_out[0] = low
    sums[5:6] = sums[5:6] + column_sum(low.astype(FLOAT))
    att_out[0] = nt(low, held[:, 4 * width :]).astype(BRAIN)


def time_back_kernel(q_in, k_in, v_in, prob_in, att_in, q_out, own_out, far_out):
    own, rows, width = q_in.shape
    frames = k_in.shape[0]
    mapping = head_map(width)
    spread = head_spread(width)
    size = 16

    def chunk(index, carry):
        at = pl.ds(pl.multiple_of(index * size, size), size)
        values = [v_in[g, at] for g in range(frames)]
        att = [att_in[f, at] for f in range(own)]
        products = jnp.concatenate([att[f] * values[g] for f in range(own) for g in range(frames)], axis=0)
        prob_grad = nn(products, mapping)
        probs = [prob_in[f, g, at] for f in range(own) for g in range(frames)]
        scores = []
        for f in range(own):
            wide = [probs[f * frames + g].astype(FLOAT) for g in range(frames)]
            weighted = [
                wide[g] * prob_grad[(f * frames + g) * size : (f * frames + g + 1) * size] for g in range(frames)
            ]
            rowdot = sum(weighted)
            scores += [(weighted[g] - wide[g] * rowdot).astype(BRAIN) for g in range(frames)]
        score_wide = nn(jnp.concatenate(scores, axis=0), spread)
        prob_wide = nn(jnp.concatenate(probs, axis=0), spread)

        def part(array, f, g):
            return array[(f * frames + g) * size : (f * frames + g + 1) * size]

        for f in range(own):
            total = sum(part(score_wide, f, g) * k_in[g, at].astype(FLOAT) for g in range(frames))
            q_out[f, at] = (total * HEAD_DIM ** (-0.5)).astype(BRAIN)
        queries = [q_in[f, at].astype(FLOAT) for f in range(own)]
        wide_att = [a.astype(FLOAT) for a in att]
        for g in range(frames):
            key_grad = sum(part(score_wide, f, g) * queries[f] for f in range(own)).astype(BRAIN)
            value_grad = sum(part(prob_wide, f, g) * wide_att[f] for f in range(own)).astype(BRAIN)
            if g < own:
                own_out[0, g, at] = key_grad
                own_out[1, g, at] = value_grad
            else:
                far_out[0, g - own, at] = key_grad
                far_out[1, g - own, at] = value_grad
        return carry

    lax.fori_loop(0, rows // size, chunk, 0)


def time_mix_back_kernel(info, tokens, vectors, mixed, after_grad, w_mine, w_other, token_out, sums, held, sems):
    step = pl.program_id(0)
    width = tokens.shape[-1]

    @pl.when(step == 0)
    def _():
        sums[...] = jnp.zeros_like(sums)
        wait_all(load_columns(info[0], w_mine, w_other, held, sems))

    sums[2:3] = sums[2:3] + column_sum(mixed[0, :, :width].astype(FLOAT))
    sums[3:4] = sums[3:4] + column_sum(mixed[0, :, 2 * width :].astype(FLOAT))
    upstream = nt(mixed[0], held[...])
    unit, inverse = unit_of(tokens[0].astype(FLOAT))
    token_out[0] = after_grad[0] + norm_back(unit, inverse, vectors[0:1], upstream)
    sums[0:1] = sums[0:1] + column_sum(upstream * unit)
    sums[1:2] = sums[1:2] + column_sum(upstream)


def time_outer_kernel(info, left, right, sums, out):
    half = right.shape[1]
    out[:, :half] = tn(left[...], right[...]).astype(BRAIN)
    out[:, half:] = sums[...].astype(BRAIN)


def space_outer_kernel(info, low, mixed, att, branch, time_att, time_grad, out):
    width = low.shape[1]
    half = out.shape[1]
    rest = 3 * width - half

    @pl.when(info[0] == 0)
    def _():
        out[...] = tn(low[...], mixed[:, :half]).astype(BRAIN)

    @pl.when(info[0] == 1)
    def _():
        out[:, :rest] = tn(low[...], mixed[:, half:]).astype(BRAIN)
        out[:, rest : rest + width] = tn(att[...], branch[...]).astype(BRAIN)
        out[:, rest + width :] = tn(time_att[...], time_grad[...]).astype(BRAIN)


def mlp_outer_kernel(info, low, before, hidden, feed, mine, other):
    step = pl.program_id(0)
    blocks, total, width = mine.shape
    cut = total // 4
    per = blocks // pl.num_programs(0)
    part = tn(low[...], before[...]).astype(BRAIN).reshape(blocks, cut, width)
    at = pl.ds(pl.multiple_of((step % 2) * cut, 16), cut)
    is_mine = step // 2 == info[0]

    @pl.when(is_mine)
    def _():
        mine[:, at] = part

    @pl.when(jnp.logical_not(is_mine))
    def _():
        other[:, at] = part

    value = tn(hidden[...], feed[...]).astype(BRAIN).reshape(per, 2, 2 * cut, width)
    first = info[0] == 0
    rows = pl.ds(pl.multiple_of(step * per, per), per)
    mine[rows, 2 * cut :] = jnp.where(first, value[:, 0], value[:, 1])
    other[rows, 2 * cut :] = jnp.where(first, value[:, 1], value[:, 0])


def smem():
    return pl.BlockSpec(memory_space=pltpu.SMEM)


def hbm():
    return pl.BlockSpec(memory_space=pl.ANY)


def whole(shape):
    return pl.BlockSpec(shape, lambda *_: (0,) * len(shape))


def per_frame(shape, first=0):
    return pl.BlockSpec((1,) + shape[1:], lambda s: (s + first,) + (0,) * (len(shape) - 1))


def sds(shape, kind):
    return jax.ShapeDtypeStruct(shape, kind)


def call(kernel, grid, inputs, outputs, scratch=(), flops=0, nbytes=0, deps=(), previous=(), prefetch=0):
    count = len(inputs)
    skip = len(previous) + len(deps)

    def inner(*refs):
        kernel(*refs[:count], *refs[count + skip :])

    specs = [spec for spec, _ in inputs[prefetch:]] + [hbm()] * skip
    common = dict(
        out_shape=[shape for _, shape in outputs],
        compiler_params=pltpu.CompilerParams(vmem_limit_bytes=VMEM_BYTES),
        input_output_aliases={count + n: n for n in range(len(previous))},
        cost_estimate=pl.CostEstimate(flops=1, bytes_accessed=1, transcendentals=0),
    )
    places = dict(grid=grid, in_specs=specs, out_specs=[spec for spec, _ in outputs], scratch_shapes=list(scratch))
    if prefetch:
        common["grid_spec"] = pltpu.PrefetchScalarGridSpec(num_scalar_prefetch=prefetch, **places)
    else:
        common.update(places)
    return pl.pallas_call(inner, **common)(*[array for _, array in inputs], *previous, *deps)


def time_outer(slot, left, right, sums, deps=()):
    rows, width = left.shape
    half = right.shape[1] // 2
    shape = (width, half + sums.shape[1])
    return call(
        time_outer_kernel, (1,),
        [
            (None, slot),
            (pl.BlockSpec((rows, width), lambda s, info: (0, 0)), left),
            (pl.BlockSpec((rows, half), lambda s, info: (0, info[0])), right),
            (pl.BlockSpec(sums.shape, lambda s, info: (0, 0)), sums),
        ],
        [(pl.BlockSpec(shape, lambda s, info: (0, 0)), sds(shape, BRAIN))],
        flops=2 * rows * width * half, nbytes=4 * rows * (width + half), deps=deps, prefetch=1,
    )[0]


def space_outer(slot, *operands, deps=()):
    rows, width = operands[0].shape
    half = width * 5 // 2
    return call(
        space_outer_kernel, (1,),
        [(smem(), slot)] + [(whole(v.shape), v) for v in operands],
        [(whole((width, half)), sds((width, half), BRAIN))],
        flops=2 * rows * width * half, nbytes=4 * rows * (width + half), deps=deps,
    )[0]


def mlp_outer(slot, low, before, hidden, feed, deps=()):
    rows, width = low.shape
    wide = hidden.shape[1]
    shape = (BLOCKS, 4 * (width // BLOCKS), width)
    fixed = pl.BlockSpec((rows, width), lambda s, info: (0, 0))
    moving = pl.BlockSpec((rows, width), lambda s, info: (0, s))
    return call(
        mlp_outer_kernel, (wide // width,),
        [(None, slot), (fixed, low), (moving, before), (moving, hidden), (fixed, feed)],
        [(pl.BlockSpec(shape, lambda s, info: (0, 0, 0)), sds(shape, BRAIN))] * 2,
        flops=4 * rows * width * wide, nbytes=4 * rows * (wide + width), deps=deps, prefetch=1,
    )


def gate(value, deps):
    return pl.pallas_call(
        lambda source, *refs: None,
        in_specs=[hbm()] * (1 + len(deps)),
        out_specs=hbm(),
        out_shape=sds(value.shape, value.dtype),
        input_output_aliases={0: 0},
    )(value, *deps)


def stack_kernel(*refs):
    for n, ref in enumerate(refs[:-1]):
        refs[-1][n] = ref[...]


def add_kernel(left, right, out):
    out[...] = left[...] + right[...]


def add_after(left, right, deps):
    inputs = [(whole(left.shape), left), (whole(right.shape), right)]
    return call(add_kernel, (1,), inputs, [(whole(left.shape), sds(left.shape, left.dtype))], deps=deps)[0]


def assemble_kernel(info, o4, rx, ry, ra, rb, out):
    depth = info[2]
    plane = info[3]
    for m in range(4):
        for n in range(4):
            if n < 3:
                value = (o4, rx, ry)[n][m]
            else:
                value = ra[m] if m < 2 else rb[m - 2]
            out[(depth ^ m) * 4 + (plane ^ n)] = value


def pack_kernel(info, time_qkv, space_qkv, space_proj, time_proj, up, time_vec, space_vec, mlp_vec, bias, send, keep):
    width = time_proj.shape[1]
    half = width // 2
    pieces = [time_qkv[:, n * half : (n + 1) * half] for n in range(6)]
    pieces += [space_qkv[:, n * half : (n + 1) * half] for n in range(6)]
    pieces += [space_proj[:, :half], space_proj[:, half:], time_proj[:, :half], time_proj[:, half:]]
    pieces += [up[:, n * half : (n + 1) * half] for n in range(8)]
    first = info[0] == 0
    at = 0
    for begin, count in ((0, 3), (6, 5), (16, 4)):
        for n in range(count):
            low, high = pieces[begin + n], pieces[begin + count + n]
            keep[:, at : at + half] = jnp.where(first, low, high)
            send[:, at : at + half] = jnp.where(first, high, low)
            at += half
    line = 0
    total = jnp.zeros((keep.shape[0], LANES), FLOAT)
    for source in (time_vec, space_vec, mlp_vec, bias):
        count = source.shape[0]
        lane = lax.broadcasted_iota(jnp.int32, (count, LANES), 1)
        chosen = (lane == row_index((count, LANES)) + line).astype(FLOAT)
        total = total + lax.dot_general(
            source[...].astype(FLOAT), chosen, (((0,), (0,)), ((), ())), preferred_element_type=FLOAT
        )
        line += count
    keep[:, at:] = total.astype(BRAIN)
    send[:, at:] = total.astype(BRAIN)


def turn_kernel(source, out):
    out[...] = source[...].astype(FLOAT).T


def join_kernel(info, keep, come, down, time_out, space_out, mlp_out):
    first = info[0] == 0
    width = down.shape[1]
    mine, far = keep[...].astype(FLOAT), come[...].astype(FLOAT)
    both = jnp.concatenate([jnp.where(first, mine, far), jnp.where(first, far, mine)], axis=0).astype(BRAIN)
    cut = both.shape[0]
    end = time_out.shape[1] - LANES
    time_out[:, :end] = both[:, :end]
    time_out[:, end:] = both[:, both.shape[1] - LANES :]
    space_out[...] = both[:, end : end + space_out.shape[1]]
    at = end + space_out.shape[1]
    mlp_out[:cut] = both[:, at : at + width]
    mlp_out[cut : 2 * cut] = both[:, at + width : at + 2 * width]
    mlp_out[2 * cut :] = down[...]


def added(*values):
    return sum(v.astype(FLOAT) for v in values).astype(BRAIN)


def reduce_first_kernel(info, mine, far, to_y, to_x, near_x, near_y, own):
    step = pl.program_id(0)
    plane = info[3]
    own[0] = added(mine[0, plane], far[0, plane])
    near_x[0] = added(mine[0, plane ^ 1], far[0, plane ^ 1])
    near_y[0] = added(mine[0, plane ^ 2], far[0, plane ^ 2])
    diagonal = added(mine[0, plane ^ 3], far[0, plane ^ 3])

    @pl.when(step < 2)
    def _():
        to_y[0] = diagonal

    @pl.when(step >= 2)
    def _():
        to_x[0] = diagonal


def reduce_second_kernel(near_x, near_y, from_y, from_x, out_x, out_y):
    step = pl.program_id(0)

    @pl.when(step < 2)
    def _():
        out_x[0] = added(near_x[0], from_y[0])
        out_y[0] = near_y[0]

    @pl.when(step >= 2)
    def _():
        out_x[0] = near_x[0]
        out_y[0] = added(near_y[0], from_x[0])


def reduce_third_kernel(info, own, from_x, from_y, first, second, others):
    for m in range(4):
        at = info[2] ^ m
        value = added(own[at], from_x[at], from_y[at])
        if m == 0:
            first[...] = value
        elif m == 1:
            second[...] = value
        else:
            others[m - 2] = value


def reduce_fourth_kernel(first, second, come, first_out, second_out):
    first_out[...] = first[...].astype(FLOAT) + come[0].astype(FLOAT)
    second_out[...] = added(second[...], come[1])


def clip_swap(values, bits, count):
    return lax.ppermute(values, "clip", [(i, i ^ bits) for i in range(count)])


def core_swap(values):
    return lax.ppermute(values, "frame", [(0, 1), (1, 0)])


class Near:
    def __init__(self, clips, info):
        self.clips = clips
        self.info = info
        self.core = lax.axis_index("frame")

    def swap(self, values, bits):
        return clip_swap(values, bits, self.clips)

    def in_order(self, mine, far, axis):
        return jnp.where(
            self.core == 0, jnp.concatenate([mine, far], axis=axis), jnp.concatenate([far, mine], axis=axis)
        )

    def stack(self, pieces, deps):
        shape = (len(pieces),) + pieces[0].shape
        return call(
            stack_kernel, (1,), [(whole(v.shape), v) for v in pieces], [(whole(shape), sds(shape, BRAIN))],
            nbytes=4 * len(pieces) * pieces[0].size, deps=deps,
        )[0]

    def depth_direct(self, own, deps):
        return self.stack([own] + [self.swap(own, 4 * m) for m in (1, 2, 3)], deps)

    def depth_near(self, own, deps):
        return self.stack([own, self.swap(own, 4)], deps)

    def depth_far(self, two, deps):
        come = self.swap(two, 8)
        return self.stack([two[0], two[1], come[0], come[1]], deps)

    def plane_step(self, o4, deps):
        rx = self.swap(o4, 1)
        ry = self.swap(o4, 2)
        if deps:
            rx, ry = gate(rx, deps), gate(ry, deps)
        return rx, ry, rx[:2], ry[2:]

    def diagonal_step(self, o4, planes, deps):
        rx, ry, sx, sy = planes
        pieces = (o4, rx, ry, self.swap(sx, 2), self.swap(sy, 1))
        shape = (self.clips,) + o4.shape[1:]
        return call(
            assemble_kernel, (1,), [(smem(), self.info)] + [(whole(v.shape), v) for v in pieces],
            [(whole(shape), sds(shape, BRAIN))], nbytes=16 * o4.size, deps=deps,
        )[0]

    def reduce_first(self, mine, far, deps):
        block = mine.shape[1:]
        four = (4, 4) + block
        view = pl.BlockSpec((1, 4) + block, lambda s: (s, 0, 0, 0))
        one = lambda pick: pl.BlockSpec((1,) + block, lambda s: (pick(s), 0, 0))
        each = (one(lambda s: s), sds((4,) + block, BRAIN))
        return call(
            reduce_first_kernel, (4,),
            [(smem(), self.info), (view, mine.reshape(four)), (view, far.reshape(four))],
            [
                (one(lambda s: jnp.minimum(s, 1)), sds((2,) + block, BRAIN)),
                (one(lambda s: jnp.maximum(s - 2, 0)), sds((2,) + block, BRAIN)),
                each, each, each,
            ],
            nbytes=6 * mine.size, deps=deps,
        )

    def reduce_second(self, near_x, near_y, to_y, to_x, deps):
        from_y, from_x = self.swap(to_y, 2), self.swap(to_x, 1)
        block = near_x.shape[1:]
        one = lambda pick: pl.BlockSpec((1,) + block, lambda s: (pick(s), 0, 0))
        each = one(lambda s: s)
        return call(
            reduce_second_kernel, (4,),
            [
                (each, near_x), (each, near_y), (one(lambda s: jnp.minimum(s, 1)), from_y),
                (one(lambda s: jnp.maximum(s - 2, 0)), from_x),
            ],
            [(each, sds(near_x.shape, BRAIN))] * 2, nbytes=10 * near_x.size, deps=deps,
        )

    def reduce_third(self, own, near_x, near_y, deps):
        from_x, from_y = self.swap(near_x, 1), self.swap(near_y, 2)
        block = own.shape[1:]
        return call(
            reduce_third_kernel, (1,),
            [(smem(), self.info)] + [(whole(v.shape), v) for v in (own, from_x, from_y)],
            [(whole(shape), sds(shape, BRAIN)) for shape in (block, block, (2,) + block)],
            nbytes=8 * own.size, deps=deps,
        )

    def reduce_fourth(self, first, second, others, deps):
        come = self.swap(others, 8)
        inputs = [(whole(v.shape), v) for v in (first, second, come)]
        outs = [(whole(first.shape), sds(first.shape, kind)) for kind in (FLOAT, BRAIN)]
        return call(reduce_fourth_kernel, (1,), inputs, outs, nbytes=8 * first.size, deps=deps)

    def reduce_end(self, first, second):
        return first + self.swap(second, 4).astype(FLOAT)

    def reduce_direct(self, first, second, others):
        total = first.astype(FLOAT) + self.swap(second, 4).astype(FLOAT)
        return total + self.swap(others[0], 8).astype(FLOAT) + self.swap(others[1], 12).astype(FLOAT)

    def owner_rows(self, value):
        rows = value.shape[0] // 2
        mine = lax.dynamic_slice_in_dim(value, self.core * rows, rows, 0)
        theirs = lax.dynamic_slice_in_dim(value, (1 - self.core) * rows, rows, 0)
        return self.in_order(mine, core_swap(theirs), 1)


AXES = ("clip", "frame")


def body(
    clips, cores, clip_tokens, clip_class, output_grad, class_grad, clip_count,
    time_qkv, time_proj, time_vec, space_qkv, space_proj, space_vec, mlp_up, mlp_down, mlp_vec, mlp_bias,
):
    _, own, places_here, width = clip_tokens.shape
    rows = -(-(places_here + 1) // 16) * 16
    frames = own * cores
    wide = mlp_up.shape[1]
    cut = width // BLOCKS
    core = lax.axis_index("frame")
    place = lax.axis_index("clip")
    shard = place * cores + core
    leader = (core == 0).astype(jnp.int32)
    alive = (jnp.arange(1, dtype=jnp.int32) < clip_count[0]).astype(FLOAT)
    is_near = clips == 16 and cores == 2
    slot = core if is_near else core * 0
    info = jnp.stack([slot, leader, place // 4, place % 4, shard]).astype(jnp.int32)
    near = Near(clips, info) if is_near else None
    my_slot = info[0:1]
    far_slot = 1 - my_slot

    class_block = jnp.broadcast_to(clip_class[0][None, None], (own, 1, width))
    blank = jnp.zeros((own, rows - places_here - 1, width), BRAIN)
    tokens = jnp.concatenate([clip_tokens[0], class_block, blank], axis=1)
    last = (jnp.arange(own) == own - 1)[:, None, None]
    class_rows = jnp.where(last, class_grad[0][None, None], jnp.zeros((), BRAIN))
    grads = jnp.concatenate([output_grad[0], class_rows, blank], axis=1)

    bias_rows = wide // width
    zeros = jnp.zeros((8, width), FLOAT)
    flat = lambda v: v.reshape((own * rows,) + v.shape[2:])

    if near is not None:
        packed = (
            time_qkv, space_qkv, space_proj, time_proj, mlp_up, time_vec, space_vec, mlp_vec,
            mlp_bias.reshape(-1, bias_rows).T,
        )
        line = sds((time_qkv.shape[0], 6 * width + LANES), BRAIN)
        send, keep = call(
            pack_kernel, (1,), [(smem(), info)] + [(whole(v.shape), v) for v in packed],
            [(whole(line.shape), line), (whole(line.shape), line)],
        )
        shapes = [(cut, 3 * width // 2 + LANES), (cut, 5 * width // 2), (4 * cut, width)]
        time_own, space_own, mlp_own = call(
            join_kernel, (1,),
            [(smem(), info)] + [(whole(v.shape), v) for v in (keep, core_swap(send), mlp_down)],
            [(whole(shape), sds(shape, BRAIN)) for shape in shapes],
        )
        join = lambda two: tuple(h.reshape(width, h.shape[-1]) for h in two)
        time_line = near.depth_direct(time_own, [])
        all_tokens = jnp.concatenate([tokens, core_swap(gate(tokens, [time_own]))], axis=0)
        space_own = gate(space_own, [time_line])
        space_line = near.depth_direct(space_own, [])
        time_mine = near.diagonal_step(time_line, near.plane_step(time_line, []), [grads, all_tokens, space_line])
        space_line = gate(space_line, [time_mine])
        time_far = core_swap(time_mine)
        time_w = join((time_mine, time_far))
        vec_block = pl.BlockSpec((width, LANES), lambda s: (0, time_w[0].shape[1] // LANES - 1))
        vectors = call(
            turn_kernel, (1,), [(vec_block, time_w[0])], [(whole((LANES, width)), sds((LANES, width), FLOAT))],
            deps=[space_line],
        )[0]
        n_vec = time_vec.shape[0] + space_vec.shape[0] + mlp_vec.shape[0]
        bias = vectors[n_vec : n_vec + bias_rows].T.reshape(bias_rows, width)
        mlp_own = gate(mlp_own, [time_far, space_line])
        mix_deps = [space_line, mlp_own]
    else:
        everywhere = lax.all_gather(tokens, "frame", axis=0, tiled=True)
        all_tokens = jnp.roll(everywhere, -core * own, axis=0)
        vec_shard = jnp.concatenate([time_vec, space_vec, mlp_vec], axis=0)
        blank_rows = jnp.zeros((16 - vec_shard.shape[0], width), FLOAT)
        space_shard = jnp.concatenate([space_qkv, space_proj, time_proj], axis=1)
        vectors = lax.all_gather(vec_shard, AXES, axis=1, tiled=True).astype(FLOAT)
        bias = lax.all_gather(mlp_bias, AXES, axis=0, tiled=True).astype(FLOAT).reshape(bias_rows, width)
        vectors = jnp.concatenate([vectors, blank_rows], axis=0)

        def halves(value):
            full = lax.all_gather(value, AXES, axis=0, tiled=True)
            half = full.shape[1] // 2
            return full[:, :half], full[:, half:]

        time_w, space_w = halves(time_qkv), halves(space_shard)
        up = lax.all_gather(mlp_up, AXES, axis=0, tiled=True).reshape(BLOCKS, cut, 2, 2, width)
        up = jnp.transpose(up, (2, 0, 3, 1, 4)).reshape(2, BLOCKS, 2 * cut, width)
        down = lax.all_gather(mlp_down, AXES, axis=0, tiled=True).reshape(BLOCKS, 2, 2 * cut, width)
        mlp_w = tuple(jnp.concatenate([up[n], down[:, n]], axis=1) for n in (0, 1))
        mix_deps = []

    frame_shape = (own, rows, width)
    all_shape = (frames, rows, width)
    heads = width // HEAD_DIM
    prob_shape = (own, frames, rows, LANES)
    sprob_shape = (own, heads, rows, rows)
    mixed_shape = (own, rows, 3 * width)
    hidden_shape = (own, rows, wide)
    sum_out = (whole((8, width)), sds((8, width), FLOAT))
    row_bytes = own * rows * width
    square = 2 * own * rows * width * width
    low_out = lambda shape, first=0: (per_frame(shape, first), sds(shape, BRAIN))
    wide_out = lambda shape, first=0: (per_frame(shape, first), sds(shape, FLOAT))
    vec_in = (whole(vectors.shape), vectors)
    pair = lambda two: [(hbm(), two[0]), (hbm(), two[1])]
    time_held = [pltpu.VMEM((width, 3 * width), BRAIN), pltpu.SemaphoreType.DMA((2,))]
    space_held = [pltpu.VMEM((width, 5 * width), BRAIN), pltpu.SemaphoreType.DMA((2,))]
    mlp_held = [
        pltpu.VMEM((wide // width, BLOCKS, cut, width), BRAIN),
        pltpu.VMEM((BLOCKS, 2, 2 * cut, width), BRAIN),
        pltpu.SemaphoreType.DMA((6,)),
    ]

    own_map = pl.BlockSpec((1, rows, width), lambda s: (jnp.minimum(s, own - 1), 0, 0))
    queries, key_rows, value_rows, time_low = call(
        functools.partial(time_mix_kernel, own), (frames,),
        [(smem(), info), (per_frame(all_shape), all_tokens), vec_in] + pair(time_w),
        [(own_map, sds(frame_shape, BRAIN)), low_out(all_shape), low_out(all_shape), (own_map, sds(frame_shape, BRAIN))],
        time_held, flops=5 * square, nbytes=20 * row_bytes, deps=mix_deps,
    )

    if near is not None:
        mlp_line = near.depth_direct(mlp_own, [])
        space_mine = near.diagonal_step(space_line, near.plane_step(space_line, [queries, mlp_line]), [])
        space_w = join((space_mine, core_swap(space_mine)))
        mlp_line = gate(mlp_line, [space_mine])

    parts = [(0, own)] if near is None else [(0, own // 2), (own // 2, own - own // 2)]
    deps = [] if near is None else [mlp_line]
    kept, class_own = (), zeros
    for first, count in parts:
        outs = call(
            functools.partial(attention_kernel, places_here), (count,),
            [
                (smem(), info), (per_frame(frame_shape, first), tokens), vec_in, (per_frame(frame_shape, first), queries),
                (whole(all_shape), key_rows), (whole(all_shape), value_rows), (whole((8, width)), class_own),
            ]
            + pair(space_w),
            [
                low_out(prob_shape, first), low_out(frame_shape, first), wide_out(frame_shape, first),
                low_out(frame_shape, first), low_out(mixed_shape, first), low_out(sprob_shape, first),
                low_out(frame_shape, first), wide_out(frame_shape, first), sum_out,
            ],
            space_held, flops=15 * square * count // own, nbytes=40 * row_bytes * count // own,
            deps=deps, previous=kept,
        )
        kept, class_own = tuple(outs[:-1]), outs[-1]
        if near is not None and first == 0:
            mlp_planes = near.plane_step(mlp_line, [class_own])
            deps = list(mlp_planes[2:])
    time_prob, time_att, after, space_low, space_mixed, space_prob, space_att, places = kept

    if near is not None:
        mlp_mine = near.diagonal_step(mlp_line, mlp_planes, [places])
        mlp_w = (mlp_mine, core_swap(mlp_mine))
        class_far = core_swap(class_own)
    else:
        class_far = lax.psum(class_own, "frame") - class_own
    class_row = jnp.broadcast_to(clip_class.astype(FLOAT), (8, width))
    small = whole((8, width))
    result, mlp_low, hidden, feed_grad, before_grad, rows_grad, mlp_sums = call(
        functools.partial(mlp_kernel, places_here, frames), (own,),
        [
            (smem(), info), (smem(), alive), (per_frame(frame_shape), places), (per_frame(frame_shape), grads),
            (small, class_row), (small, class_own), (small, class_far), vec_in, (whole(bias.shape), bias),
        ]
        + pair(mlp_w),
        [
            low_out(frame_shape), low_out(frame_shape), low_out(hidden_shape), low_out(frame_shape),
            low_out(hidden_shape), wide_out(frame_shape), sum_out,
        ],
        [pltpu.VMEM((wide // width, rows, width), FLOAT)] + mlp_held,
        flops=30 * square, nbytes=40 * row_bytes,
    )

    mlp_mine, mlp_far = mlp_outer(my_slot, flat(mlp_low), flat(before_grad), flat(hidden), flat(feed_grad))
    class_block_at = places_here // 16
    class_spec = pl.BlockSpec((1, 16, width), lambda s: (own - 1, class_block_at, 0))

    def space_back(first, count, sums, deps, previous):
        return call(
            functools.partial(space_back_kernel, places_here, frames), (count,),
            [
                (smem(), info), (per_frame(frame_shape, first), rows_grad), (class_spec, rows_grad),
                (per_frame(frame_shape, first), after), (per_frame(mixed_shape, first), space_mixed),
                (per_frame(sprob_shape, first), space_prob), vec_in, (small, sums),
            ]
            + pair(space_w),
            [
                low_out(frame_shape, first), low_out(mixed_shape, first), wide_out(frame_shape, first),
                low_out(frame_shape, first), low_out(frame_shape, first), sum_out,
            ],
            space_held, flops=20 * square * count // own, nbytes=40 * row_bytes * count // own,
            deps=deps, previous=previous,
        )

    half = own // 2
    if near is not None:
        outs = space_back(0, half, zeros, [mlp_far], ())
        mlp_a, mlp_b, mlp_x, mlp_y, mlp_own = near.reduce_first(mlp_mine, core_swap(mlp_far), [outs[0]])
        outs = space_back(half, own - half, outs[-1], [mlp_a, mlp_b], tuple(outs[:-1]))
        mlp_x, mlp_y = near.reduce_second(mlp_x, mlp_y, mlp_a, mlp_b, [outs[0]])
        time_deps = [mlp_x, mlp_y]
    else:
        outs = space_back(0, own, zeros, [], ())
        time_deps = []
    branch_grad, space_mixed_grad, after_grad, time_grad, time_att_grad, space_sums = outs

    far_frames = frames - own
    q_grad, own_grad, far_grad = call(
        time_back_kernel, (1,),
        [(whole(v.shape), v) for v in (queries, key_rows, value_rows, time_prob, time_att_grad)],
        [
            (whole(shape), sds(shape, BRAIN))
            for shape in (frame_shape, (2,) + frame_shape, (2, far_frames, rows, width))
        ],
        flops=6 * square, nbytes=40 * row_bytes, deps=time_deps,
    )
    operands = [flat(v) for v in (space_low, space_mixed_grad, space_att, branch_grad, time_att, time_grad)]
    if near is not None:
        from_far = core_swap(far_grad)
        mlp_parts = near.reduce_third(mlp_own, mlp_x, mlp_y, [q_grad])
        mlp_first, mlp_second, mlp_others = mlp_parts
        space_far = space_outer(far_slot, *operands, deps=[far_grad, mlp_second])
        space_mine = space_outer(my_slot, *operands, deps=[space_far])
        blocked = lambda v: v.reshape(BLOCKS, cut, v.shape[1])
        space_a, space_b, space_x, space_y, space_own = near.reduce_first(
            blocked(space_mine), core_swap(blocked(space_far)), [from_far]
        )
    else:
        padded = jnp.concatenate([jnp.zeros_like(own_grad), far_grad], axis=1)
        padded = jnp.roll(padded, core * own, axis=1)
        from_far = lax.psum_scatter(padded, "frame", scatter_dimension=1, tiled=True)
        space_mine, space_far = space_outer(my_slot, *operands), space_outer(far_slot, *operands)
    both = (own_grad.astype(FLOAT) + from_far.astype(FLOAT)).astype(BRAIN)
    time_mixed_grad = jnp.concatenate([q_grad, both[0], both[1]], axis=-1)
    outer = (flat(time_low), flat(time_mixed_grad))

    back_deps = [] if near is None else [space_a, space_b]
    token_grad, time_sums = call(
        time_mix_back_kernel, (own,),
        [
            (smem(), info), (per_frame(frame_shape), tokens), vec_in, (per_frame(mixed_shape), time_mixed_grad),
            (per_frame(frame_shape), after_grad),
        ]
        + pair(time_w),
        [wide_out(frame_shape), sum_out],
        time_held, flops=3 * square, nbytes=30 * row_bytes, deps=back_deps,
    )
    bias_grad = mlp_sums[3 : 3 + bias_rows].reshape(width, bias_rows)
    sums = jnp.concatenate([time_sums[:4], space_sums[5:6], space_sums[:5], mlp_sums[:3]], axis=0).T
    n_sums = sums.shape[1]
    blank = jnp.zeros((width, LANES - n_sums - bias_rows), FLOAT)
    sums = jnp.concatenate([sums, bias_grad, blank], axis=1)

    if near is not None:
        mlp_grads = near.reduce_direct(mlp_first, mlp_second, mlp_others)
        space_x, space_y = near.reduce_second(space_x, space_y, space_a, space_b, [token_grad])
        time_far = time_outer(far_slot, *outer, sums, deps=[space_x, space_y])
        time_mine = time_outer(my_slot, *outer, sums, deps=[time_far])
        space_parts = near.reduce_third(space_own, space_x, space_y, [time_mine])
        time_a, time_b, time_x, time_y, time_own = near.reduce_first(
            blocked(time_mine), core_swap(blocked(time_far)), []
        )
        time_x, time_y = near.reduce_second(time_x, time_y, time_a, time_b, [space_parts[1]])
        time_parts = near.reduce_third(time_own, time_x, time_y, [])
        grad_space = near.owner_rows(near.reduce_direct(*space_parts))
        total = near.reduce_direct(*time_parts)
        half = 3 * width // 2
        grad_time = near.owner_rows(total[:, :half])
        step = cut // 2
        sums = lax.dynamic_slice_in_dim(total[:, half:], core * step, step, 0)
        grad_mlp_down = mlp_grads[2 * cut :]
        grad_mlp_up = near.owner_rows(jnp.concatenate([mlp_grads[:cut], mlp_grads[cut : 2 * cut]], axis=1))
        class_total = space_sums[6:7] + core_swap(space_sums)[6:7]
    else:
        send = lambda v: lax.psum_scatter(v, AXES, scatter_dimension=0, tiled=True).astype(FLOAT)
        time_mine, time_far = (time_outer(slot, *outer, sums)[:, : 3 * width // 2] for slot in (my_slot, far_slot))
        up = jnp.stack([v[:, : 2 * cut].reshape(BLOCKS, 2, cut, width) for v in (mlp_mine, mlp_far)])
        grad_mlp_up = send(jnp.transpose(up, (1, 3, 0, 2, 4)).reshape(width, wide))
        grad_mlp_down = send(jnp.stack([v[:, 2 * cut :] for v in (mlp_mine, mlp_far)], axis=1).reshape(wide, width))
        grad_space = send(jnp.concatenate([space_mine, space_far], axis=1))
        grad_time = send(jnp.concatenate([time_mine, time_far], axis=1))
        class_total = lax.psum(space_sums[6:7], "frame")
        step = width // (clips * cores)
        sums = lax.dynamic_slice_in_dim(lax.psum(sums, AXES), shard * step, step, 0)
    class_in_grad = rows_grad[own - 1, places_here][None] + class_total
    lines = sums.T
    grad_time_vec, grad_space_vec, grad_mlp_vec = lines[:5], lines[5:10], lines[10:13]
    grad_mlp_bias = sums[:, n_sums : n_sums + bias_rows].reshape(-1)
    return (
        result[:, :places_here][None],
        result[own - 1, places_here][None],
        token_grad[:, :places_here][None],
        class_in_grad,
        grad_time,
        grad_space[:, 4 * width :],
        grad_time_vec,
        grad_space[:, : 3 * width],
        grad_space[:, 3 * width : 4 * width],
        grad_space_vec,
        grad_mlp_up,
        grad_mlp_down,
        grad_mlp_vec,
        grad_mlp_bias,
    )


def solution(mesh):
    both = ("clip", "frame")
    rows = P(both, None)
    columns = P(None, both)
    weights = (rows, rows, columns, rows, rows, columns, rows, rows, columns, P(both))
    block = P("clip", "frame", None, None)
    classes = P("clip", None)
    return jax.shard_map(
        functools.partial(body, mesh.shape["clip"], mesh.shape["frame"]),
        mesh=mesh,
        in_specs=(block, classes, block, classes, P("clip")) + weights,
        out_specs=(block, classes, block, classes) + weights,
        check_vma=False,
    )
```

```python
import functools

import jax
import jax.numpy as jnp
from jax import lax
from jax.experimental import pallas as pl
from jax.experimental.pallas import tpu as pltpu
from jax.sharding import PartitionSpec as P

HEAD_DIM = 64
EPSILON = 1e-06
FLOAT = jnp.float32
BRAIN = jnp.bfloat16
LANES = 128
BLOCKS = 16
RATE = 1e9
VMEM_BYTES = 56 * 1024 * 1024


def nn(left, right):
    return lax.dot_general(left, right, (((1,), (0,)), ((), ())), preferred_element_type=FLOAT)


def nt(left, right):
    return lax.dot_general(left, right, (((1,), (1,)), ((), ())), preferred_element_type=FLOAT)


def tn(left, right):
    return lax.dot_general(left, right, (((0,), (0,)), ((), ())), preferred_element_type=FLOAT)


def unit_of(values):
    average = jnp.mean(values, axis=-1, keepdims=True)
    centred = values - average
    spread = jnp.mean(centred * centred, axis=-1, keepdims=True)
    inverse = lax.rsqrt(spread + EPSILON)
    return centred * inverse, inverse


def norm_back(unit, inverse, gain, upstream):
    scaled = upstream * gain
    inner = jnp.mean(scaled, axis=-1, keepdims=True)
    along = jnp.mean(scaled * unit, axis=-1, keepdims=True)
    return inverse * (scaled - inner - unit * along)


def column_sum(values):
    return jnp.sum(values, axis=0, keepdims=True)


def row_index(shape):
    return lax.broadcasted_iota(jnp.int32, shape, 0)


def head_map(width):
    lane = lax.broadcasted_iota(jnp.int32, (width, LANES), 0) // HEAD_DIM
    head = lax.broadcasted_iota(jnp.int32, (width, LANES), 1)
    return (lane == head).astype(FLOAT).astype(BRAIN)


def head_spread(width):
    head = lax.broadcasted_iota(jnp.int32, (LANES, width), 0)
    lane = lax.broadcasted_iota(jnp.int32, (LANES, width), 1) // HEAD_DIM
    return (lane == head).astype(FLOAT).astype(BRAIN)


def column_copies(core, mine, other, held, sems):
    half = held.shape[1] // 2
    copies = []
    for n, (source, slot) in enumerate(((mine, core), (other, 1 - core))):
        target = held.at[:, pl.ds(pl.multiple_of(slot * half, LANES), half)]
        copies.append(pltpu.make_async_copy(source.at[:, :half], target, sems.at[n]))
    return copies


def mlp_copies(core, mine, other, up, down, sems):
    cut = up.shape[2]
    ups, downs = [], []
    for k, (source, slot) in enumerate(((mine, core), (other, 1 - core))):
        for t in (0, 1):
            part = source.at[:, t * cut : (t + 1) * cut]
            ups.append(pltpu.make_async_copy(part, up.at[2 * slot + t], sems.at[3 * k + t]))
        downs.append(pltpu.make_async_copy(source.at[:, 2 * cut :], down.at[:, slot], sems.at[3 * k + 2]))
    return ups, downs


def start_first(copies):
    @pl.when(pl.program_id(0) == 0)
    def _():
        for copy in copies:
            copy.start()


def wait_first(copies):
    @pl.when(pl.program_id(0) == 0)
    def _():
        for copy in copies:
            copy.wait()


def merged(ref):
    return ref[...].reshape(ref.shape[0] * ref.shape[1], ref.shape[2])


def store(ref, value):
    ref[...] = value.astype(ref.dtype).reshape(ref.shape)


def marks(count, rows, low, high):
    index = row_index((count * rows, 1))
    found = (index >= low) & (index < high)
    for n in range(1, count):
        found = found | ((index >= n * rows + low) & (index < n * rows + high))
    return found


def time_mix_kernel(own_steps, info, tokens, vectors, w_mine, w_other, q_out, k_out, v_out, low_out, held, sems):
    step = pl.program_id(0)
    width = tokens.shape[-1]

    copies = column_copies(info[0], w_mine, w_other, held, sems)
    start_first(copies)
    unit, _ = unit_of(merged(tokens).astype(FLOAT))
    low = (unit * vectors[0:1] + vectors[1:2]).astype(BRAIN)
    wait_first(copies)
    store(k_out, nn(low, held[:, width : 2 * width]))
    store(v_out, nn(low, held[:, 2 * width :]) + vectors[3:4])

    @pl.when(step < own_steps)
    def _():
        queries = (nn(low, held[:, :width]) + vectors[2:3]).astype(BRAIN)
        store(q_out, queries * jnp.asarray(HEAD_DIM ** (-0.5), BRAIN))
        store(low_out, low)


def tree_sum(values):
    values = list(values)
    while len(values) > 1:
        values = [a + b for a, b in zip(values[::2], values[1::2])] + values[len(values) & ~1 :]
    return values[0]


def attention_kernel(
    places_here, info, tokens, vectors, q_in, k_in, v_in, begin, sw_mine, sw_other,
    prob_out, att_out, after_out, low_out, mixed_out, sprob_out, satt_out, places_out, class_out,
    held, sems,
):
    step = pl.program_id(0)
    frames = k_in.shape[0]
    count, rows, width = tokens.shape
    core = info[0]

    copies = column_copies(core, sw_mine, sw_other, held, sems)
    start_first(copies)
    mapping = head_map(width)
    spread = head_spread(width)
    for n in range(count):
        queries = q_in[n]
        scores = [nn(queries * k_in[g], mapping) for g in range(frames)]
        top = functools.reduce(jnp.maximum, scores)
        powers = [jnp.exp(s - top) for s in scores]
        scale = 1.0 / sum(powers)
        parts = []
        for g in range(frames):
            prob = (powers[g] * scale).astype(BRAIN)
            prob_out[n, g] = prob
            parts.append(nn(prob, spread).astype(BRAIN) * v_in[g])
        att_out[n] = tree_sum(parts)
    wait_first(copies)
    attended = merged(att_out)
    place = marks(count, rows, 0, places_here)
    base = merged(tokens).astype(FLOAT)
    after = jnp.where(place, base + (nn(attended, held[:, 4 * width :]) + vectors[4:5]), base)
    store(after_out, after)
    unit, _ = unit_of(after)
    low = (unit * vectors[5:6] + vectors[6:7]).astype(BRAIN)
    store(low_out, low)
    shape = (count, rows, width)
    queries = (nn(low, held[:, :width]) + vectors[7:8]).astype(BRAIN) * jnp.asarray(HEAD_DIM ** (-0.5), BRAIN)
    mixed_out[:, :, :width] = queries.reshape(shape)
    mixed_out[:, :, width : 2 * width] = nn(low, held[:, width : 2 * width]).astype(BRAIN).reshape(shape)
    mixed_out[:, :, 2 * width :] = (
        (nn(low, held[:, 2 * width : 3 * width]) + vectors[8:9]).astype(BRAIN).reshape(shape)
    )
    lane = lax.broadcasted_iota(jnp.int32, (1, LANES), 1)
    masks = [(lane // HEAD_DIM == e).astype(FLOAT).astype(BRAIN) for e in (0, 1)]
    key_ok = row_index((rows, 1)) <= places_here
    for n in range(count):
        for pair in range(width // LANES):
            at = pair * LANES
            q2 = mixed_out[n, :, at : at + LANES]
            k2 = mixed_out[n, :, width + at : width + at + LANES]
            v2 = mixed_out[n, :, 2 * width + at : 2 * width + at + LANES]
            result = []
            for e in (0, 1):
                logits = jnp.where(key_ok, nt(k2, q2 * masks[e]), -1e30)
                power = jnp.exp(logits - jnp.max(logits, axis=0, keepdims=True))
                prob = (power * (1.0 / jnp.sum(power, axis=0, keepdims=True))).astype(BRAIN)
                sprob_out[n, 2 * pair + e] = prob
                result.append(tn(prob, v2))
            satt_out[n, :, at : at + LANES] = jnp.where(lane < HEAD_DIM, result[0], result[1]).astype(BRAIN)
    spatial = nn(merged(satt_out), held[:, 3 * width : 4 * width]) + vectors[9:10]
    store(places_out, jnp.where(place, after, 0.0) + spatial)

    @pl.when(step == 0)
    def _():
        class_out[...] = begin[...]

    class_row = column_sum(jnp.where(marks(count, rows, places_here, places_here + 1), spatial, 0.0))
    class_out[0:1] = class_out[0:1] + class_row


def gelu_parts(values):
    half = 0.5 + 0.5 * lax.erf(values * (0.5 ** 0.5))
    density = jnp.exp(values * values * (-0.5)) * (0.5 / 3.141592653589793) ** 0.5
    return values * half, half + values * density


def mlp_kernel(
    places_here, all_frames, info, alive, places, grads, class_row, class_own, class_far, vectors, bias,
    w_mine, w_other,
    out, low_out, hidden_out, feed_out, before_out, rows_out, sums, slopes, up, down, sems,
):
    step = pl.program_id(0)
    count, rows, width = places.shape
    core = info[0]

    ups, downs = mlp_copies(core, w_mine, w_other, up, down, sems)
    start_first(ups + downs)

    @pl.when(step == 0)
    def _():
        sums[...] = jnp.zeros_like(sums)

    class_mid = class_row[0:1] + (class_own[0:1] + class_far[0:1]) * all_frames ** (-0.5)
    last = (count - 1) * rows + places_here
    is_class = (row_index((count * rows, 1)) == last) & (step == pl.num_programs(0) - 1)
    kept = jnp.logical_not(marks(count, rows, places_here, places_here + 1) & (info[1] == 0))
    values = jnp.where(is_class, class_mid, merged(places))
    unit, inverse = unit_of(values)
    low = (unit * vectors[10:11] + vectors[11:12]).astype(BRAIN)
    store(low_out, low)
    feed = jnp.zeros((count * rows, width), FLOAT)
    chunks = hidden_out.shape[-1] // width
    per = down.shape[0] // chunks
    wait_first(ups)
    for j in range(chunks):
        before = nn(low, up[j].reshape(width, width)) + bias[j : j + 1]
        hidden, slope = gelu_parts(before)
        hidden = hidden.astype(BRAIN)
        hidden_out[:, :, j * width : (j + 1) * width] = hidden.reshape(count, rows, width)
        slopes[j] = slope
        if j == 0:
            wait_first(downs)
        feed = feed + nn(hidden, down[j * per : (j + 1) * per].reshape(width, width))
    store(out, (values + (feed + vectors[12:13])) * alive[0])

    row_grad = merged(grads).astype(FLOAT) * alive[0]
    feed_grad = row_grad.astype(BRAIN)
    feed_kept = jnp.where(kept, row_grad, 0.0).astype(BRAIN)
    store(feed_out, feed_kept)
    sums[2:3] = sums[2:3] + column_sum(feed_kept.astype(FLOAT))
    upstream = jnp.zeros((count * rows, width), FLOAT)
    for j in range(chunks):
        hidden_grad = nt(feed_grad, down[j * per : (j + 1) * per].reshape(width, width))
        before_grad = (hidden_grad * slopes[j]).astype(BRAIN)
        before_kept = jnp.where(kept, before_grad.astype(FLOAT), 0.0)
        before_out[:, :, j * width : (j + 1) * width] = before_kept.astype(BRAIN).reshape(count, rows, width)
        sums[3 + j : 4 + j] = sums[3 + j : 4 + j] + column_sum(before_kept)
        upstream = upstream + nt(before_grad, up[j].reshape(width, width))
    store(rows_out, row_grad + norm_back(unit, inverse, vectors[10:11], upstream))
    upstream = jnp.where(kept, upstream, 0.0)
    sums[0:1] = sums[0:1] + column_sum(upstream * unit)
    sums[1:2] = sums[1:2] + column_sum(upstream)


def space_back_kernel(
    places_here, all_frames, info, rows_grad, class_grad, after, mixed, sprob, satt, vectors, begin,
    sw_mine, sw_other,
    branch_out, mixed_out, after_out, time_out, att_out, sums, held, sems,
):
    step = pl.program_id(0)
    count, rows, width = after.shape
    core = info[0]

    copies = column_copies(core, sw_mine, sw_other, held, sems)
    start_first(copies)

    @pl.when(step == 0)
    def _():
        sums[...] = begin[...]

    place = marks(count, rows, 0, places_here)
    class_at = marks(count, rows, places_here, places_here + 1)
    offset = places_here % 16
    share = class_grad[0, offset : offset + 1] * all_frames ** (-0.5)
    direct = jnp.where(place, merged(rows_grad), 0.0)
    branch = jnp.where(class_at, share, direct).astype(BRAIN)
    store(branch_out, branch)
    sums[4:5] = sums[4:5] + column_sum(branch.astype(FLOAT))
    unit, inverse = unit_of(merged(after))
    wait_first(copies)
    att_grad = nt(branch, held[:, 3 * width : 4 * width]).astype(BRAIN)
    store(att_out, att_grad)
    spread = head_spread(width)
    lane = lax.broadcasted_iota(jnp.int32, (1, LANES), 1)
    masks = [(lane // HEAD_DIM == e).astype(FLOAT).astype(BRAIN) for e in (0, 1)]
    left = lane < HEAD_DIM
    for n in range(count):
        product = att_out[n].astype(FLOAT) * satt[n].astype(FLOAT)
        high = product.astype(BRAIN)
        rowdots = nt(spread, high) + nt(spread, (product - high.astype(FLOAT)).astype(BRAIN))
        for pair in range(width // LANES):
            at = pair * LANES
            a2 = att_out[n, :, at : at + LANES]
            q2 = mixed[n, :, at : at + LANES]
            k2 = mixed[n, :, width + at : width + at + LANES]
            v2 = mixed[n, :, 2 * width + at : 2 * width + at + LANES]
            queries, key_rows, value_rows = [], [], []
            for e in (0, 1):
                head = 2 * pair + e
                prob = sprob[n, head]
                prob_grad = nt(v2, a2 * masks[e])
                score = (prob.astype(FLOAT) * (prob_grad - rowdots[head : head + 1])).astype(BRAIN)
                queries.append(tn(score, k2))
                key_rows.append(nn(score, q2))
                value_rows.append(nn(prob, a2))
            q_grad = (jnp.where(left, queries[0], queries[1]) * HEAD_DIM ** (-0.5)).astype(BRAIN)
            k_grad = jnp.where(left, key_rows[0], key_rows[1]).astype(BRAIN)
            v_grad = jnp.where(left, value_rows[0], value_rows[1]).astype(BRAIN)
            mixed_out[n, :, at : at + LANES] = q_grad
            mixed_out[n, :, width + at : width + at + LANES] = k_grad
            mixed_out[n, :, 2 * width + at : 2 * width + at + LANES] = v_grad
    mixed_grad = merged(mixed_out)
    sums[2:3] = sums[2:3] + column_sum(mixed_grad[:, :width].astype(FLOAT))
    sums[3:4] = sums[3:4] + column_sum(mixed_grad[:, 2 * width :].astype(FLOAT))
    upstream = nt(mixed_grad, held[:, : 3 * width])
    inner = norm_back(unit, inverse, vectors[5:6], upstream)
    sums[0:1] = sums[0:1] + column_sum(upstream * unit)
    sums[1:2] = sums[1:2] + column_sum(upstream)
    sums[6:7] = sums[6:7] + column_sum(jnp.where(class_at, inner, 0.0))
    after_grad = jnp.where(place, direct + inner, 0.0)
    store(after_out, after_grad)
    low = after_grad.astype(BRAIN)
    store(time_out, low)
    sums[5:6] = sums[5:6] + column_sum(low.astype(FLOAT))
    store(att_out, nt(low, held[:, 4 * width :]))


def time_back_kernel(q_in, k_in, v_in, prob_in, att_in, q_out, own_out, far_out):
    own, rows, width = q_in.shape
    frames = k_in.shape[0]
    mapping = head_map(width)
    spread = head_spread(width)
    size = 16

    def chunk(index, carry):
        at = pl.ds(pl.multiple_of(index * size, size), size)
        values = [v_in[g, at] for g in range(frames)]
        att = [att_in[f, at] for f in range(own)]
        products = jnp.concatenate([att[f] * values[g] for f in range(own) for g in range(frames)], axis=0)
        prob_grad = nn(products, mapping)
        probs = [prob_in[f, g, at] for f in range(own) for g in range(frames)]
        scores = []
        for f in range(own):
            wide = [probs[f * frames + g].astype(FLOAT) for g in range(frames)]
            weighted = [
                wide[g] * prob_grad[(f * frames + g) * size : (f * frames + g + 1) * size] for g in range(frames)
            ]
            rowdot = sum(weighted)
            scores += [(weighted[g] - wide[g] * rowdot).astype(BRAIN) for g in range(frames)]
        score_wide = nn(jnp.concatenate(scores, axis=0), spread).astype(BRAIN)
        prob_wide = nn(jnp.concatenate(probs, axis=0), spread).astype(BRAIN)

        def part(array, f, g):
            return array[(f * frames + g) * size : (f * frames + g + 1) * size]

        keys = [k_in[g, at] for g in range(frames)]
        for f in range(own):
            total = tree_sum(part(score_wide, f, g) * keys[g] for g in range(frames))
            q_out[f, at] = total * jnp.asarray(HEAD_DIM ** (-0.5), BRAIN)
        queries = [q_in[f, at] for f in range(own)]
        for g in range(frames):
            key_grad = tree_sum(part(score_wide, f, g) * queries[f] for f in range(own))
            value_grad = tree_sum(part(prob_wide, f, g) * att[f] for f in range(own))
            if g < own:
                own_out[0, g, at] = key_grad
                own_out[1, g, at] = value_grad
            else:
                far_out[0, g - own, at] = key_grad
                far_out[1, g - own, at] = value_grad
        return carry

    lax.fori_loop(0, rows // size, chunk, 0)


def time_mix_back_kernel(info, tokens, vectors, mixed, after_grad, w_mine, w_other, token_out, sums, held, sems):
    step = pl.program_id(0)
    width = tokens.shape[-1]

    copies = column_copies(info[0], w_mine, w_other, held, sems)
    start_first(copies)

    @pl.when(step == 0)
    def _():
        sums[...] = jnp.zeros_like(sums)

    mixed_grad = merged(mixed)
    sums[2:3] = sums[2:3] + column_sum(mixed_grad[:, :width].astype(FLOAT))
    sums[3:4] = sums[3:4] + column_sum(mixed_grad[:, 2 * width :].astype(FLOAT))
    unit, inverse = unit_of(merged(tokens).astype(FLOAT))
    wait_first(copies)
    upstream = nt(mixed_grad, held[...])
    store(token_out, merged(after_grad) + norm_back(unit, inverse, vectors[0:1], upstream))
    sums[0:1] = sums[0:1] + column_sum(upstream * unit)
    sums[1:2] = sums[1:2] + column_sum(upstream)


def mixed_grad_kernel(queries, own, far, out):
    width = queries.shape[2]
    out[:, :, :width] = queries[...]
    out[:, :, width : 2 * width] = (own[0].astype(FLOAT) + far[0].astype(FLOAT)).astype(BRAIN)
    out[:, :, 2 * width :] = (own[1].astype(FLOAT) + far[1].astype(FLOAT)).astype(BRAIN)


def sums_kernel(time_sums, space_sums, mlp_sums, bias, out, lines):
    lines[...] = jnp.zeros_like(lines)
    lines[0:4] = time_sums[0:4]
    lines[4:5] = space_sums[5:6]
    lines[5:10] = space_sums[0:5]
    lines[10:13] = mlp_sums[0:3]
    count = bias.shape[1]
    place = lax.broadcasted_iota(jnp.int32, (count, LANES), 1) == row_index((count, LANES)) + 13
    spread = lax.dot_general(
        bias[...], place.astype(FLOAT), (((1,), (0,)), ((), ())), preferred_element_type=FLOAT,
        precision=lax.Precision.HIGHEST,
    )
    out[...] = lines[...].T + spread


def halves_kernel(left, right, left_out, right_out):
    left_out[...] = left[...]
    right_out[...] = right[...]


def share_rows(info, value, mine, other, at=slice(None)):
    value = value.reshape(mine.shape[0], 2, mine.shape[1], value.shape[-1])
    first = info[0] == 0
    mine[:, :, at] = jnp.where(first, value[:, 0], value[:, 1]).astype(BRAIN)
    other[:, :, at] = jnp.where(first, value[:, 1], value[:, 0]).astype(BRAIN)


def time_outer_kernel(info, left, right, sums, mine, other):
    step = pl.program_id(0)
    width = left.shape[1]

    for n in range(3):

        @pl.when(step == n)
        def _():
            share_rows(info, tn(left[...], right[...]), mine, other, slice(n * width, (n + 1) * width))

    @pl.when(step == 0)
    def _():
        share_rows(info, sums[...], mine, other, slice(3 * width, 3 * width + sums.shape[1]))


def space_outer_kernel(info, low, mixed, att, branch, time_att, time_grad, mine, other):
    step = pl.program_id(0)

    @pl.when(step < 3)
    def _():
        share_rows(info, tn(low[...], mixed[...]), mine, other)

    @pl.when(step == 3)
    def _():
        share_rows(info, tn(att[...], branch[...]), mine, other)

    @pl.when(step == 4)
    def _():
        share_rows(info, tn(time_att[...], time_grad[...]), mine, other)


def mlp_outer_kernel(info, low, before, hidden, feed, mine, other, turned, ups, downs, sems):
    step = pl.program_id(0)
    steps = ups.shape[0]
    blocks, cut, width = ups.shape[1:]
    per = downs.shape[2]

    @pl.when(step == 0)
    def _():
        turned[...] = low[...].T

    ups[step] = nn(turned[...], before[...]).astype(BRAIN).reshape(blocks, cut, width)
    value = tn(hidden[...], feed[...]).astype(BRAIN).reshape(per, 2, 2 * cut, width)
    downs[step, 0] = value[:, 0]
    downs[step, 1] = value[:, 1]

    for n in range(steps):
        targets = (mine, other)
        for k, slot in ((0, info[0]), (1, 1 - info[0])):
            up_copy = pltpu.make_async_copy(
                ups.at[n], targets[k].at[:, (n % 2) * cut : (n % 2 + 1) * cut], sems.at[0, n]
            )
            down_copy = pltpu.make_async_copy(
                downs.at[n, slot], targets[k].at[n * per : (n + 1) * per, 2 * cut :], sems.at[1 + k, n]
            )

            @pl.when((step == n) & (slot == n // 2))
            def _():
                up_copy.start()

            @pl.when(step == n)
            def _():
                down_copy.start()

            @pl.when((step == steps - 1) & (slot == n // 2))
            def _():
                up_copy.wait()

            @pl.when(step == steps - 1)
            def _():
                down_copy.wait()


def smem():
    return pl.BlockSpec(memory_space=pltpu.SMEM)


def hbm():
    return pl.BlockSpec(memory_space=pl.ANY)


def whole(shape):
    return pl.BlockSpec(shape, lambda *_: (0,) * len(shape))


def per_frame(shape, first=0, count=1):
    return pl.BlockSpec((count,) + shape[1:], lambda s: (s + first // count,) + (0,) * (len(shape) - 1))


def sds(shape, kind):
    return jax.ShapeDtypeStruct(shape, kind)


def call(kernel, grid, inputs, outputs, scratch=(), micros=2, deps=(), previous=(), prefetch=0):
    count = len(inputs)
    skip = len(previous) + len(deps)

    def inner(*refs):
        kernel(*refs[:count], *refs[count + skip :])

    specs = [spec for spec, _ in inputs[prefetch:]] + [hbm()] * skip
    common = dict(
        name=getattr(kernel, "func", kernel).__name__,
        out_shape=[shape for _, shape in outputs],
        compiler_params=pltpu.CompilerParams(vmem_limit_bytes=VMEM_BYTES),
        input_output_aliases={count + n: n for n in range(len(previous))},
        cost_estimate=pl.CostEstimate(flops=int(micros * RATE), bytes_accessed=1, transcendentals=0),
    )
    places = dict(grid=grid, in_specs=specs, out_specs=[spec for spec, _ in outputs], scratch_shapes=list(scratch))
    if prefetch:
        common["grid_spec"] = pltpu.PrefetchScalarGridSpec(num_scalar_prefetch=prefetch, **places)
    else:
        common.update(places)
    return pl.pallas_call(inner, **common)(*[array for _, array in inputs], *previous, *deps)


def time_outer(slot, left, right, sums, deps=()):
    rows, width = left.shape
    wide = right.shape[1]
    shape = (BLOCKS, width // (2 * BLOCKS), wide + sums.shape[1])
    return call(
        time_outer_kernel, (3,),
        [
            (smem(), slot), (whole(left.shape), left), (pl.BlockSpec((rows, width), lambda s: (0, s)), right),
            (whole(sums.shape), sums),
        ],
        [(whole(shape), sds(shape, BRAIN))] * 2, micros=8, deps=deps,
    )


def space_outer(slot, low, mixed, *others, deps=()):
    rows, width = low.shape
    shape = (BLOCKS, width // (2 * BLOCKS), width)
    moving = pl.BlockSpec((rows, width), lambda s: (0, jnp.minimum(s, 2)))
    return call(
        space_outer_kernel, (5,),
        [(smem(), slot), (whole(low.shape), low), (moving, mixed)] + [(whole(v.shape), v) for v in others],
        [(pl.BlockSpec(shape, lambda s: (0, 0, s)), sds(shape[:2] + (5 * width,), BRAIN))] * 2, micros=12, deps=deps,
    )


def mlp_outer(slot, low, before, hidden, feed, deps=()):
    rows, width = low.shape
    wide = hidden.shape[1]
    cut = width // BLOCKS
    shape = (BLOCKS, 4 * cut, width)
    fixed = pl.BlockSpec((rows, width), lambda s, info: (0, 0))
    moving = pl.BlockSpec((rows, width), lambda s, info: (0, s))
    return call(
        mlp_outer_kernel, (wide // width,),
        [(None, slot), (fixed, low), (moving, before), (moving, hidden), (fixed, feed)],
        [(hbm(), sds(shape, BRAIN))] * 2,
        [
            pltpu.VMEM((width, rows), BRAIN),
            pltpu.VMEM((wide // width, BLOCKS, cut, width), BRAIN),
            pltpu.VMEM((wide // width, 2, BLOCKS * width // wide, 2 * cut, width), BRAIN),
            pltpu.SemaphoreType.DMA((3, wide // width)),
        ],
        micros=21, deps=deps, prefetch=1,
    )


def gate(value, deps):
    return pl.pallas_call(
        lambda source, *refs: None,
        in_specs=[hbm()] * (1 + len(deps)),
        out_specs=hbm(),
        out_shape=sds(value.shape, value.dtype),
        input_output_aliases={0: 0},
    )(value, *deps)


def stack_kernel(*refs):
    for n, ref in enumerate(refs[:-1]):
        refs[-1][n] = ref[...]


def add_kernel(left, right, out):
    out[...] = left[...] + right[...]


def add_after(left, right, deps):
    inputs = [(whole(left.shape), left), (whole(right.shape), right)]
    return call(add_kernel, (1,), inputs, [(whole(left.shape), sds(left.shape, left.dtype))], deps=deps)[0]


def assemble_kernel(info, o4, rx, ry, ra, rb, out):
    depth = info[2]
    plane = info[3]
    for m in range(4):
        for n in range(4):
            if n < 3:
                value = (o4, rx, ry)[n][m]
            else:
                value = ra[m] if m < 2 else rb[m - 2]
            out[(depth ^ m) * 4 + (plane ^ n)] = value


def pack_kernel(info, time_qkv, space_qkv, space_proj, time_proj, up, time_vec, space_vec, mlp_vec, bias, send, keep):
    width = time_proj.shape[1]
    half = width // 2
    pieces = [time_qkv[:, n * half : (n + 1) * half] for n in range(6)]
    pieces += [space_qkv[:, n * half : (n + 1) * half] for n in range(6)]
    pieces += [space_proj[:, :half], space_proj[:, half:], time_proj[:, :half], time_proj[:, half:]]
    pieces += [up[:, n * half : (n + 1) * half] for n in range(8)]
    first = info[0] == 0
    at = 0
    for begin, count in ((0, 3), (6, 5), (16, 4)):
        for n in range(count):
            low, high = pieces[begin + n], pieces[begin + count + n]
            keep[:, at : at + half] = jnp.where(first, low, high)
            send[:, at : at + half] = jnp.where(first, high, low)
            at += half
    line = 0
    total = jnp.zeros((keep.shape[0], LANES), FLOAT)
    for source in (time_vec, space_vec, mlp_vec, bias):
        count = source.shape[0]
        lane = lax.broadcasted_iota(jnp.int32, (count, LANES), 1)
        chosen = (lane == row_index((count, LANES)) + line).astype(FLOAT)
        total = total + lax.dot_general(
            source[...].astype(FLOAT), chosen, (((0,), (0,)), ((), ())), preferred_element_type=FLOAT
        )
        line += count
    keep[:, at:] = total.astype(BRAIN)
    send[:, at:] = total.astype(BRAIN)


def turn_kernel(source, out):
    out[...] = source[...].astype(FLOAT).T


def join_kernel(info, keep, come, down, time_out, space_out, mlp_out):
    first = info[0] == 0
    width = down.shape[1]
    mine, far = keep[...].astype(FLOAT), come[...].astype(FLOAT)
    both = jnp.concatenate([jnp.where(first, mine, far), jnp.where(first, far, mine)], axis=0).astype(BRAIN)
    cut = both.shape[0]
    end = time_out.shape[1] - LANES
    time_out[:, :end] = both[:, :end]
    time_out[:, end:] = both[:, both.shape[1] - LANES :]
    space_out[...] = both[:, end : end + space_out.shape[1]]
    at = end + space_out.shape[1]
    mlp_out[:cut] = both[:, at : at + width]
    mlp_out[cut : 2 * cut] = both[:, at + width : at + 2 * width]
    mlp_out[2 * cut :] = down[...]


def added(*values):
    return sum(v.astype(FLOAT) for v in values).astype(BRAIN)


def reduce_first_kernel(info, mine, far, to_y, to_x, near_x, near_y, own):
    step = pl.program_id(0)
    plane = info[3]
    own[0] = added(mine[0, plane], far[0, plane])
    near_x[0] = added(mine[0, plane ^ 1], far[0, plane ^ 1])
    near_y[0] = added(mine[0, plane ^ 2], far[0, plane ^ 2])
    diagonal = added(mine[0, plane ^ 3], far[0, plane ^ 3])

    @pl.when(step < 2)
    def _():
        to_y[0] = diagonal

    @pl.when(step >= 2)
    def _():
        to_x[0] = diagonal


def reduce_second_kernel(near_x, near_y, from_y, from_x, out_x, out_y):
    step = pl.program_id(0)

    @pl.when(step < 2)
    def _():
        out_x[0] = added(near_x[0], from_y[0])
        out_y[0] = near_y[0]

    @pl.when(step >= 2)
    def _():
        out_x[0] = near_x[0]
        out_y[0] = added(near_y[0], from_x[0])


def reduce_third_kernel(info, own, from_x, from_y, first, second, others):
    for m in range(4):
        at = info[2] ^ m
        value = added(own[at], from_x[at], from_y[at])
        if m == 0:
            first[...] = value
        elif m == 1:
            second[...] = value
        else:
            others[m - 2] = value


def reduce_fourth_kernel(first, second, come, first_out, second_out):
    first_out[...] = first[...].astype(FLOAT) + come[0].astype(FLOAT)
    second_out[...] = added(second[...], come[1])


def clip_swap(values, bits, count):
    return lax.ppermute(values, "clip", [(i, i ^ bits) for i in range(count)])


def core_swap(values):
    return lax.ppermute(values, "frame", [(0, 1), (1, 0)])


class Near:
    def __init__(self, clips, info):
        self.clips = clips
        self.info = info
        self.core = lax.axis_index("frame")

    def swap(self, values, bits):
        return clip_swap(values, bits, self.clips)

    def in_order(self, mine, far, axis):
        return jnp.where(
            self.core == 0, jnp.concatenate([mine, far], axis=axis), jnp.concatenate([far, mine], axis=axis)
        )

    def stack(self, pieces, deps):
        shape = (len(pieces),) + pieces[0].shape
        return call(
            stack_kernel, (1,), [(whole(v.shape), v) for v in pieces], [(whole(shape), sds(shape, BRAIN))],
            micros=3, deps=deps,
        )[0]

    def depth_direct(self, own, deps):
        return self.stack([own] + [self.swap(own, 4 * m) for m in (1, 2, 3)], deps)

    def depth_near(self, own, deps):
        return self.stack([own, self.swap(own, 4)], deps)

    def depth_far(self, two, deps):
        come = self.swap(two, 8)
        return self.stack([two[0], two[1], come[0], come[1]], deps)

    def plane_step(self, o4, deps):
        rx = self.swap(o4, 1)
        ry = self.swap(o4, 2)
        half = (2,) + o4.shape[1:]
        first = pl.BlockSpec(half, lambda s: (0, 0, 0))
        second = pl.BlockSpec(half, lambda s: (1, 0, 0))
        sx, sy = call(
            halves_kernel, (1,), [(first, rx), (second, ry)], [(whole(half), sds(half, BRAIN))] * 2, deps=deps
        )
        return rx, ry, sx, sy

    def diagonal_step(self, o4, planes, deps):
        rx, ry, sx, sy = planes
        pieces = (o4, rx, ry, self.swap(sx, 2), self.swap(sy, 1))
        shape = (self.clips,) + o4.shape[1:]
        return call(
            assemble_kernel, (1,), [(smem(), self.info)] + [(whole(v.shape), v) for v in pieces],
            [(whole(shape), sds(shape, BRAIN))], micros=3, deps=deps,
        )[0]

    def reduce_first(self, mine, far, deps):
        block = mine.shape[1:]
        four = (4, 4) + block
        view = pl.BlockSpec((1, 4) + block, lambda s: (s, 0, 0, 0))
        one = lambda pick: pl.BlockSpec((1,) + block, lambda s: (pick(s), 0, 0))
        each = (one(lambda s: s), sds((4,) + block, BRAIN))
        return call(
            reduce_first_kernel, (4,),
            [(smem(), self.info), (view, mine.reshape(four)), (view, far.reshape(four))],
            [
                (one(lambda s: jnp.minimum(s, 1)), sds((2,) + block, BRAIN)),
                (one(lambda s: jnp.maximum(s - 2, 0)), sds((2,) + block, BRAIN)),
                each, each, each,
            ],
            micros=20, deps=deps,
        )

    def reduce_second(self, near_x, near_y, to_y, to_x, deps):
        from_y, from_x = self.swap(to_y, 2), self.swap(to_x, 1)
        block = near_x.shape[1:]
        one = lambda pick: pl.BlockSpec((1,) + block, lambda s: (pick(s), 0, 0))
        each = one(lambda s: s)
        return call(
            reduce_second_kernel, (4,),
            [
                (each, near_x), (each, near_y), (one(lambda s: jnp.minimum(s, 1)), from_y),
                (one(lambda s: jnp.maximum(s - 2, 0)), from_x),
            ],
            [(each, sds(near_x.shape, BRAIN))] * 2, micros=20, deps=deps,
        )

    def reduce_third(self, own, near_x, near_y, deps):
        from_x, from_y = self.swap(near_x, 1), self.swap(near_y, 2)
        block = own.shape[1:]
        return call(
            reduce_third_kernel, (1,),
            [(smem(), self.info)] + [(whole(v.shape), v) for v in (own, from_x, from_y)],
            [(whole(shape), sds(shape, BRAIN)) for shape in (block, block, (2,) + block)],
            micros=20, deps=deps,
        )

    def reduce_fourth(self, first, second, others, deps):
        come = self.swap(others, 8)
        inputs = [(whole(v.shape), v) for v in (first, second, come)]
        outs = [(whole(first.shape), sds(first.shape, kind)) for kind in (FLOAT, BRAIN)]
        return call(reduce_fourth_kernel, (1,), inputs, outs, micros=20, deps=deps)

    def reduce_end(self, first, second):
        return first + self.swap(second, 4).astype(FLOAT)

    def reduce_direct(self, first, second, others):
        total = first.astype(FLOAT) + self.swap(second, 4).astype(FLOAT)
        return total + self.swap(others[0], 8).astype(FLOAT) + self.swap(others[1], 12).astype(FLOAT)

    def owner_rows(self, value):
        rows = value.shape[0] // 2
        mine = lax.dynamic_slice_in_dim(value, self.core * rows, rows, 0)
        theirs = lax.dynamic_slice_in_dim(value, (1 - self.core) * rows, rows, 0)
        return self.in_order(mine, core_swap(theirs), 1)


AXES = ("clip", "frame")


def body(
    clips, cores, clip_tokens, clip_class, output_grad, class_grad, clip_count,
    time_qkv, time_proj, time_vec, space_qkv, space_proj, space_vec, mlp_up, mlp_down, mlp_vec, mlp_bias,
):
    _, own, places_here, width = clip_tokens.shape
    rows = -(-(places_here + 1) // 16) * 16
    frames = own * cores
    wide = mlp_up.shape[1]
    cut = width // BLOCKS
    core = lax.axis_index("frame")
    place = lax.axis_index("clip")
    shard = place * cores + core
    leader = (core == 0).astype(jnp.int32)
    alive = (jnp.arange(1, dtype=jnp.int32) < clip_count[0]).astype(FLOAT)
    is_near = clips == 16 and cores == 2
    slot = core if is_near else core * 0
    info = jnp.stack([slot, leader, place // 4, place % 4, shard]).astype(jnp.int32)
    near = Near(clips, info) if is_near else None
    my_slot = info[0:1]
    far_slot = 1 - my_slot

    class_block = jnp.broadcast_to(clip_class[0][None, None], (own, 1, width))
    blank = jnp.zeros((own, rows - places_here - 1, width), BRAIN)
    tokens = jnp.concatenate([clip_tokens[0], class_block, blank], axis=1)
    last = (jnp.arange(own) == own - 1)[:, None, None]
    class_rows = jnp.where(last, class_grad[0][None, None], jnp.zeros((), BRAIN))
    grads = jnp.concatenate([output_grad[0], class_rows, blank], axis=1)

    bias_rows = wide // width
    zeros = jnp.zeros((8, width), FLOAT)
    flat = lambda v: v.reshape((own * rows,) + v.shape[2:])

    if near is not None:
        packed = (
            time_qkv, space_qkv, space_proj, time_proj, mlp_up, time_vec, space_vec, mlp_vec,
            mlp_bias.reshape(-1, bias_rows).T,
        )
        line = sds((time_qkv.shape[0], 6 * width + LANES), BRAIN)
        send, keep = call(
            pack_kernel, (1,), [(smem(), info)] + [(whole(v.shape), v) for v in packed],
            [(whole(line.shape), line), (whole(line.shape), line)],
        )
        shapes = [(cut, 3 * width // 2 + LANES), (cut, 5 * width // 2), (4 * cut, width)]
        time_own, space_own, mlp_own = call(
            join_kernel, (1,),
            [(smem(), info)] + [(whole(v.shape), v) for v in (keep, core_swap(send), mlp_down)],
            [(whole(shape), sds(shape, BRAIN)) for shape in shapes],
        )
        join = lambda two: tuple(h.reshape(width, h.shape[-1]) for h in two)
        time_line = near.depth_direct(time_own, [])
        all_tokens = jnp.concatenate([tokens, core_swap(gate(tokens, [time_own]))], axis=0)
        space_own = gate(space_own, [time_line])
        space_line = near.depth_direct(space_own, [])
        time_mine = near.diagonal_step(time_line, near.plane_step(time_line, []), [grads, all_tokens, space_line])
        space_line = gate(space_line, [time_mine])
        time_far = core_swap(time_mine)
        time_w = join((time_mine, time_far))
        vec_block = pl.BlockSpec((width, LANES), lambda s: (0, time_w[0].shape[1] // LANES - 1))
        vectors = call(
            turn_kernel, (1,), [(vec_block, time_w[0])], [(whole((LANES, width)), sds((LANES, width), FLOAT))],
            deps=[space_line],
        )[0]
        n_vec = time_vec.shape[0] + space_vec.shape[0] + mlp_vec.shape[0]
        bias = vectors[n_vec : n_vec + bias_rows].T.reshape(bias_rows, width)
        mlp_own = gate(mlp_own, [time_mine])
        mix_deps = [space_line, mlp_own]
    else:
        everywhere = lax.all_gather(tokens, "frame", axis=0, tiled=True)
        all_tokens = jnp.roll(everywhere, -core * own, axis=0)
        vec_shard = jnp.concatenate([time_vec, space_vec, mlp_vec], axis=0)
        blank_rows = jnp.zeros((16 - vec_shard.shape[0], width), FLOAT)
        space_shard = jnp.concatenate([space_qkv, space_proj, time_proj], axis=1)
        vectors = lax.all_gather(vec_shard, AXES, axis=1, tiled=True).astype(FLOAT)
        bias = lax.all_gather(mlp_bias, AXES, axis=0, tiled=True).astype(FLOAT).reshape(bias_rows, width)
        vectors = jnp.concatenate([vectors, blank_rows], axis=0)

        def halves(value):
            full = lax.all_gather(value, AXES, axis=0, tiled=True)
            half = full.shape[1] // 2
            return full[:, :half], full[:, half:]

        time_w, space_w = halves(time_qkv), halves(space_shard)
        up = lax.all_gather(mlp_up, AXES, axis=0, tiled=True).reshape(BLOCKS, cut, 2, 2, width)
        up = jnp.transpose(up, (2, 0, 3, 1, 4)).reshape(2, BLOCKS, 2 * cut, width)
        down = lax.all_gather(mlp_down, AXES, axis=0, tiled=True).reshape(BLOCKS, 2, 2 * cut, width)
        mlp_w = tuple(jnp.concatenate([up[n], down[:, n]], axis=1) for n in (0, 1))
        mix_deps = []

    frame_shape = (own, rows, width)
    all_shape = (frames, rows, width)
    heads = width // HEAD_DIM
    prob_shape = (own, frames, rows, LANES)
    sprob_shape = (own, heads, rows, rows)
    mixed_shape = (own, rows, 3 * width)
    hidden_shape = (own, rows, wide)
    sum_out = (whole((8, width)), sds((8, width), FLOAT))
    row_bytes = own * rows * width
    square = 2 * own * rows * width * width
    group = 2 if own % 2 == 0 else 1
    frames_in = lambda array, first=0: (per_frame(array.shape, first, group), array)
    low_out = lambda shape, first=0: (per_frame(shape, first, group), sds(shape, BRAIN))
    wide_out = lambda shape, first=0: (per_frame(shape, first, group), sds(shape, FLOAT))
    vec_in = (whole(vectors.shape), vectors)
    pair = lambda two: [(hbm(), two[0]), (hbm(), two[1])]
    time_held = [pltpu.VMEM((width, 3 * width), BRAIN), pltpu.SemaphoreType.DMA((2,))]
    space_held = [pltpu.VMEM((width, 5 * width), BRAIN), pltpu.SemaphoreType.DMA((2,))]
    mlp_held = [
        pltpu.VMEM((wide // width, BLOCKS, cut, width), BRAIN),
        pltpu.VMEM((BLOCKS, 2, 2 * cut, width), BRAIN),
        pltpu.SemaphoreType.DMA((6,)),
    ]

    own_map = pl.BlockSpec((group, rows, width), lambda s: (jnp.minimum(s, own // group - 1), 0, 0))
    queries, key_rows, value_rows, time_low = call(
        functools.partial(time_mix_kernel, own // group), (frames // group,),
        [(smem(), info), frames_in(all_tokens), vec_in] + pair(time_w),
        [(own_map, sds(frame_shape, BRAIN)), low_out(all_shape), low_out(all_shape), (own_map, sds(frame_shape, BRAIN))],
        time_held, micros=12, deps=mix_deps,
    )

    if near is not None:
        mlp_line = near.depth_direct(mlp_own, [queries])
        space_mine = near.diagonal_step(space_line, near.plane_step(space_line, [queries, mlp_line]), [])
        space_w = join((space_mine, core_swap(space_mine)))
        mlp_line = gate(mlp_line, [space_mine])

    parts = [(0, own)] if near is None else [(0, own // 2), (own // 2, own - own // 2)]
    deps = [] if near is None else [mlp_line]
    kept, class_own = (), zeros
    for first, count in parts:
        outs = call(
            functools.partial(attention_kernel, places_here), (count // group,),
            [
                (smem(), info), frames_in(tokens, first), vec_in, frames_in(queries, first),
                (whole(all_shape), key_rows), (whole(all_shape), value_rows), (whole((8, width)), class_own),
            ]
            + pair(space_w),
            [
                low_out(prob_shape, first), low_out(frame_shape, first), wide_out(frame_shape, first),
                low_out(frame_shape, first), low_out(mixed_shape, first), low_out(sprob_shape, first),
                low_out(frame_shape, first), wide_out(frame_shape, first), sum_out,
            ],
            space_held, micros=27 * count / own, deps=deps, previous=kept,
        )
        kept, class_own = tuple(outs[:-1]), outs[-1]
        if near is not None and first == 0:
            mlp_planes = near.plane_step(mlp_line, [class_own])
            deps = list(mlp_planes[2:])
    time_prob, time_att, after, space_low, space_mixed, space_prob, space_att, places = kept

    if near is not None:
        mlp_mine = near.diagonal_step(mlp_line, mlp_planes, [places])
        mlp_w = (mlp_mine, core_swap(mlp_mine))
        class_far = core_swap(class_own)
    else:
        class_far = lax.psum(class_own, "frame") - class_own
    class_row = jnp.broadcast_to(clip_class.astype(FLOAT), (8, width))
    small = whole((8, width))
    result, mlp_low, hidden, feed_grad, before_grad, rows_grad, mlp_sums = call(
        functools.partial(mlp_kernel, places_here, frames), (own // group,),
        [
            (smem(), info), (smem(), alive), frames_in(places), frames_in(grads),
            (small, class_row), (small, class_own), (small, class_far), vec_in, (whole(bias.shape), bias),
        ]
        + pair(mlp_w),
        [
            low_out(frame_shape), low_out(frame_shape), low_out(hidden_shape), low_out(frame_shape),
            low_out(hidden_shape), wide_out(frame_shape), sum_out,
        ],
        [pltpu.VMEM((wide // width, group * rows, width), FLOAT)] + mlp_held,
        micros=25,
    )

    mlp_mine, mlp_far = mlp_outer(my_slot, flat(mlp_low), flat(before_grad), flat(hidden), flat(feed_grad))
    class_block_at = places_here // 16
    class_spec = pl.BlockSpec((1, 16, width), lambda s: (own - 1, class_block_at, 0))

    def space_back(first, count, sums, deps, previous):
        return call(
            functools.partial(space_back_kernel, places_here, frames), (count // group,),
            [
                (smem(), info), frames_in(rows_grad, first), (class_spec, rows_grad), frames_in(after, first),
                frames_in(space_mixed, first), frames_in(space_prob, first), frames_in(space_att, first),
                vec_in, (small, sums),
            ]
            + pair(space_w),
            [
                low_out(frame_shape, first), low_out(mixed_shape, first), wide_out(frame_shape, first),
                low_out(frame_shape, first), low_out(frame_shape, first), sum_out,
            ],
            space_held, micros=30 * count / own, deps=deps, previous=previous,
        )

    half = own // 2
    if near is not None:
        outs = space_back(0, half, zeros, [mlp_far], ())
        mlp_a, mlp_b, mlp_x, mlp_y, mlp_own = near.reduce_first(mlp_mine, core_swap(mlp_far), [outs[0]])
        outs = space_back(half, own - half, outs[-1], [mlp_a, mlp_b], tuple(outs[:-1]))
        mlp_x, mlp_y = near.reduce_second(mlp_x, mlp_y, mlp_a, mlp_b, [outs[0]])
        time_deps = [mlp_x, mlp_y]
    else:
        outs = space_back(0, own, zeros, [], ())
        time_deps = []
    branch_grad, space_mixed_grad, after_grad, time_grad, time_att_grad, space_sums = outs

    space_mine, space_far = space_outer(
        my_slot, *[flat(v) for v in (space_low, space_mixed_grad, space_att, branch_grad, time_att, time_grad)],
        deps=time_deps,
    )
    time_deps = time_deps + [space_far]
    far_frames = frames - own
    q_grad, own_grad, far_grad = call(
        time_back_kernel, (1,),
        [(whole(v.shape), v) for v in (queries, key_rows, value_rows, time_prob, time_att_grad)],
        [
            (whole(shape), sds(shape, BRAIN))
            for shape in (frame_shape, (2,) + frame_shape, (2, far_frames, rows, width))
        ],
        micros=22, deps=time_deps,
    )
    if near is not None:
        from_far = core_swap(far_grad)
        mlp_first, mlp_second, mlp_others = near.reduce_third(mlp_own, mlp_x, mlp_y, [q_grad])
        space_a, space_b, space_x, space_y, space_own = near.reduce_first(space_mine, core_swap(space_far), [mlp_second])
        mixed_deps = [space_own]
    else:
        mixed_deps = []
        padded = jnp.concatenate([jnp.zeros_like(own_grad), far_grad], axis=1)
        padded = jnp.roll(padded, core * own, axis=1)
        from_far = lax.psum_scatter(padded, "frame", scatter_dimension=1, tiled=True)
    pair_in = lambda v: (pl.BlockSpec((2, group, rows, width), lambda s: (0, s, 0, 0)), v)
    time_mixed_grad = call(
        mixed_grad_kernel, (own // group,), [frames_in(q_grad), pair_in(own_grad), pair_in(from_far)],
        [low_out(mixed_shape)], micros=3, deps=mixed_deps,
    )[0]
    outer = (flat(time_low), flat(time_mixed_grad))

    back_deps = [] if near is None else [mlp_second, space_a, space_b]
    token_grad, time_sums = call(
        time_mix_back_kernel, (own // group,),
        [(smem(), info), frames_in(tokens), vec_in, frames_in(time_mixed_grad), frames_in(after_grad)]
        + pair(time_w),
        [wide_out(frame_shape), sum_out],
        time_held, micros=10, deps=back_deps,
    )
    bias_grad = mlp_sums[3 : 3 + bias_rows].reshape(width, bias_rows)
    n_sums = 13
    sums = call(
        sums_kernel, (1,), [(small, time_sums), (small, space_sums), (small, mlp_sums), (whole(bias_grad.shape), bias_grad)],
        [(whole((width, LANES)), sds((width, LANES), FLOAT))], [pltpu.VMEM((LANES, width), FLOAT)],
    )[0]

    if near is not None:
        space_x, space_y = near.reduce_second(space_x, space_y, space_a, space_b, [token_grad])
        time_mine, time_far = time_outer(my_slot, *outer, sums, deps=[space_x, space_y])
        mlp_grads = near.reduce_direct(gate(mlp_first, [token_grad]), mlp_second, mlp_others)
        time_a, time_b, time_x, time_y, time_own = near.reduce_first(time_mine, core_swap(time_far), [])
        space_parts = near.reduce_third(space_own, space_x, space_y, [time_own])
        time_x, time_y = near.reduce_second(time_x, time_y, time_a, time_b, [space_parts[1]])
        time_parts = near.reduce_third(time_own, time_x, time_y, [])
        grad_space = near.reduce_direct(*space_parts)
        total = near.reduce_direct(*time_parts)
        grad_time, sums = total[:, : 3 * width], total[:, 3 * width :]
        grad_mlp_down = mlp_grads[2 * cut :]
        grad_mlp_up = near.owner_rows(jnp.concatenate([mlp_grads[:cut], mlp_grads[cut : 2 * cut]], axis=1))
        class_total = space_sums[6:7] + core_swap(space_sums)[6:7]
    else:
        send = lambda v: lax.psum_scatter(v, AXES, scatter_dimension=0, tiled=True).astype(FLOAT)
        spread = lambda mine, far: jnp.stack([mine, far], axis=1).reshape(width, mine.shape[2])
        time_mine, time_far = time_outer(my_slot, *outer, sums)
        up = jnp.stack([v[:, : 2 * cut].reshape(BLOCKS, 2, cut, width) for v in (mlp_mine, mlp_far)])
        grad_mlp_up = send(jnp.transpose(up, (1, 3, 0, 2, 4)).reshape(width, wide))
        grad_mlp_down = send(jnp.stack([v[:, 2 * cut :] for v in (mlp_mine, mlp_far)], axis=1).reshape(wide, width))
        grad_space = send(spread(space_mine, space_far))
        grad_time = send(spread(time_mine, time_far)[:, : 3 * width])
        class_total = lax.psum(space_sums[6:7], "frame")
        step = width // (clips * cores)
        sums = lax.dynamic_slice_in_dim(lax.psum(sums, AXES), shard * step, step, 0)
    class_in_grad = rows_grad[own - 1, places_here][None] + class_total
    lines = sums.T
    grad_time_vec, grad_space_vec, grad_mlp_vec = lines[:5], lines[5:10], lines[10:13]
    grad_mlp_bias = sums[:, n_sums : n_sums + bias_rows].reshape(-1)
    return (
        result[:, :places_here][None],
        result[own - 1, places_here][None],
        token_grad[:, :places_here][None],
        class_in_grad,
        grad_time,
        grad_space[:, 4 * width :],
        grad_time_vec,
        grad_space[:, : 3 * width],
        grad_space[:, 3 * width : 4 * width],
        grad_space_vec,
        grad_mlp_up,
        grad_mlp_down,
        grad_mlp_vec,
        grad_mlp_bias,
    )


def solution(mesh):
    both = ("clip", "frame")
    rows = P(both, None)
    columns = P(None, both)
    weights = (rows, rows, columns, rows, rows, columns, rows, rows, columns, P(both))
    block = P("clip", "frame", None, None)
    classes = P("clip", None)
    return jax.shard_map(
        functools.partial(body, mesh.shape["clip"], mesh.shape["frame"]),
        mesh=mesh,
        in_specs=(block, classes, block, classes, P("clip")) + weights,
        out_specs=(block, classes, block, classes) + weights,
        check_vma=False,
    )
```

```python
import functools

import jax
import jax.numpy as jnp
from jax import lax
from jax.experimental import pallas as pl
from jax.experimental.pallas import tpu as pltpu
from jax.sharding import PartitionSpec as P

HEAD_DIM = 64
EPSILON = 1e-06
FLOAT = jnp.float32
BRAIN = jnp.bfloat16
LANES = 128
BLOCKS = 16
RATE = 1e9
VMEM_BYTES = 60 * 1024 * 1024


def nn(left, right):
    return lax.dot_general(left, right, (((1,), (0,)), ((), ())), preferred_element_type=FLOAT)


def nt(left, right):
    return lax.dot_general(left, right, (((1,), (1,)), ((), ())), preferred_element_type=FLOAT)


def tn(left, right):
    return lax.dot_general(left, right, (((0,), (0,)), ((), ())), preferred_element_type=FLOAT)


def unit_of(values):
    average = jnp.mean(values, axis=-1, keepdims=True)
    centred = values - average
    spread = jnp.mean(centred * centred, axis=-1, keepdims=True)
    inverse = lax.rsqrt(spread + EPSILON)
    return centred * inverse, inverse


def norm_back(unit, inverse, gain, upstream):
    scaled = upstream * gain
    inner = jnp.mean(scaled, axis=-1, keepdims=True)
    along = jnp.mean(scaled * unit, axis=-1, keepdims=True)
    return inverse * (scaled - inner - unit * along)


def column_sum(values):
    return jnp.sum(values, axis=0, keepdims=True)


def row_index(shape):
    return lax.broadcasted_iota(jnp.int32, shape, 0)


def head_map(width, first=0):
    lane = lax.broadcasted_iota(jnp.int32, (width, LANES), 0) // HEAD_DIM + first
    head = lax.broadcasted_iota(jnp.int32, (width, LANES), 1)
    return (lane == head).astype(FLOAT).astype(BRAIN)


def head_spread(width, first=0):
    head = lax.broadcasted_iota(jnp.int32, (LANES, width), 0)
    lane = lax.broadcasted_iota(jnp.int32, (LANES, width), 1) // HEAD_DIM + first
    return (lane == head).astype(FLOAT).astype(BRAIN)


def column_copies(core, mine, other, held, sems):
    half = held.shape[1] // 2
    copies = []
    for n, (source, slot) in enumerate(((mine, core), (other, 1 - core))):
        target = held.at[:, pl.ds(pl.multiple_of(slot * half, LANES), half)]
        copies.append(pltpu.make_async_copy(source.at[:, :half], target, sems.at[n]))
    return copies


def mlp_copies(core, plane, mine, other, up, down, sems):
    cut = up.shape[3]
    ups, downs = [], []
    for k, (sources, slot) in enumerate(((mine, core), (other, 1 - core))):
        for n, source in enumerate(sources):
            if len(sources) == 1:
                at, tail = (), (slice(None),)
            else:
                at, tail = ((slice(None), slice(0, 2), slice(2, 4))[max(n - 2, 0)], plane ^ min(n, 3)), ()
            rows = lambda low, high: source.at[(slice(None),) + tail + (slice(low, high),)]
            for t in (0, 1):
                part = up.at[(2 * slot + t,) + at]
                ups.append(pltpu.make_async_copy(rows(t * cut, (t + 1) * cut), part, sems.at[k, 3 * n + t]))
            part = down.at[at + (slot,)] if at else down.at[:, :, slot]
            downs.append(pltpu.make_async_copy(rows(2 * cut, 4 * cut), part, sems.at[k, 3 * n + 2]))
    return ups, downs


def start_first(copies):
    @pl.when(pl.program_id(0) == 0)
    def _():
        for copy in copies:
            copy.start()


def wait_first(copies):
    @pl.when(pl.program_id(0) == 0)
    def _():
        for copy in copies:
            copy.wait()


def merged(ref):
    return ref[...].reshape(ref.shape[0] * ref.shape[1], ref.shape[2])


def store(ref, value):
    ref[...] = value.astype(ref.dtype).reshape(ref.shape)


def marks(count, rows, low, high):
    index = row_index((count * rows, 1))
    found = (index >= low) & (index < high)
    for n in range(1, count):
        found = found | ((index >= n * rows + low) & (index < n * rows + high))
    return found


def time_mix_kernel(own_steps, info, tokens, vectors, w_mine, w_other, q_out, k_out, v_out, low_out, held, sems):
    step = pl.program_id(0)
    width = tokens.shape[-1]

    copies = column_copies(info[0], w_mine, w_other, held, sems)
    start_first(copies)
    unit, _ = unit_of(merged(tokens).astype(FLOAT))
    low = (unit * vectors[0:1] + vectors[1:2]).astype(BRAIN)
    wait_first(copies)
    store(k_out, nn(low, held[:, width : 2 * width]))
    store(v_out, nn(low, held[:, 2 * width :]) + vectors[3:4])

    @pl.when(step < own_steps)
    def _():
        queries = (nn(low, held[:, :width]) + vectors[2:3]).astype(BRAIN)
        store(q_out, queries * jnp.asarray(HEAD_DIM ** (-0.5), BRAIN))
        store(low_out, low)


def tree_sum(values):
    values = list(values)
    while len(values) > 1:
        values = [a + b for a, b in zip(values[::2], values[1::2])] + values[len(values) & ~1 :]
    return values[0]


def attention_kernel(
    places_here, info, tokens, vectors, q_in, k_in, v_in, begin, sw_mine, sw_other,
    prob_out, att_out, after_out, low_out, mixed_out, sprob_out, satt_out, places_out, class_out,
    held, sems,
):
    step = pl.program_id(0)
    frames = k_in.shape[0]
    count, rows, width = tokens.shape
    core = info[0]

    copies = column_copies(core, sw_mine, sw_other, held, sems)
    start_first(copies)
    mapping = head_map(width)
    spread = head_spread(width)
    for n in range(count):
        queries = q_in[n]
        scores = [nn(queries * k_in[g], mapping) for g in range(frames)]
        top = functools.reduce(jnp.maximum, scores)
        powers = [jnp.exp(s - top) for s in scores]
        scale = 1.0 / sum(powers)
        parts = []
        for g in range(frames):
            prob = (powers[g] * scale).astype(BRAIN)
            prob_out[n, g] = prob
            parts.append(nn(prob, spread).astype(BRAIN) * v_in[g])
        att_out[n] = tree_sum(parts)
    wait_first(copies)
    attended = merged(att_out)
    place = marks(count, rows, 0, places_here)
    base = merged(tokens).astype(FLOAT)
    after = jnp.where(place, base + (nn(attended, held[:, 4 * width :]) + vectors[4:5]), base)
    store(after_out, after)
    unit, _ = unit_of(after)
    low = (unit * vectors[5:6] + vectors[6:7]).astype(BRAIN)
    store(low_out, low)
    shape = (count, rows, width)
    queries = (nn(low, held[:, :width]) + vectors[7:8]).astype(BRAIN) * jnp.asarray(HEAD_DIM ** (-0.5), BRAIN)
    mixed_out[:, :, :width] = queries.reshape(shape)
    mixed_out[:, :, width : 2 * width] = nn(low, held[:, width : 2 * width]).astype(BRAIN).reshape(shape)
    mixed_out[:, :, 2 * width :] = (
        (nn(low, held[:, 2 * width : 3 * width]) + vectors[8:9]).astype(BRAIN).reshape(shape)
    )
    lane = lax.broadcasted_iota(jnp.int32, (1, LANES), 1)
    masks = [(lane // HEAD_DIM == e).astype(FLOAT).astype(BRAIN) for e in (0, 1)]
    key_ok = row_index((rows, 1)) <= places_here
    for n in range(count):
        for pair in range(width // LANES):
            at = pair * LANES
            q2 = mixed_out[n, :, at : at + LANES]
            k2 = mixed_out[n, :, width + at : width + at + LANES]
            v2 = mixed_out[n, :, 2 * width + at : 2 * width + at + LANES]
            result = []
            for e in (0, 1):
                logits = jnp.where(key_ok, nt(k2, q2 * masks[e]), -1e30)
                power = jnp.exp(logits - jnp.max(logits, axis=0, keepdims=True))
                prob = (power * (1.0 / jnp.sum(power, axis=0, keepdims=True))).astype(BRAIN)
                sprob_out[n, 2 * pair + e] = prob
                result.append(tn(prob, v2))
            satt_out[n, :, at : at + LANES] = jnp.where(lane < HEAD_DIM, result[0], result[1]).astype(BRAIN)
    spatial = nn(merged(satt_out), held[:, 3 * width : 4 * width]) + vectors[9:10]
    store(places_out, jnp.where(place, after, 0.0) + spatial)

    @pl.when(step == 0)
    def _():
        class_out[...] = begin[...]

    class_row = column_sum(jnp.where(marks(count, rows, places_here, places_here + 1), spatial, 0.0))
    class_out[0:1] = class_out[0:1] + class_row


def gelu_parts(values):
    half = 0.5 + 0.5 * lax.erf(values * (0.5 ** 0.5))
    density = jnp.exp(values * values * (-0.5)) * (0.5 / 3.141592653589793) ** 0.5
    return values * half, half + values * density


def mlp_kernel(
    places_here, all_frames, pieces, info, alive, places, grads, class_row, class_own, class_far, vectors, bias,
    *others,
):
    mine, other, others = others[:pieces], others[pieces : 2 * pieces], others[2 * pieces :]
    out, class_out, low_out, hidden_out, feed_out, before_out, rows_out, sums, slopes, up, down, sems = others
    step = pl.program_id(0)
    count, rows, width = places.shape
    core = info[0]

    ups, downs = mlp_copies(core, info[3], mine, other, up, down, sems)
    start_first(ups + downs)

    @pl.when(step == 0)
    def _():
        sums[...] = jnp.zeros_like(sums)

    class_mid = class_row[0:1] + (class_own[0:1] + class_far[0:1]) * all_frames ** (-0.5)
    last = (count - 1) * rows + places_here
    is_class = (row_index((count * rows, 1)) == last) & (step == pl.num_programs(0) - 1)
    kept = jnp.logical_not(marks(count, rows, places_here, places_here + 1) & (info[1] == 0))
    values = jnp.where(is_class, class_mid, merged(places))
    unit, inverse = unit_of(values)
    low = (unit * vectors[10:11] + vectors[11:12]).astype(BRAIN)
    store(low_out, low)
    feed = jnp.zeros((count * rows, width), FLOAT)
    chunks = hidden_out.shape[-1] // width
    wait_first(ups)
    for j in range(chunks):
        before = nn(low, up[j].reshape(width, width)) + bias[j : j + 1]
        hidden, slope = gelu_parts(before)
        hidden = hidden.astype(BRAIN)
        hidden_out[:, :, j * width : (j + 1) * width] = hidden.reshape(count, rows, width)
        slopes[j] = slope
        if j == 0:
            wait_first(downs)
        feed = feed + nn(hidden, down[j].reshape(width, width))
    result = ((values + (feed + vectors[12:13])) * alive[0]).reshape(count, rows, width)
    out[...] = result[:, :places_here].astype(BRAIN)
    class_out[...] = result[count - 1, places_here - places_here % 8 : places_here - places_here % 8 + 8]

    row_grad = merged(grads).astype(FLOAT) * alive[0]
    feed_grad = row_grad.astype(BRAIN)
    feed_kept = jnp.where(kept, row_grad, 0.0).astype(BRAIN)
    store(feed_out, feed_kept)
    sums[2:3] = sums[2:3] + column_sum(feed_kept.astype(FLOAT))
    upstream = jnp.zeros((count * rows, width), FLOAT)
    for j in range(chunks):
        hidden_grad = nt(feed_grad, down[j].reshape(width, width))
        before_grad = (hidden_grad * slopes[j]).astype(BRAIN)
        before_kept = jnp.where(kept, before_grad.astype(FLOAT), 0.0)
        before_out[:, :, j * width : (j + 1) * width] = before_kept.astype(BRAIN).reshape(count, rows, width)
        sums[3 + j : 4 + j] = sums[3 + j : 4 + j] + column_sum(before_kept)
        upstream = upstream + nt(before_grad, up[j].reshape(width, width))
    store(rows_out, row_grad + norm_back(unit, inverse, vectors[10:11], upstream))
    upstream = jnp.where(kept, upstream, 0.0)
    sums[0:1] = sums[0:1] + column_sum(upstream * unit)
    sums[1:2] = sums[1:2] + column_sum(upstream)


def space_back_kernel(
    places_here, all_frames, info, rows_grad, class_grad, after, mixed, sprob, satt, vectors, begin,
    sw_mine, sw_other,
    branch_out, mixed_out, after_out, time_out, att_out, sums, held, sems,
):
    step = pl.program_id(0)
    count, rows, width = after.shape
    core = info[0]

    copies = column_copies(core, sw_mine, sw_other, held, sems)
    start_first(copies)

    @pl.when(step == 0)
    def _():
        sums[...] = begin[...]

    place = marks(count, rows, 0, places_here)
    class_at = marks(count, rows, places_here, places_here + 1)
    offset = places_here % 16
    share = class_grad[0, offset : offset + 1] * all_frames ** (-0.5)
    direct = jnp.where(place, merged(rows_grad), 0.0)
    branch = jnp.where(class_at, share, direct).astype(BRAIN)
    store(branch_out, branch)
    sums[4:5] = sums[4:5] + column_sum(branch.astype(FLOAT))
    unit, inverse = unit_of(merged(after))
    wait_first(copies)
    att_grad = nt(branch, held[:, 3 * width : 4 * width]).astype(BRAIN)
    store(att_out, att_grad)
    spread = head_spread(width)
    lane = lax.broadcasted_iota(jnp.int32, (1, LANES), 1)
    masks = [(lane // HEAD_DIM == e).astype(FLOAT).astype(BRAIN) for e in (0, 1)]
    left = lane < HEAD_DIM
    for n in range(count):
        product = att_out[n].astype(FLOAT) * satt[n].astype(FLOAT)
        high = product.astype(BRAIN)
        rowdots = nt(spread, high) + nt(spread, (product - high.astype(FLOAT)).astype(BRAIN))
        for pair in range(width // LANES):
            at = pair * LANES
            a2 = att_out[n, :, at : at + LANES]
            q2 = mixed[n, :, at : at + LANES]
            k2 = mixed[n, :, width + at : width + at + LANES]
            v2 = mixed[n, :, 2 * width + at : 2 * width + at + LANES]
            queries, key_rows, value_rows = [], [], []
            for e in (0, 1):
                head = 2 * pair + e
                prob = sprob[n, head]
                prob_grad = nt(v2, a2 * masks[e])
                score = (prob.astype(FLOAT) * (prob_grad - rowdots[head : head + 1])).astype(BRAIN)
                queries.append(tn(score, k2))
                key_rows.append(nn(score, q2))
                value_rows.append(nn(prob, a2))
            q_grad = (jnp.where(left, queries[0], queries[1]) * HEAD_DIM ** (-0.5)).astype(BRAIN)
            k_grad = jnp.where(left, key_rows[0], key_rows[1]).astype(BRAIN)
            v_grad = jnp.where(left, value_rows[0], value_rows[1]).astype(BRAIN)
            mixed_out[n, :, at : at + LANES] = q_grad
            mixed_out[n, :, width + at : width + at + LANES] = k_grad
            mixed_out[n, :, 2 * width + at : 2 * width + at + LANES] = v_grad
    mixed_grad = merged(mixed_out)
    sums[2:3] = sums[2:3] + column_sum(mixed_grad[:, :width].astype(FLOAT))
    sums[3:4] = sums[3:4] + column_sum(mixed_grad[:, 2 * width :].astype(FLOAT))
    upstream = nt(mixed_grad, held[:, : 3 * width])
    inner = norm_back(unit, inverse, vectors[5:6], upstream)
    sums[0:1] = sums[0:1] + column_sum(upstream * unit)
    sums[1:2] = sums[1:2] + column_sum(upstream)
    sums[6:7] = sums[6:7] + column_sum(jnp.where(class_at, inner, 0.0))
    after_grad = jnp.where(place, direct + inner, 0.0)
    store(after_out, after_grad)
    low = after_grad.astype(BRAIN)
    store(time_out, low)
    sums[5:6] = sums[5:6] + column_sum(low.astype(FLOAT))
    store(att_out, nt(low, held[:, 4 * width :]))


def time_back_kernel(q_in, k_in, v_in, prob_in, att_in, q_out, own_out, far_out):
    own, rows, width = q_in.shape
    frames = k_in.shape[0]
    first = pl.program_id(0) * (width // HEAD_DIM)
    mapping = head_map(width, first)
    spread = head_spread(width, first)
    size = 16

    def chunk(index, carry):
        at = pl.ds(pl.multiple_of(index * size, size), size)
        values = [v_in[g, at] for g in range(frames)]
        att = [att_in[f, at] for f in range(own)]
        products = jnp.concatenate([att[f] * values[g] for f in range(own) for g in range(frames)], axis=0)
        prob_grad = nn(products, mapping)
        probs = [prob_in[f, g, at] for f in range(own) for g in range(frames)]
        scores = []
        for f in range(own):
            wide = [probs[f * frames + g].astype(FLOAT) for g in range(frames)]
            weighted = [
                wide[g] * prob_grad[(f * frames + g) * size : (f * frames + g + 1) * size] for g in range(frames)
            ]
            rowdot = sum(weighted)
            scores += [(weighted[g] - wide[g] * rowdot).astype(BRAIN) for g in range(frames)]
        score_wide = nn(jnp.concatenate(scores, axis=0), spread).astype(BRAIN)
        prob_wide = nn(jnp.concatenate(probs, axis=0), spread).astype(BRAIN)

        def part(array, f, g):
            return array[(f * frames + g) * size : (f * frames + g + 1) * size]

        keys = [k_in[g, at] for g in range(frames)]
        for f in range(own):
            total = tree_sum(part(score_wide, f, g) * keys[g] for g in range(frames))
            q_out[f, at] = total * jnp.asarray(HEAD_DIM ** (-0.5), BRAIN)
        queries = [q_in[f, at] for f in range(own)]
        for g in range(frames):
            key_grad = tree_sum(part(score_wide, f, g) * queries[f] for f in range(own))
            value_grad = tree_sum(part(prob_wide, f, g) * att[f] for f in range(own))
            if g < own:
                own_out[0, g, at] = key_grad
                own_out[1, g, at] = value_grad
            else:
                far_out[0, g - own, at] = key_grad
                far_out[1, g - own, at] = value_grad
        return carry

    lax.fori_loop(0, rows // size, chunk, 0, unroll=True)


def time_mix_back_kernel(info, tokens, vectors, mixed, after_grad, w_mine, w_other, token_out, sums, held, sems):
    step = pl.program_id(0)
    width = tokens.shape[-1]

    copies = column_copies(info[0], w_mine, w_other, held, sems)
    start_first(copies)

    @pl.when(step == 0)
    def _():
        sums[...] = jnp.zeros_like(sums)

    mixed_grad = merged(mixed)
    sums[2:3] = sums[2:3] + column_sum(mixed_grad[:, :width].astype(FLOAT))
    sums[3:4] = sums[3:4] + column_sum(mixed_grad[:, 2 * width :].astype(FLOAT))
    unit, inverse = unit_of(merged(tokens).astype(FLOAT))
    wait_first(copies)
    upstream = nt(mixed_grad, held[...])
    result = merged(after_grad) + norm_back(unit, inverse, vectors[0:1], upstream)
    token_out[...] = result.reshape(mixed.shape[:2] + (width,))[:, : token_out.shape[1]]
    sums[0:1] = sums[0:1] + column_sum(upstream * unit)
    sums[1:2] = sums[1:2] + column_sum(upstream)


def mixed_grad_kernel(queries, own, far, out):
    width = queries.shape[2]
    out[:, :, :width] = queries[...]
    out[:, :, width : 2 * width] = (own[0].astype(FLOAT) + far[0].astype(FLOAT)).astype(BRAIN)
    out[:, :, 2 * width :] = (own[1].astype(FLOAT) + far[1].astype(FLOAT)).astype(BRAIN)


def sums_kernel(time_sums, space_sums, mlp_sums, bias, out, lines):
    lines[...] = jnp.zeros_like(lines)
    lines[0:4] = time_sums[0:4]
    lines[4:5] = space_sums[5:6]
    lines[5:10] = space_sums[0:5]
    lines[10:13] = mlp_sums[0:3]
    count = bias.shape[1]
    place = lax.broadcasted_iota(jnp.int32, (count, LANES), 1) == row_index((count, LANES)) + 13
    spread = lax.dot_general(
        bias[...], place.astype(FLOAT), (((1,), (0,)), ((), ())), preferred_element_type=FLOAT,
        precision=lax.Precision.HIGHEST,
    )
    out[...] = lines[...].T + spread


def halves_kernel(left, right, left_out, right_out):
    left_out[...] = left[...]
    right_out[...] = right[...]


def share_rows(info, value, mine, other, at=slice(None)):
    value = value.reshape(mine.shape[0], 2, mine.shape[1], value.shape[-1])
    first = info[0] == 0
    mine[:, :, at] = jnp.where(first, value[:, 0], value[:, 1]).astype(BRAIN)
    other[:, :, at] = jnp.where(first, value[:, 1], value[:, 0]).astype(BRAIN)


def time_outer_kernel(info, left, right, sums, mine, other):
    step = pl.program_id(0)
    width = left.shape[1]

    for n in range(3):

        @pl.when(step == n)
        def _():
            share_rows(info, tn(left[...], right[...]), mine, other, slice(n * width, (n + 1) * width))

    @pl.when(step == 0)
    def _():
        share_rows(info, sums[...], mine, other, slice(3 * width, 3 * width + sums.shape[1]))


def space_outer_kernel(info, low, mixed, att, branch, time_att, time_grad, mine, other):
    step = pl.program_id(0)

    @pl.when(step < 3)
    def _():
        share_rows(info, tn(low[...], mixed[...]), mine, other)

    @pl.when(step == 3)
    def _():
        share_rows(info, tn(att[...], branch[...]), mine, other)

    @pl.when(step == 4)
    def _():
        share_rows(info, tn(time_att[...], time_grad[...]), mine, other)


def mlp_outer_kernel(info, low, before, hidden, feed, mine, other, turned, ups, downs, sems):
    step = pl.program_id(0)
    steps = ups.shape[0]
    blocks, cut, width = ups.shape[1:]
    per = downs.shape[2]

    @pl.when(step == 0)
    def _():
        turned[...] = low[...].T

    ups[step] = nn(turned[...], before[...]).astype(BRAIN).reshape(blocks, cut, width)
    value = tn(hidden[...], feed[...]).astype(BRAIN).reshape(per, 2, 2 * cut, width)
    downs[step, 0] = value[:, 0]
    downs[step, 1] = value[:, 1]

    for n in range(steps):
        targets = (mine, other)
        for k, slot in ((0, info[0]), (1, 1 - info[0])):
            up_copy = pltpu.make_async_copy(
                ups.at[n], targets[k].at[:, (n % 2) * cut : (n % 2 + 1) * cut], sems.at[0, n]
            )
            down_copy = pltpu.make_async_copy(
                downs.at[n, slot], targets[k].at[n * per : (n + 1) * per, 2 * cut :], sems.at[1 + k, n]
            )

            @pl.when((step == n) & (slot == n // 2))
            def _():
                up_copy.start()

            @pl.when(step == n)
            def _():
                down_copy.start()

            @pl.when((step == steps - 1) & (slot == n // 2))
            def _():
                up_copy.wait()

            @pl.when(step == steps - 1)
            def _():
                down_copy.wait()


def smem():
    return pl.BlockSpec(memory_space=pltpu.SMEM)


def hbm():
    return pl.BlockSpec(memory_space=pl.ANY)


def whole(shape):
    return pl.BlockSpec(shape, lambda *_: (0,) * len(shape))


def per_frame(shape, first=0, count=1):
    return pl.BlockSpec((count,) + shape[1:], lambda s: (s + first // count,) + (0,) * (len(shape) - 1))


def sds(shape, kind):
    return jax.ShapeDtypeStruct(shape, kind)


def call(kernel, grid, inputs, outputs, scratch=(), micros=2, deps=(), previous=(), prefetch=0):
    count = len(inputs)
    skip = len(previous) + len(deps)

    def inner(*refs):
        kernel(*refs[:count], *refs[count + skip :])

    specs = [spec for spec, _ in inputs[prefetch:]] + [hbm()] * skip
    common = dict(
        name=getattr(kernel, "func", kernel).__name__,
        out_shape=[shape for _, shape in outputs],
        compiler_params=pltpu.CompilerParams(vmem_limit_bytes=VMEM_BYTES),
        input_output_aliases={count + n: n for n in range(len(previous))},
        cost_estimate=pl.CostEstimate(flops=int(micros * RATE), bytes_accessed=1, transcendentals=0),
    )
    places = dict(grid=grid, in_specs=specs, out_specs=[spec for spec, _ in outputs], scratch_shapes=list(scratch))
    if prefetch:
        common["grid_spec"] = pltpu.PrefetchScalarGridSpec(num_scalar_prefetch=prefetch, **places)
    else:
        common.update(places)
    return pl.pallas_call(inner, **common)(*[array for _, array in inputs], *previous, *deps)


def time_outer(slot, left, right, sums, deps=()):
    rows, width = left.shape
    wide = right.shape[1]
    shape = (BLOCKS, width // (2 * BLOCKS), wide + sums.shape[1])
    return call(
        time_outer_kernel, (3,),
        [
            (smem(), slot), (whole(left.shape), left), (pl.BlockSpec((rows, width), lambda s: (0, s)), right),
            (whole(sums.shape), sums),
        ],
        [(whole(shape), sds(shape, BRAIN))] * 2, micros=8, deps=deps,
    )


def space_outer(slot, low, mixed, *others, deps=()):
    rows, width = low.shape
    shape = (BLOCKS, width // (2 * BLOCKS), width)
    moving = pl.BlockSpec((rows, width), lambda s: (0, jnp.minimum(s, 2)))
    return call(
        space_outer_kernel, (5,),
        [(smem(), slot), (whole(low.shape), low), (moving, mixed)] + [(whole(v.shape), v) for v in others],
        [(pl.BlockSpec(shape, lambda s: (0, 0, s)), sds(shape[:2] + (5 * width,), BRAIN))] * 2, micros=12, deps=deps,
    )


def mlp_outer(slot, low, before, hidden, feed, deps=()):
    rows, width = low.shape
    wide = hidden.shape[1]
    cut = width // BLOCKS
    shape = (BLOCKS, 4 * cut, width)
    fixed = pl.BlockSpec((rows, width), lambda s, info: (0, 0))
    moving = pl.BlockSpec((rows, width), lambda s, info: (0, s))
    return call(
        mlp_outer_kernel, (wide // width,),
        [(None, slot), (fixed, low), (moving, before), (moving, hidden), (fixed, feed)],
        [(hbm(), sds(shape, BRAIN))] * 2,
        [
            pltpu.VMEM((width, rows), BRAIN),
            pltpu.VMEM((wide // width, BLOCKS, cut, width), BRAIN),
            pltpu.VMEM((wide // width, 2, BLOCKS * width // wide, 2 * cut, width), BRAIN),
            pltpu.SemaphoreType.DMA((3, wide // width)),
        ],
        micros=21, deps=deps, prefetch=1,
    )


def gate(value, deps):
    return pl.pallas_call(
        lambda source, *refs: None,
        in_specs=[hbm()] * (1 + len(deps)),
        out_specs=hbm(),
        out_shape=sds(value.shape, value.dtype),
        input_output_aliases={0: 0},
    )(value, *deps)


def stack_at_kernel(info, *refs):
    for n, ref in enumerate(refs[:-1]):
        refs[-1][info[2] ^ n] = ref[...]


def stack_kernel(*refs):
    for n, ref in enumerate(refs[:-1]):
        refs[-1][n] = ref[...]


def add_kernel(left, right, out):
    out[...] = left[...] + right[...]


def add_after(left, right, deps):
    inputs = [(whole(left.shape), left), (whole(right.shape), right)]
    return call(add_kernel, (1,), inputs, [(whole(left.shape), sds(left.shape, left.dtype))], deps=deps)[0]


def assemble_kernel(info, o4, rx, ry, ra, rb, out):
    depth = info[2]
    plane = info[3]
    for m in range(4):
        for n in range(4):
            if n < 3:
                value = (o4, rx, ry)[n][m]
            else:
                value = ra[m] if m < 2 else rb[m - 2]
            out[(depth ^ m) * 4 + (plane ^ n)] = value


def pack_kernel(info, time_qkv, space_qkv, space_proj, time_proj, up, time_vec, space_vec, mlp_vec, bias, send, keep):
    width = time_proj.shape[1]
    half = width // 2
    pieces = [time_qkv[:, n * half : (n + 1) * half] for n in range(6)]
    pieces += [space_qkv[:, n * half : (n + 1) * half] for n in range(6)]
    pieces += [space_proj[:, :half], space_proj[:, half:], time_proj[:, :half], time_proj[:, half:]]
    pieces += [up[:, n * half : (n + 1) * half] for n in range(8)]
    first = info[0] == 0
    at = 0
    for begin, count in ((0, 3), (6, 5), (16, 4)):
        for n in range(count):
            low, high = pieces[begin + n], pieces[begin + count + n]
            keep[:, at : at + half] = jnp.where(first, low, high)
            send[:, at : at + half] = jnp.where(first, high, low)
            at += half
    line = 0
    total = jnp.zeros((keep.shape[0], LANES), FLOAT)
    for source in (time_vec, space_vec, mlp_vec, bias):
        count = source.shape[0]
        lane = lax.broadcasted_iota(jnp.int32, (count, LANES), 1)
        chosen = (lane == row_index((count, LANES)) + line).astype(FLOAT)
        total = total + lax.dot_general(
            source[...].astype(FLOAT), chosen, (((0,), (0,)), ((), ())), preferred_element_type=FLOAT
        )
        line += count
    keep[:, at:] = total.astype(BRAIN)
    send[:, at:] = total.astype(BRAIN)


def turn_kernel(source, out):
    out[...] = source[...].astype(FLOAT).T


def join_kernel(info, keep, come, down, time_out, space_out, mlp_out):
    first = info[0] == 0
    width = down.shape[1]
    mine, far = keep[...].astype(FLOAT), come[...].astype(FLOAT)
    both = jnp.concatenate([jnp.where(first, mine, far), jnp.where(first, far, mine)], axis=0).astype(BRAIN)
    cut = both.shape[0]
    end = time_out.shape[1] - LANES
    time_out[:, :end] = both[:, :end]
    time_out[:, end:] = both[:, both.shape[1] - LANES :]
    space_out[...] = both[:, end : end + space_out.shape[1]]
    at = end + space_out.shape[1]
    mlp_out[:cut] = both[:, at : at + width]
    mlp_out[cut : 2 * cut] = both[:, at + width : at + 2 * width]
    mlp_out[2 * cut :] = down[...]


def added(*values):
    return sum(v.astype(FLOAT) for v in values).astype(BRAIN)


def reduce_first_kernel(info, mine, far, to_y, to_x, near_x, near_y, own):
    step = pl.program_id(0)
    plane = info[3]
    own[0] = added(mine[0, plane], far[0, plane])
    near_x[0] = added(mine[0, plane ^ 1], far[0, plane ^ 1])
    near_y[0] = added(mine[0, plane ^ 2], far[0, plane ^ 2])
    diagonal = added(mine[0, plane ^ 3], far[0, plane ^ 3])

    @pl.when(step < 2)
    def _():
        to_y[0] = diagonal

    @pl.when(step >= 2)
    def _():
        to_x[0] = diagonal


def reduce_second_kernel(near_x, near_y, from_y, from_x, out_x, out_y):
    step = pl.program_id(0)

    @pl.when(step < 2)
    def _():
        out_x[0] = added(near_x[0], from_y[0])
        out_y[0] = near_y[0]

    @pl.when(step >= 2)
    def _():
        out_x[0] = near_x[0]
        out_y[0] = added(near_y[0], from_x[0])


def reduce_third_kernel(info, own, from_x, from_y, first, second, others):
    for m in range(4):
        at = info[2] ^ m
        value = added(own[at], from_x[at], from_y[at])
        if m == 0:
            first[...] = value
        elif m == 1:
            second[...] = value
        else:
            others[m - 2] = value


def final_kernel(first, second, third, fourth, out):
    out[...] = (first[...].astype(FLOAT) + second[...].astype(FLOAT)) + (
        third[...].astype(FLOAT) + fourth[...].astype(FLOAT)
    )


def reduce_fourth_kernel(first, second, come, first_out, second_out):
    first_out[...] = first[...].astype(FLOAT) + come[0].astype(FLOAT)
    second_out[...] = added(second[...], come[1])


def clip_swap(values, bits, count):
    return lax.ppermute(values, "clip", [(i, i ^ bits) for i in range(count)])


def core_swap(values):
    return lax.ppermute(values, "frame", [(0, 1), (1, 0)])


class Near:
    def __init__(self, clips, info):
        self.clips = clips
        self.info = info
        self.core = lax.axis_index("frame")

    def swap(self, values, bits):
        return clip_swap(values, bits, self.clips)

    def in_order(self, mine, far, axis):
        return jnp.where(
            self.core == 0, jnp.concatenate([mine, far], axis=axis), jnp.concatenate([far, mine], axis=axis)
        )

    def stack(self, pieces, deps):
        shape = (len(pieces),) + pieces[0].shape
        return call(
            stack_kernel, (1,), [(whole(v.shape), v) for v in pieces], [(whole(shape), sds(shape, BRAIN))],
            micros=3, deps=deps,
        )[0]

    def depth_direct(self, own, deps):
        return self.stack([own] + [self.swap(own, 4 * m) for m in (1, 2, 3)], deps)

    def depth_in_order(self, own, deps):
        pieces = [own] + [self.swap(own, 4 * m) for m in (1, 2, 3)]
        shape = (4,) + own.shape
        return call(
            stack_at_kernel, (1,), [(smem(), self.info)] + [(whole(v.shape), v) for v in pieces],
            [(whole(shape), sds(shape, BRAIN))], micros=3, deps=deps,
        )[0]

    def depth_near(self, own, deps):
        return self.stack([own, self.swap(own, 4)], deps)

    def depth_far(self, two, deps):
        come = self.swap(two, 8)
        return self.stack([two[0], two[1], come[0], come[1]], deps)

    def plane_step(self, o4, deps):
        rx = self.swap(o4, 1)
        ry = self.swap(o4, 2)
        half = (2,) + o4.shape[1:]
        first = pl.BlockSpec(half, lambda s: (0, 0, 0))
        second = pl.BlockSpec(half, lambda s: (1, 0, 0))
        sx, sy = call(
            halves_kernel, (1,), [(first, rx), (second, ry)], [(whole(half), sds(half, BRAIN))] * 2, deps=deps
        )
        return rx, ry, sx, sy

    def diagonal_step(self, o4, planes, deps):
        rx, ry, sx, sy = planes
        pieces = (o4, rx, ry, self.swap(sx, 2), self.swap(sy, 1))
        shape = (self.clips,) + o4.shape[1:]
        return call(
            assemble_kernel, (1,), [(smem(), self.info)] + [(whole(v.shape), v) for v in pieces],
            [(whole(shape), sds(shape, BRAIN))], micros=3, deps=deps,
        )[0]

    def reduce_first(self, mine, far, deps, micros=20):
        block = mine.shape[1:]
        four = (4, 4) + block
        view = pl.BlockSpec((1, 4) + block, lambda s: (s, 0, 0, 0))
        one = lambda pick: pl.BlockSpec((1,) + block, lambda s: (pick(s), 0, 0))
        each = (one(lambda s: s), sds((4,) + block, BRAIN))
        return call(
            reduce_first_kernel, (4,),
            [(smem(), self.info), (view, mine.reshape(four)), (view, far.reshape(four))],
            [
                (one(lambda s: jnp.minimum(s, 1)), sds((2,) + block, BRAIN)),
                (one(lambda s: jnp.maximum(s - 2, 0)), sds((2,) + block, BRAIN)),
                each, each, each,
            ],
            micros=micros, deps=deps,
        )

    def reduce_second(self, near_x, near_y, to_y, to_x, deps):
        from_y, from_x = self.swap(to_y, 2), self.swap(to_x, 1)
        block = near_x.shape[1:]
        one = lambda pick: pl.BlockSpec((1,) + block, lambda s: (pick(s), 0, 0))
        each = one(lambda s: s)
        return call(
            reduce_second_kernel, (4,),
            [
                (each, near_x), (each, near_y), (one(lambda s: jnp.minimum(s, 1)), from_y),
                (one(lambda s: jnp.maximum(s - 2, 0)), from_x),
            ],
            [(each, sds(near_x.shape, BRAIN))] * 2, micros=20, deps=deps,
        )

    def reduce_third(self, own, near_x, near_y, deps):
        from_x, from_y = self.swap(near_x, 1), self.swap(near_y, 2)
        block = own.shape[1:]
        return call(
            reduce_third_kernel, (1,),
            [(smem(), self.info)] + [(whole(v.shape), v) for v in (own, from_x, from_y)],
            [(whole(shape), sds(shape, BRAIN)) for shape in (block, block, (2,) + block)],
            micros=20, deps=deps,
        )

    def reduce_fourth(self, first, second, others, deps):
        come = self.swap(others, 8)
        inputs = [(whole(v.shape), v) for v in (first, second, come)]
        outs = [(whole(first.shape), sds(first.shape, kind)) for kind in (FLOAT, BRAIN)]
        return call(reduce_fourth_kernel, (1,), inputs, outs, micros=20, deps=deps)

    def reduce_end(self, first, second):
        return first + self.swap(second, 4).astype(FLOAT)

    def reduce_direct(self, first, second, others, deps=()):
        pieces = [first, self.swap(second, 4), self.swap(others[0], 8), self.swap(others[1], 12)]
        inputs = [(whole(v.shape), v) for v in pieces]
        return call(final_kernel, (1,), inputs, [(whole(first.shape), sds(first.shape, FLOAT))], deps=deps)[0]

    def owner_rows(self, value):
        rows = value.shape[0] // 2
        mine = lax.dynamic_slice_in_dim(value, self.core * rows, rows, 0)
        theirs = lax.dynamic_slice_in_dim(value, (1 - self.core) * rows, rows, 0)
        return self.in_order(mine, core_swap(theirs), 1)


AXES = ("clip", "frame")


def body(
    clips, cores, clip_tokens, clip_class, output_grad, class_grad, clip_count,
    time_qkv, time_proj, time_vec, space_qkv, space_proj, space_vec, mlp_up, mlp_down, mlp_vec, mlp_bias,
):
    _, own, places_here, width = clip_tokens.shape
    rows = -(-(places_here + 1) // 16) * 16
    frames = own * cores
    wide = mlp_up.shape[1]
    cut = width // BLOCKS
    core = lax.axis_index("frame")
    place = lax.axis_index("clip")
    shard = place * cores + core
    leader = (core == 0).astype(jnp.int32)
    alive = (jnp.arange(1, dtype=jnp.int32) < clip_count[0]).astype(FLOAT)
    is_near = clips == 16 and cores == 2
    slot = core if is_near else core * 0
    info = jnp.stack([slot, leader, place // 4, place % 4, shard]).astype(jnp.int32)
    near = Near(clips, info) if is_near else None
    my_slot = info[0:1]
    far_slot = 1 - my_slot

    class_block = jnp.broadcast_to(clip_class[0][None, None], (own, 1, width))
    blank = jnp.zeros((own, rows - places_here - 1, width), BRAIN)
    tokens = jnp.concatenate([clip_tokens[0], class_block, blank], axis=1)
    last = (jnp.arange(own) == own - 1)[:, None, None]
    class_rows = jnp.where(last, class_grad[0][None, None], jnp.zeros((), BRAIN))
    grads = jnp.concatenate([output_grad[0], class_rows, blank], axis=1)

    bias_rows = wide // width
    zeros = jnp.zeros((8, width), FLOAT)
    flat = lambda v: v.reshape((own * rows,) + v.shape[2:])

    if near is not None:
        packed = (
            time_qkv, space_qkv, space_proj, time_proj, mlp_up, time_vec, space_vec, mlp_vec,
            mlp_bias.reshape(-1, bias_rows).T,
        )
        line = sds((time_qkv.shape[0], 6 * width + LANES), BRAIN)
        send, keep = call(
            pack_kernel, (1,), [(smem(), info)] + [(whole(v.shape), v) for v in packed],
            [(whole(line.shape), line), (whole(line.shape), line)],
        )
        shapes = [(cut, 3 * width // 2 + LANES), (cut, 5 * width // 2), (4 * cut, width)]
        time_own, space_own, mlp_own = call(
            join_kernel, (1,),
            [(smem(), info)] + [(whole(v.shape), v) for v in (keep, core_swap(send), mlp_down)],
            [(whole(shape), sds(shape, BRAIN)) for shape in shapes],
        )
        join = lambda two: tuple(h.reshape(width, h.shape[-1]) for h in two)
        time_line = near.depth_direct(time_own, [])
        all_tokens = jnp.concatenate([tokens, core_swap(gate(tokens, [time_own]))], axis=0)
        space_own = gate(space_own, [time_line])
        space_line = near.depth_direct(space_own, [])
        time_mine = near.diagonal_step(time_line, near.plane_step(time_line, []), [grads, all_tokens, space_line])
        space_line = gate(space_line, [time_mine])
        time_far = core_swap(time_mine)
        time_w = join((time_mine, time_far))
        vec_block = pl.BlockSpec((width, LANES), lambda s: (0, time_w[0].shape[1] // LANES - 1))
        vectors = call(
            turn_kernel, (1,), [(vec_block, time_w[0])], [(whole((LANES, width)), sds((LANES, width), FLOAT))],
            deps=[space_line],
        )[0]
        n_vec = time_vec.shape[0] + space_vec.shape[0] + mlp_vec.shape[0]
        bias = vectors[n_vec : n_vec + bias_rows].T.reshape(bias_rows, width)
        mlp_own = gate(mlp_own, [time_mine])
        mix_deps = [space_line, mlp_own]
    else:
        everywhere = lax.all_gather(tokens, "frame", axis=0, tiled=True)
        all_tokens = jnp.roll(everywhere, -core * own, axis=0)
        vec_shard = jnp.concatenate([time_vec, space_vec, mlp_vec], axis=0)
        blank_rows = jnp.zeros((16 - vec_shard.shape[0], width), FLOAT)
        space_shard = jnp.concatenate([space_qkv, space_proj, time_proj], axis=1)
        vectors = lax.all_gather(vec_shard, AXES, axis=1, tiled=True).astype(FLOAT)
        bias = lax.all_gather(mlp_bias, AXES, axis=0, tiled=True).astype(FLOAT).reshape(bias_rows, width)
        vectors = jnp.concatenate([vectors, blank_rows], axis=0)

        def halves(value):
            full = lax.all_gather(value, AXES, axis=0, tiled=True)
            half = full.shape[1] // 2
            return full[:, :half], full[:, half:]

        time_w, space_w = halves(time_qkv), halves(space_shard)
        up = lax.all_gather(mlp_up, AXES, axis=0, tiled=True).reshape(BLOCKS, cut, 2, 2, width)
        up = jnp.transpose(up, (2, 0, 3, 1, 4)).reshape(2, BLOCKS, 2 * cut, width)
        down = lax.all_gather(mlp_down, AXES, axis=0, tiled=True).reshape(BLOCKS, 2, 2 * cut, width)
        mlp_w = tuple(
            (jnp.concatenate([up[n], down[:, n]], axis=1).reshape(4, BLOCKS // 4, 4 * cut, width),) for n in (0, 1)
        )
        mix_deps = []

    frame_shape = (own, rows, width)
    out_shape = (own, places_here, width)
    all_shape = (frames, rows, width)
    heads = width // HEAD_DIM
    prob_shape = (own, frames, rows, LANES)
    sprob_shape = (own, heads, rows, rows)
    mixed_shape = (own, rows, 3 * width)
    hidden_shape = (own, rows, wide)
    sum_out = (whole((8, width)), sds((8, width), FLOAT))
    row_bytes = own * rows * width
    square = 2 * own * rows * width * width
    group = 2 if own % 2 == 0 else 1
    frames_in = lambda array, first=0: (per_frame(array.shape, first, group), array)
    low_out = lambda shape, first=0: (per_frame(shape, first, group), sds(shape, BRAIN))
    wide_out = lambda shape, first=0: (per_frame(shape, first, group), sds(shape, FLOAT))
    vec_in = (whole(vectors.shape), vectors)
    pair = lambda two: [(hbm(), two[0]), (hbm(), two[1])]
    time_held = [pltpu.VMEM((width, 3 * width), BRAIN), pltpu.SemaphoreType.DMA((2,))]
    space_held = [pltpu.VMEM((width, 5 * width), BRAIN), pltpu.SemaphoreType.DMA((2,))]
    mlp_held = [
        pltpu.VMEM((wide // width, 4, BLOCKS // 4, cut, width), BRAIN),
        pltpu.VMEM((4, BLOCKS // 4, 2, 2 * cut, width), BRAIN),
        pltpu.SemaphoreType.DMA((2, 15)),
    ]

    own_map = pl.BlockSpec((group, rows, width), lambda s: (jnp.minimum(s, own // group - 1), 0, 0))
    queries, key_rows, value_rows, time_low = call(
        functools.partial(time_mix_kernel, own // group), (frames // group,),
        [(smem(), info), frames_in(all_tokens), vec_in] + pair(time_w),
        [(own_map, sds(frame_shape, BRAIN)), low_out(all_shape), low_out(all_shape), (own_map, sds(frame_shape, BRAIN))],
        time_held, micros=1, deps=mix_deps,
    )

    if near is not None:
        mlp_line = near.depth_direct(mlp_own, [queries])
        space_mine = near.diagonal_step(space_line, near.plane_step(space_line, [queries]), [mlp_line])
        space_w = join((space_mine, core_swap(space_mine)))
        mlp_line = gate(mlp_line, [space_mine])

    parts = [(0, own)] if near is None else [(0, own // 2), (own // 2, own - own // 2)]
    deps = [] if near is None else [mlp_line]
    kept, class_own = (), zeros
    for first, count in parts:
        outs = call(
            functools.partial(attention_kernel, places_here), (count // group,),
            [
                (smem(), info), frames_in(tokens, first), vec_in, frames_in(queries, first),
                (whole(all_shape), key_rows), (whole(all_shape), value_rows), (whole((8, width)), class_own),
            ]
            + pair(space_w),
            [
                low_out(prob_shape, first), low_out(frame_shape, first), wide_out(frame_shape, first),
                low_out(frame_shape, first), low_out(mixed_shape, first), low_out(sprob_shape, first),
                low_out(frame_shape, first), wide_out(frame_shape, first), sum_out,
            ],
            space_held, micros=27 * count / own, deps=deps, previous=kept,
        )
        kept, class_own = tuple(outs[:-1]), outs[-1]
        if near is not None and first == 0:
            mlp_planes = near.plane_step(mlp_line, [class_own])
            deps = list(mlp_planes[2:])
    time_prob, time_att, after, space_low, space_mixed, space_prob, space_att, places = kept

    if near is not None:
        mlp_mine = near.diagonal_step(mlp_line, mlp_planes, [places])
        mlp_w = tuple((v.reshape(4, BLOCKS // 4, 4 * cut, width),) for v in (mlp_mine, core_swap(mlp_mine)))
        class_far = core_swap(class_own)
    else:
        class_far = lax.psum(class_own, "frame") - class_own
    class_row = jnp.broadcast_to(clip_class.astype(FLOAT), (8, width))
    small = whole((8, width))
    result, class_result, mlp_low, hidden, feed_grad, before_grad, rows_grad, mlp_sums = call(
        functools.partial(mlp_kernel, places_here, frames, len(mlp_w[0])), (own // group,),
        [
            (smem(), info), (smem(), alive), frames_in(places), frames_in(grads),
            (small, class_row), (small, class_own), (small, class_far), vec_in, (whole(bias.shape), bias),
        ]
        + [(hbm(), v) for v in mlp_w[0] + mlp_w[1]],
        [
            low_out(out_shape), sum_out, low_out(frame_shape), low_out(hidden_shape), low_out(frame_shape),
            low_out(hidden_shape), wide_out(frame_shape), sum_out,
        ],
        [pltpu.VMEM((wide // width, group * rows, width), FLOAT)] + mlp_held,
        micros=25,
    )

    mlp_mine, mlp_far = mlp_outer(my_slot, flat(mlp_low), flat(before_grad), flat(hidden), flat(feed_grad))
    class_block_at = places_here // 16
    class_spec = pl.BlockSpec((1, 16, width), lambda s: (own - 1, class_block_at, 0))

    def space_back(first, count, sums, deps, previous):
        return call(
            functools.partial(space_back_kernel, places_here, frames), (count // group,),
            [
                (smem(), info), frames_in(rows_grad, first), (class_spec, rows_grad), frames_in(after, first),
                frames_in(space_mixed, first), frames_in(space_prob, first), frames_in(space_att, first),
                vec_in, (small, sums),
            ]
            + pair(space_w),
            [
                low_out(frame_shape, first), low_out(mixed_shape, first), wide_out(frame_shape, first),
                low_out(frame_shape, first), low_out(frame_shape, first), sum_out,
            ],
            space_held, micros=30 * count / own, deps=deps, previous=previous,
        )

    half = own // 2
    if near is not None:
        outs = space_back(0, half, zeros, [mlp_far], ())
        mlp_a, mlp_b, mlp_x, mlp_y, mlp_own = near.reduce_first(mlp_mine, core_swap(mlp_far), [outs[0]])
        outs = space_back(half, own - half, outs[-1], [mlp_a, mlp_b], tuple(outs[:-1]))
        mlp_x, mlp_y = near.reduce_second(mlp_x, mlp_y, mlp_a, mlp_b, [outs[0]])
        time_deps = [mlp_x, mlp_y]
    else:
        outs = space_back(0, own, zeros, [], ())
        time_deps = []
    branch_grad, space_mixed_grad, after_grad, time_grad, time_att_grad, space_sums = outs

    space_mine, space_far = space_outer(
        my_slot, *[flat(v) for v in (space_low, space_mixed_grad, space_att, branch_grad, time_att, time_grad)],
        deps=time_deps,
    )
    time_deps = time_deps + [space_far]
    far_frames = frames - own
    lanes_of = lambda shape: pl.BlockSpec(shape[:-1] + (2 * LANES,), lambda s: (0,) * (len(shape) - 1) + (s,))
    lanes_in = lambda v: (lanes_of(v.shape), v)
    q_grad, own_grad, far_grad = call(
        time_back_kernel, (width // LANES // 2,),
        [
            lanes_in(queries), lanes_in(key_rows), lanes_in(value_rows), (whole(prob_shape), time_prob),
            lanes_in(time_att_grad),
        ],
        [
            (lanes_of(shape), sds(shape, BRAIN))
            for shape in (frame_shape, (2,) + frame_shape, (2, far_frames, rows, width))
        ],
        micros=19, deps=time_deps,
    )
    if near is not None:
        from_far = core_swap(far_grad)
        mlp_first, mlp_second, mlp_others = near.reduce_third(mlp_own, mlp_x, mlp_y, [q_grad])
        space_a, space_b, space_x, space_y, space_own = near.reduce_first(space_mine, core_swap(space_far), [mlp_second])
        mixed_deps = [space_own]
    else:
        mixed_deps = []
        padded = jnp.concatenate([jnp.zeros_like(own_grad), far_grad], axis=1)
        padded = jnp.roll(padded, core * own, axis=1)
        from_far = lax.psum_scatter(padded, "frame", scatter_dimension=1, tiled=True)
    pair_in = lambda v: (pl.BlockSpec((2, group, rows, width), lambda s: (0, s, 0, 0)), v)
    time_mixed_grad = call(
        mixed_grad_kernel, (own // group,), [frames_in(q_grad), pair_in(own_grad), pair_in(from_far)],
        [low_out(mixed_shape)], micros=3, deps=mixed_deps,
    )[0]
    outer = (flat(time_low), flat(time_mixed_grad))

    back_deps = [] if near is None else [mlp_second, space_a, space_b]
    token_grad, time_sums = call(
        time_mix_back_kernel, (own // group,),
        [(smem(), info), frames_in(tokens), vec_in, frames_in(time_mixed_grad), frames_in(after_grad)]
        + pair(time_w),
        [wide_out(out_shape), sum_out],
        time_held, micros=4, deps=back_deps,
    )
    bias_grad = mlp_sums[3 : 3 + bias_rows].reshape(width, bias_rows)
    n_sums = 13
    sums = call(
        sums_kernel, (1,), [(small, time_sums), (small, space_sums), (small, mlp_sums), (whole(bias_grad.shape), bias_grad)],
        [(whole((width, LANES)), sds((width, LANES), FLOAT))], [pltpu.VMEM((LANES, width), FLOAT)],
    )[0]

    if near is not None:
        space_x, space_y = near.reduce_second(space_x, space_y, space_a, space_b, [token_grad])
        mlp_grads = near.reduce_direct(mlp_first, mlp_second, mlp_others, [token_grad])
        time_mine, time_far = time_outer(my_slot, *outer, sums, deps=[space_x, space_y, mlp_grads])
        space_parts = near.reduce_third(space_own, space_x, space_y, [time_mine])
        time_a, time_b, time_x, time_y, time_own = near.reduce_first(
            time_mine, core_swap(time_far), [space_parts[1]]
        )
        time_x, time_y = near.reduce_second(time_x, time_y, time_a, time_b, [])
        time_parts = near.reduce_third(time_own, time_x, time_y, [])
        grad_space = near.reduce_direct(*space_parts)
        total = near.reduce_direct(*time_parts)
        grad_time, sums = total[:, : 3 * width], total[:, 3 * width :]
        grad_mlp_down = mlp_grads[2 * cut :]
        grad_mlp_up = near.owner_rows(jnp.concatenate([mlp_grads[:cut], mlp_grads[cut : 2 * cut]], axis=1))
        class_total = space_sums[6:7] + core_swap(space_sums)[6:7]
    else:
        send = lambda v: lax.psum_scatter(v, AXES, scatter_dimension=0, tiled=True).astype(FLOAT)
        spread = lambda mine, far: jnp.stack([mine, far], axis=1).reshape(width, mine.shape[2])
        time_mine, time_far = time_outer(my_slot, *outer, sums)
        up = jnp.stack([v[:, : 2 * cut].reshape(BLOCKS, 2, cut, width) for v in (mlp_mine, mlp_far)])
        grad_mlp_up = send(jnp.transpose(up, (1, 3, 0, 2, 4)).reshape(width, wide))
        grad_mlp_down = send(jnp.stack([v[:, 2 * cut :] for v in (mlp_mine, mlp_far)], axis=1).reshape(wide, width))
        grad_space = send(spread(space_mine, space_far))
        grad_time = send(spread(time_mine, time_far)[:, : 3 * width])
        class_total = lax.psum(space_sums[6:7], "frame")
        step = width // (clips * cores)
        sums = lax.dynamic_slice_in_dim(lax.psum(sums, AXES), shard * step, step, 0)
    class_in_grad = rows_grad[own - 1, places_here][None] + class_total
    lines = sums.T
    grad_time_vec, grad_space_vec, grad_mlp_vec = lines[:5], lines[5:10], lines[10:13]
    grad_mlp_bias = sums[:, n_sums : n_sums + bias_rows].reshape(-1)
    return (
        result[None],
        class_result[places_here % 8][None].astype(BRAIN),
        token_grad[None],
        class_in_grad,
        grad_time,
        grad_space[:, 4 * width :],
        grad_time_vec,
        grad_space[:, : 3 * width],
        grad_space[:, 3 * width : 4 * width],
        grad_space_vec,
        grad_mlp_up,
        grad_mlp_down,
        grad_mlp_vec,
        grad_mlp_bias,
    )


def solution(mesh):
    both = ("clip", "frame")
    rows = P(both, None)
    columns = P(None, both)
    weights = (rows, rows, columns, rows, rows, columns, rows, rows, columns, P(both))
    block = P("clip", "frame", None, None)
    classes = P("clip", None)
    return jax.shard_map(
        functools.partial(body, mesh.shape["clip"], mesh.shape["frame"]),
        mesh=mesh,
        in_specs=(block, classes, block, classes, P("clip")) + weights,
        out_specs=(block, classes, block, classes) + weights,
        check_vma=False,
    )
```

```python
import functools

import jax
import jax.numpy as jnp
from jax import lax
from jax.experimental import pallas as pl
from jax.experimental.pallas import tpu as pltpu
from jax.sharding import PartitionSpec as P

HEAD_DIM = 64
EPSILON = 1e-06
FLOAT = jnp.float32
BRAIN = jnp.bfloat16
LANES = 128
BLOCKS = 16
RATE = 1e9
VMEM_BYTES = 60 * 1024 * 1024


def nn(left, right):
    return lax.dot_general(left, right, (((1,), (0,)), ((), ())), preferred_element_type=FLOAT)


def nt(left, right):
    return lax.dot_general(left, right, (((1,), (1,)), ((), ())), preferred_element_type=FLOAT)


def tn(left, right):
    return lax.dot_general(left, right, (((0,), (0,)), ((), ())), preferred_element_type=FLOAT)


def unit_of(values):
    average = jnp.mean(values, axis=-1, keepdims=True)
    centred = values - average
    spread = jnp.mean(centred * centred, axis=-1, keepdims=True)
    inverse = lax.rsqrt(spread + EPSILON)
    return centred * inverse, inverse


def norm_back(unit, inverse, gain, upstream):
    scaled = upstream * gain
    inner = jnp.mean(scaled, axis=-1, keepdims=True)
    along = jnp.mean(scaled * unit, axis=-1, keepdims=True)
    return inverse * (scaled - inner - unit * along)


def column_sum(values):
    return jnp.sum(values, axis=0, keepdims=True)


def row_index(shape):
    return lax.broadcasted_iota(jnp.int32, shape, 0)


def head_map(width, first=0):
    lane = lax.broadcasted_iota(jnp.int32, (width, LANES), 0) // HEAD_DIM + first
    head = lax.broadcasted_iota(jnp.int32, (width, LANES), 1)
    return (lane == head).astype(FLOAT).astype(BRAIN)


def head_spread(width, first=0):
    head = lax.broadcasted_iota(jnp.int32, (LANES, width), 0)
    lane = lax.broadcasted_iota(jnp.int32, (LANES, width), 1) // HEAD_DIM + first
    return (lane == head).astype(FLOAT).astype(BRAIN)


def column_copies(core, mine, other, held, sems):
    half = held.shape[1] // 2
    copies = []
    for n, (source, slot) in enumerate(((mine, core), (other, 1 - core))):
        target = held.at[:, pl.ds(pl.multiple_of(slot * half, LANES), half)]
        copies.append(pltpu.make_async_copy(source.at[:, :half], target, sems.at[n]))
    return copies


def mlp_copies(core, plane, mine, other, up, down, sems):
    cut = up.shape[3]
    ups, downs = [], []
    for k, (sources, slot) in enumerate(((mine, core), (other, 1 - core))):
        for n, source in enumerate(sources):
            if len(sources) == 1:
                at, tail = (), (slice(None),)
            else:
                at, tail = ((slice(None), slice(0, 2), slice(2, 4))[max(n - 2, 0)], plane ^ min(n, 3)), ()
            rows = lambda low, high: source.at[(slice(None),) + tail + (slice(low, high),)]
            for t in (0, 1):
                part = up.at[(2 * slot + t,) + at]
                ups.append(pltpu.make_async_copy(rows(t * cut, (t + 1) * cut), part, sems.at[k, 3 * n + t]))
            part = down.at[at + (slot,)] if at else down.at[:, :, slot]
            downs.append(pltpu.make_async_copy(rows(2 * cut, 4 * cut), part, sems.at[k, 3 * n + 2]))
    return ups, downs


def start_first(copies):
    @pl.when(pl.program_id(0) == 0)
    def _():
        for copy in copies:
            copy.start()


def wait_first(copies):
    @pl.when(pl.program_id(0) == 0)
    def _():
        for copy in copies:
            copy.wait()


def merged(ref):
    return ref[...].reshape(ref.shape[0] * ref.shape[1], ref.shape[2])


def store(ref, value):
    ref[...] = value.astype(ref.dtype).reshape(ref.shape)


def marks(count, rows, low, high):
    index = row_index((count * rows, 1))
    found = (index >= low) & (index < high)
    for n in range(1, count):
        found = found | ((index >= n * rows + low) & (index < n * rows + high))
    return found


def time_mix_kernel(own_steps, info, tokens, vectors, w_mine, w_other, q_out, k_out, v_out, low_out, held, sems):
    step = pl.program_id(0)
    width = tokens.shape[-1]

    copies = column_copies(info[0], w_mine, w_other, held, sems)
    start_first(copies)
    unit, _ = unit_of(merged(tokens).astype(FLOAT))
    low = (unit * vectors[0:1] + vectors[1:2]).astype(BRAIN)
    wait_first(copies)
    store(k_out, nn(low, held[:, width : 2 * width]))
    store(v_out, nn(low, held[:, 2 * width :]) + vectors[3:4])

    @pl.when(step < own_steps)
    def _():
        queries = (nn(low, held[:, :width]) + vectors[2:3]).astype(BRAIN)
        store(q_out, queries * jnp.asarray(HEAD_DIM ** (-0.5), BRAIN))
        store(low_out, low)


def tree_sum(values):
    values = list(values)
    while len(values) > 1:
        values = [a + b for a, b in zip(values[::2], values[1::2])] + values[len(values) & ~1 :]
    return values[0]


def attention_kernel(
    places_here, info, tokens, vectors, q_in, k_in, v_in, begin, sw_mine, sw_other,
    prob_out, att_out, after_out, low_out, mixed_out, sprob_out, satt_out, places_out, class_out,
    held, sems,
):
    step = pl.program_id(0)
    frames = k_in.shape[0]
    count, rows, width = tokens.shape
    core = info[0]

    copies = column_copies(core, sw_mine, sw_other, held, sems)
    start_first(copies)
    mapping = head_map(width)
    spread = head_spread(width)
    for n in range(count):
        queries = q_in[n]
        scores = [nn(queries * k_in[g], mapping) for g in range(frames)]
        top = functools.reduce(jnp.maximum, scores)
        powers = [jnp.exp(s - top) for s in scores]
        scale = 1.0 / sum(powers)
        parts = []
        for g in range(frames):
            prob = (powers[g] * scale).astype(BRAIN)
            prob_out[n, g] = prob
            parts.append(nn(prob, spread).astype(BRAIN) * v_in[g])
        att_out[n] = tree_sum(parts)
    wait_first(copies)
    attended = merged(att_out)
    place = marks(count, rows, 0, places_here)
    base = merged(tokens).astype(FLOAT)
    after = jnp.where(place, base + (nn(attended, held[:, 4 * width :]) + vectors[4:5]), base)
    store(after_out, after)
    unit, _ = unit_of(after)
    low = (unit * vectors[5:6] + vectors[6:7]).astype(BRAIN)
    store(low_out, low)
    shape = (count, rows, width)
    queries = (nn(low, held[:, :width]) + vectors[7:8]).astype(BRAIN) * jnp.asarray(HEAD_DIM ** (-0.5), BRAIN)
    mixed_out[:, :, :width] = queries.reshape(shape)
    mixed_out[:, :, width : 2 * width] = nn(low, held[:, width : 2 * width]).astype(BRAIN).reshape(shape)
    mixed_out[:, :, 2 * width :] = (
        (nn(low, held[:, 2 * width : 3 * width]) + vectors[8:9]).astype(BRAIN).reshape(shape)
    )
    lane = lax.broadcasted_iota(jnp.int32, (1, LANES), 1)
    masks = [(lane // HEAD_DIM == e).astype(FLOAT).astype(BRAIN) for e in (0, 1)]
    key_ok = row_index((rows, 1)) <= places_here
    for n in range(count):
        for pair in range(width // LANES):
            at = pair * LANES
            q2 = mixed_out[n, :, at : at + LANES]
            k2 = mixed_out[n, :, width + at : width + at + LANES]
            v2 = mixed_out[n, :, 2 * width + at : 2 * width + at + LANES]
            result = []
            for e in (0, 1):
                logits = jnp.where(key_ok, nt(k2, q2 * masks[e]), -1e30)
                power = jnp.exp(logits - jnp.max(logits, axis=0, keepdims=True))
                prob = (power * (1.0 / jnp.sum(power, axis=0, keepdims=True))).astype(BRAIN)
                sprob_out[n, 2 * pair + e] = prob
                result.append(tn(prob, v2))
            satt_out[n, :, at : at + LANES] = jnp.where(lane < HEAD_DIM, result[0], result[1]).astype(BRAIN)
    spatial = nn(merged(satt_out), held[:, 3 * width : 4 * width]) + vectors[9:10]
    store(places_out, jnp.where(place, after, 0.0) + spatial)

    @pl.when(step == 0)
    def _():
        class_out[...] = begin[...]

    class_row = column_sum(jnp.where(marks(count, rows, places_here, places_here + 1), spatial, 0.0))
    class_out[0:1] = class_out[0:1] + class_row


def gelu_parts(values):
    half = 0.5 + 0.5 * lax.erf(values * (0.5 ** 0.5))
    density = jnp.exp(values * values * (-0.5)) * (0.5 / 3.141592653589793) ** 0.5
    return values * half, half + values * density


def mlp_kernel(
    places_here, all_frames, pieces, info, alive, places, grads, class_row, class_own, class_far, vectors, bias,
    *others,
):
    mine, other, others = others[:pieces], others[pieces : 2 * pieces], others[2 * pieces :]
    out, class_out, low_out, hidden_out, feed_out, before_out, rows_out, sums, slopes, up, down, sems = others
    step = pl.program_id(0)
    count, rows, width = places.shape
    core = info[0]

    ups, downs = mlp_copies(core, info[3], mine, other, up, down, sems)
    start_first(ups + downs)

    @pl.when(step == 0)
    def _():
        sums[...] = jnp.zeros_like(sums)

    class_mid = class_row[0:1] + (class_own[0:1] + class_far[0:1]) * all_frames ** (-0.5)
    last = (count - 1) * rows + places_here
    is_class = (row_index((count * rows, 1)) == last) & (step == pl.num_programs(0) - 1)
    kept = jnp.logical_not(marks(count, rows, places_here, places_here + 1) & (info[1] == 0))
    values = jnp.where(is_class, class_mid, merged(places))
    unit, inverse = unit_of(values)
    low = (unit * vectors[10:11] + vectors[11:12]).astype(BRAIN)
    store(low_out, low)
    feed = jnp.zeros((count * rows, width), FLOAT)
    chunks = hidden_out.shape[-1] // width
    wait_first(ups)
    for j in range(chunks):
        before = nn(low, up[j].reshape(width, width)) + bias[j : j + 1]
        hidden, slope = gelu_parts(before)
        hidden = hidden.astype(BRAIN)
        hidden_out[:, :, j * width : (j + 1) * width] = hidden.reshape(count, rows, width)
        slopes[j] = slope
        if j == 0:
            wait_first(downs)
        feed = feed + nn(hidden, down[j].reshape(width, width))
    result = ((values + (feed + vectors[12:13])) * alive[0]).reshape(count, rows, width)
    out[...] = result[:, :places_here].astype(BRAIN)
    class_out[...] = result[count - 1, places_here - places_here % 8 : places_here - places_here % 8 + 8]

    row_grad = merged(grads).astype(FLOAT) * alive[0]
    feed_grad = row_grad.astype(BRAIN)
    feed_kept = jnp.where(kept, row_grad, 0.0).astype(BRAIN)
    store(feed_out, feed_kept)
    sums[2:3] = sums[2:3] + column_sum(feed_kept.astype(FLOAT))
    upstream = jnp.zeros((count * rows, width), FLOAT)
    for j in range(chunks):
        hidden_grad = nt(feed_grad, down[j].reshape(width, width))
        before_grad = (hidden_grad * slopes[j]).astype(BRAIN)
        before_kept = jnp.where(kept, before_grad.astype(FLOAT), 0.0)
        before_out[:, :, j * width : (j + 1) * width] = before_kept.astype(BRAIN).reshape(count, rows, width)
        sums[3 + j : 4 + j] = sums[3 + j : 4 + j] + column_sum(before_kept)
        upstream = upstream + nt(before_grad, up[j].reshape(width, width))
    store(rows_out, row_grad + norm_back(unit, inverse, vectors[10:11], upstream))
    upstream = jnp.where(kept, upstream, 0.0)
    sums[0:1] = sums[0:1] + column_sum(upstream * unit)
    sums[1:2] = sums[1:2] + column_sum(upstream)


def space_back_kernel(
    places_here, all_frames, info, rows_grad, class_grad, after, mixed, sprob, satt, vectors, begin,
    sw_mine, sw_other,
    branch_out, mixed_out, after_out, time_out, att_out, sums, held, sems,
):
    step = pl.program_id(0)
    count, rows, width = after.shape
    core = info[0]

    copies = column_copies(core, sw_mine, sw_other, held, sems)
    start_first(copies)

    @pl.when(step == 0)
    def _():
        sums[...] = begin[...]

    place = marks(count, rows, 0, places_here)
    class_at = marks(count, rows, places_here, places_here + 1)
    offset = places_here % 16
    share = class_grad[0, offset : offset + 1] * all_frames ** (-0.5)
    direct = jnp.where(place, merged(rows_grad), 0.0)
    branch = jnp.where(class_at, share, direct).astype(BRAIN)
    store(branch_out, branch)
    sums[4:5] = sums[4:5] + column_sum(branch.astype(FLOAT))
    unit, inverse = unit_of(merged(after))
    wait_first(copies)
    att_grad = nt(branch, held[:, 3 * width : 4 * width]).astype(BRAIN)
    store(att_out, att_grad)
    spread = head_spread(width)
    lane = lax.broadcasted_iota(jnp.int32, (1, LANES), 1)
    masks = [(lane // HEAD_DIM == e).astype(FLOAT).astype(BRAIN) for e in (0, 1)]
    left = lane < HEAD_DIM
    for n in range(count):
        product = att_out[n].astype(FLOAT) * satt[n].astype(FLOAT)
        high = product.astype(BRAIN)
        rowdots = nt(spread, high) + nt(spread, (product - high.astype(FLOAT)).astype(BRAIN))
        for pair in range(width // LANES):
            at = pair * LANES
            a2 = att_out[n, :, at : at + LANES]
            q2 = mixed[n, :, at : at + LANES]
            k2 = mixed[n, :, width + at : width + at + LANES]
            v2 = mixed[n, :, 2 * width + at : 2 * width + at + LANES]
            queries, key_rows, value_rows = [], [], []
            for e in (0, 1):
                head = 2 * pair + e
                prob = sprob[n, head]
                prob_grad = nt(v2, a2 * masks[e])
                score = (prob.astype(FLOAT) * (prob_grad - rowdots[head : head + 1])).astype(BRAIN)
                queries.append(tn(score, k2))
                key_rows.append(nn(score, q2))
                value_rows.append(nn(prob, a2))
            q_grad = (jnp.where(left, queries[0], queries[1]) * HEAD_DIM ** (-0.5)).astype(BRAIN)
            k_grad = jnp.where(left, key_rows[0], key_rows[1]).astype(BRAIN)
            v_grad = jnp.where(left, value_rows[0], value_rows[1]).astype(BRAIN)
            mixed_out[n, :, at : at + LANES] = q_grad
            mixed_out[n, :, width + at : width + at + LANES] = k_grad
            mixed_out[n, :, 2 * width + at : 2 * width + at + LANES] = v_grad
    mixed_grad = merged(mixed_out)
    sums[2:3] = sums[2:3] + column_sum(mixed_grad[:, :width].astype(FLOAT))
    sums[3:4] = sums[3:4] + column_sum(mixed_grad[:, 2 * width :].astype(FLOAT))
    upstream = nt(mixed_grad, held[:, : 3 * width])
    inner = norm_back(unit, inverse, vectors[5:6], upstream)
    sums[0:1] = sums[0:1] + column_sum(upstream * unit)
    sums[1:2] = sums[1:2] + column_sum(upstream)
    sums[6:7] = sums[6:7] + column_sum(jnp.where(class_at, inner, 0.0))
    after_grad = jnp.where(place, direct + inner, 0.0)
    store(after_out, after_grad)
    low = after_grad.astype(BRAIN)
    store(time_out, low)
    sums[5:6] = sums[5:6] + column_sum(low.astype(FLOAT))
    store(att_out, nt(low, held[:, 4 * width :]))


def time_back_kernel(q_in, k_in, v_in, prob_in, att_in, q_out, own_out, far_out):
    own, rows, width = q_in.shape
    frames = k_in.shape[0]
    first = pl.program_id(0) * (width // HEAD_DIM)
    mapping = head_map(width, first)
    spread = head_spread(width, first)
    size = 16

    def chunk(index, carry):
        at = pl.ds(pl.multiple_of(index * size, size), size)
        values = [v_in[g, at] for g in range(frames)]
        att = [att_in[f, at] for f in range(own)]
        products = jnp.concatenate([att[f] * values[g] for f in range(own) for g in range(frames)], axis=0)
        prob_grad = nn(products, mapping)
        probs = [prob_in[f, g, at] for f in range(own) for g in range(frames)]
        scores = []
        for f in range(own):
            wide = [probs[f * frames + g].astype(FLOAT) for g in range(frames)]
            weighted = [
                wide[g] * prob_grad[(f * frames + g) * size : (f * frames + g + 1) * size] for g in range(frames)
            ]
            rowdot = sum(weighted)
            scores += [(weighted[g] - wide[g] * rowdot).astype(BRAIN) for g in range(frames)]
        score_wide = nn(jnp.concatenate(scores, axis=0), spread).astype(BRAIN)
        prob_wide = nn(jnp.concatenate(probs, axis=0), spread).astype(BRAIN)

        def part(array, f, g):
            return array[(f * frames + g) * size : (f * frames + g + 1) * size]

        keys = [k_in[g, at] for g in range(frames)]
        for f in range(own):
            total = tree_sum(part(score_wide, f, g) * keys[g] for g in range(frames))
            q_out[f, at] = total * jnp.asarray(HEAD_DIM ** (-0.5), BRAIN)
        queries = [q_in[f, at] for f in range(own)]
        for g in range(frames):
            key_grad = tree_sum(part(score_wide, f, g) * queries[f] for f in range(own))
            value_grad = tree_sum(part(prob_wide, f, g) * att[f] for f in range(own))
            if g < own:
                own_out[0, g, at] = key_grad
                own_out[1, g, at] = value_grad
            else:
                far_out[0, g - own, at] = key_grad
                far_out[1, g - own, at] = value_grad
        return carry

    lax.fori_loop(0, rows // size, chunk, 0, unroll=True)


def time_mix_back_kernel(info, tokens, vectors, mixed, after_grad, w_mine, w_other, token_out, sums, held, sems):
    step = pl.program_id(0)
    width = tokens.shape[-1]

    copies = column_copies(info[0], w_mine, w_other, held, sems)
    start_first(copies)

    @pl.when(step == 0)
    def _():
        sums[...] = jnp.zeros_like(sums)

    mixed_grad = merged(mixed)
    sums[2:3] = sums[2:3] + column_sum(mixed_grad[:, :width].astype(FLOAT))
    sums[3:4] = sums[3:4] + column_sum(mixed_grad[:, 2 * width :].astype(FLOAT))
    unit, inverse = unit_of(merged(tokens).astype(FLOAT))
    wait_first(copies)
    upstream = nt(mixed_grad, held[...])
    result = merged(after_grad) + norm_back(unit, inverse, vectors[0:1], upstream)
    token_out[...] = result.reshape(mixed.shape[:2] + (width,))[:, : token_out.shape[1]]
    sums[0:1] = sums[0:1] + column_sum(upstream * unit)
    sums[1:2] = sums[1:2] + column_sum(upstream)


def mixed_grad_kernel(queries, own, far, out):
    width = queries.shape[2]
    out[:, :, :width] = queries[...]
    out[:, :, width : 2 * width] = (own[0].astype(FLOAT) + far[0].astype(FLOAT)).astype(BRAIN)
    out[:, :, 2 * width :] = (own[1].astype(FLOAT) + far[1].astype(FLOAT)).astype(BRAIN)


def sums_kernel(time_sums, space_sums, mlp_sums, bias, out, lines):
    lines[...] = jnp.zeros_like(lines)
    lines[0:4] = time_sums[0:4]
    lines[4:5] = space_sums[5:6]
    lines[5:10] = space_sums[0:5]
    lines[10:13] = mlp_sums[0:3]
    count = bias.shape[1]
    place = lax.broadcasted_iota(jnp.int32, (count, LANES), 1) == row_index((count, LANES)) + 13
    spread = lax.dot_general(
        bias[...], place.astype(FLOAT), (((1,), (0,)), ((), ())), preferred_element_type=FLOAT,
        precision=lax.Precision.HIGHEST,
    )
    out[...] = lines[...].T + spread


def halves_kernel(left, right, left_out, right_out):
    left_out[...] = left[...]
    right_out[...] = right[...]


def share_rows(info, value, mine, other, at=slice(None)):
    value = value.reshape(mine.shape[0], 2, mine.shape[1], value.shape[-1])
    first = info[0] == 0
    mine[:, :, at] = jnp.where(first, value[:, 0], value[:, 1]).astype(BRAIN)
    other[:, :, at] = jnp.where(first, value[:, 1], value[:, 0]).astype(BRAIN)


def time_outer_kernel(info, left, right, sums, mine, other):
    step = pl.program_id(0)
    width = left.shape[1]

    for n in range(3):

        @pl.when(step == n)
        def _():
            share_rows(info, tn(left[...], right[...]), mine, other, slice(n * width, (n + 1) * width))

    @pl.when(step == 0)
    def _():
        share_rows(info, sums[...], mine, other, slice(3 * width, 3 * width + sums.shape[1]))


def space_outer_kernel(info, low, mixed, att, branch, time_att, time_grad, mine, other):
    step = pl.program_id(0)

    @pl.when(step < 3)
    def _():
        share_rows(info, tn(low[...], mixed[...]), mine, other)

    @pl.when(step == 3)
    def _():
        share_rows(info, tn(att[...], branch[...]), mine, other)

    @pl.when(step == 4)
    def _():
        share_rows(info, tn(time_att[...], time_grad[...]), mine, other)


def mlp_outer_kernel(info, low, before, hidden, feed, mine, other, turned, ups, downs, sems):
    step = pl.program_id(0)
    steps = ups.shape[0]
    blocks, cut, width = ups.shape[1:]
    per = downs.shape[2]

    @pl.when(step == 0)
    def _():
        turned[...] = low[...].T

    ups[step] = nn(turned[...], before[...]).astype(BRAIN).reshape(blocks, cut, width)
    value = tn(hidden[...], feed[...]).astype(BRAIN).reshape(per, 2, 2 * cut, width)
    downs[step, 0] = value[:, 0]
    downs[step, 1] = value[:, 1]

    for n in range(steps):
        targets = (mine, other)
        for k, slot in ((0, info[0]), (1, 1 - info[0])):
            up_copy = pltpu.make_async_copy(
                ups.at[n], targets[k].at[:, (n % 2) * cut : (n % 2 + 1) * cut], sems.at[0, n]
            )
            down_copy = pltpu.make_async_copy(
                downs.at[n, slot], targets[k].at[n * per : (n + 1) * per, 2 * cut :], sems.at[1 + k, n]
            )

            @pl.when((step == n) & (slot == n // 2))
            def _():
                up_copy.start()

            @pl.when(step == n)
            def _():
                down_copy.start()

            @pl.when((step == steps - 1) & (slot == n // 2))
            def _():
                up_copy.wait()

            @pl.when(step == steps - 1)
            def _():
                down_copy.wait()


def smem():
    return pl.BlockSpec(memory_space=pltpu.SMEM)


def hbm():
    return pl.BlockSpec(memory_space=pl.ANY)


def whole(shape):
    return pl.BlockSpec(shape, lambda *_: (0,) * len(shape))


def per_frame(shape, first=0, count=1):
    return pl.BlockSpec((count,) + shape[1:], lambda s: (s + first // count,) + (0,) * (len(shape) - 1))


def sds(shape, kind):
    return jax.ShapeDtypeStruct(shape, kind)


def call(kernel, grid, inputs, outputs, scratch=(), micros=2, deps=(), previous=(), prefetch=0):
    count = len(inputs)
    skip = len(previous) + len(deps)

    def inner(*refs):
        kernel(*refs[:count], *refs[count + skip :])

    specs = [spec for spec, _ in inputs[prefetch:]] + [hbm()] * skip
    common = dict(
        name=getattr(kernel, "func", kernel).__name__,
        out_shape=[shape for _, shape in outputs],
        compiler_params=pltpu.CompilerParams(vmem_limit_bytes=VMEM_BYTES),
        input_output_aliases={count + n: n for n in range(len(previous))},
        cost_estimate=pl.CostEstimate(flops=int(micros * RATE), bytes_accessed=1, transcendentals=0),
    )
    places = dict(grid=grid, in_specs=specs, out_specs=[spec for spec, _ in outputs], scratch_shapes=list(scratch))
    if prefetch:
        common["grid_spec"] = pltpu.PrefetchScalarGridSpec(num_scalar_prefetch=prefetch, **places)
    else:
        common.update(places)
    return pl.pallas_call(inner, **common)(*[array for _, array in inputs], *previous, *deps)


def time_outer(slot, left, right, sums, deps=()):
    rows, width = left.shape
    wide = right.shape[1]
    shape = (BLOCKS, width // (2 * BLOCKS), wide + sums.shape[1])
    return call(
        time_outer_kernel, (3,),
        [
            (smem(), slot), (whole(left.shape), left), (pl.BlockSpec((rows, width), lambda s: (0, s)), right),
            (whole(sums.shape), sums),
        ],
        [(whole(shape), sds(shape, BRAIN))] * 2, micros=8, deps=deps,
    )


def space_outer(slot, low, mixed, *others, deps=()):
    rows, width = low.shape
    shape = (BLOCKS, width // (2 * BLOCKS), width)
    moving = pl.BlockSpec((rows, width), lambda s: (0, jnp.minimum(s, 2)))
    return call(
        space_outer_kernel, (5,),
        [(smem(), slot), (whole(low.shape), low), (moving, mixed)] + [(whole(v.shape), v) for v in others],
        [(pl.BlockSpec(shape, lambda s: (0, 0, s)), sds(shape[:2] + (5 * width,), BRAIN))] * 2, micros=12, deps=deps,
    )


def mlp_outer(slot, low, before, hidden, feed, deps=()):
    rows, width = low.shape
    wide = hidden.shape[1]
    cut = width // BLOCKS
    shape = (BLOCKS, 4 * cut, width)
    fixed = pl.BlockSpec((rows, width), lambda s, info: (0, 0))
    moving = pl.BlockSpec((rows, width), lambda s, info: (0, s))
    return call(
        mlp_outer_kernel, (wide // width,),
        [(None, slot), (fixed, low), (moving, before), (moving, hidden), (fixed, feed)],
        [(hbm(), sds(shape, BRAIN))] * 2,
        [
            pltpu.VMEM((width, rows), BRAIN),
            pltpu.VMEM((wide // width, BLOCKS, cut, width), BRAIN),
            pltpu.VMEM((wide // width, 2, BLOCKS * width // wide, 2 * cut, width), BRAIN),
            pltpu.SemaphoreType.DMA((3, wide // width)),
        ],
        micros=21, deps=deps, prefetch=1,
    )


def gate(value, deps):
    return pl.pallas_call(
        lambda source, *refs: None,
        in_specs=[hbm()] * (1 + len(deps)),
        out_specs=hbm(),
        out_shape=sds(value.shape, value.dtype),
        input_output_aliases={0: 0},
    )(value, *deps)


def stack_at_kernel(info, *refs):
    for n, ref in enumerate(refs[:-1]):
        refs[-1][info[2] ^ n] = ref[...]


def stack_kernel(*refs):
    for n, ref in enumerate(refs[:-1]):
        refs[-1][n] = ref[...]


def add_kernel(left, right, out):
    out[...] = left[...] + right[...]


def add_after(left, right, deps):
    inputs = [(whole(left.shape), left), (whole(right.shape), right)]
    return call(add_kernel, (1,), inputs, [(whole(left.shape), sds(left.shape, left.dtype))], deps=deps)[0]


def assemble_kernel(info, o4, rx, ry, ra, rb, out):
    depth = info[2]
    plane = info[3]
    for m in range(4):
        for n in range(4):
            if n < 3:
                value = (o4, rx, ry)[n][m]
            else:
                value = ra[m] if m < 2 else rb[m - 2]
            out[(depth ^ m) * 4 + (plane ^ n)] = value


def pack_kernel(info, time_qkv, space_qkv, space_proj, time_proj, up, time_vec, space_vec, mlp_vec, bias, send, keep):
    width = time_proj.shape[1]
    half = width // 2
    pieces = [time_qkv[:, n * half : (n + 1) * half] for n in range(6)]
    pieces += [space_qkv[:, n * half : (n + 1) * half] for n in range(6)]
    pieces += [space_proj[:, :half], space_proj[:, half:], time_proj[:, :half], time_proj[:, half:]]
    pieces += [up[:, n * half : (n + 1) * half] for n in range(8)]
    first = info[0] == 0
    at = 0
    for begin, count in ((0, 3), (6, 5), (16, 4)):
        for n in range(count):
            low, high = pieces[begin + n], pieces[begin + count + n]
            keep[:, at : at + half] = jnp.where(first, low, high)
            send[:, at : at + half] = jnp.where(first, high, low)
            at += half
    line = 0
    total = jnp.zeros((keep.shape[0], LANES), FLOAT)
    for source in (time_vec, space_vec, mlp_vec, bias):
        count = source.shape[0]
        lane = lax.broadcasted_iota(jnp.int32, (count, LANES), 1)
        chosen = (lane == row_index((count, LANES)) + line).astype(FLOAT)
        total = total + lax.dot_general(
            source[...].astype(FLOAT), chosen, (((0,), (0,)), ((), ())), preferred_element_type=FLOAT
        )
        line += count
    keep[:, at:] = total.astype(BRAIN)
    send[:, at:] = total.astype(BRAIN)


def turn_kernel(source, out):
    out[...] = source[...].astype(FLOAT).T


def join_kernel(info, keep, come, down, time_out, space_out, mlp_out):
    first = info[0] == 0
    width = down.shape[1]
    mine, far = keep[...].astype(FLOAT), come[...].astype(FLOAT)
    both = jnp.concatenate([jnp.where(first, mine, far), jnp.where(first, far, mine)], axis=0).astype(BRAIN)
    cut = both.shape[0]
    end = time_out.shape[1] - LANES
    time_out[:, :end] = both[:, :end]
    time_out[:, end:] = both[:, both.shape[1] - LANES :]
    space_out[...] = both[:, end : end + space_out.shape[1]]
    at = end + space_out.shape[1]
    mlp_out[:cut] = both[:, at : at + width]
    mlp_out[cut : 2 * cut] = both[:, at + width : at + 2 * width]
    mlp_out[2 * cut :] = down[...]


def added(*values):
    return sum(v.astype(FLOAT) for v in values).astype(BRAIN)


def reduce_first_kernel(info, mine, far, to_y, to_x, near_x, near_y, own):
    step = pl.program_id(0)
    plane = info[3]
    own[0] = added(mine[0, plane], far[0, plane])
    near_x[0] = added(mine[0, plane ^ 1], far[0, plane ^ 1])
    near_y[0] = added(mine[0, plane ^ 2], far[0, plane ^ 2])
    diagonal = added(mine[0, plane ^ 3], far[0, plane ^ 3])

    @pl.when(step < 2)
    def _():
        to_y[0] = diagonal

    @pl.when(step >= 2)
    def _():
        to_x[0] = diagonal


def reduce_second_kernel(near_x, near_y, from_y, from_x, out_x, out_y):
    step = pl.program_id(0)

    @pl.when(step < 2)
    def _():
        out_x[0] = added(near_x[0], from_y[0])
        out_y[0] = near_y[0]

    @pl.when(step >= 2)
    def _():
        out_x[0] = near_x[0]
        out_y[0] = added(near_y[0], from_x[0])


def reduce_third_kernel(info, own, from_x, from_y, first, second, others):
    for m in range(4):
        at = info[2] ^ m
        value = added(own[at], from_x[at], from_y[at])
        if m == 0:
            first[...] = value
        elif m == 1:
            second[...] = value
        else:
            others[m - 2] = value


def final_kernel(first, second, third, fourth, out):
    out[...] = (first[...].astype(FLOAT) + second[...].astype(FLOAT)) + (
        third[...].astype(FLOAT) + fourth[...].astype(FLOAT)
    )


def reduce_fourth_kernel(first, second, come, first_out, second_out):
    first_out[...] = first[...].astype(FLOAT) + come[0].astype(FLOAT)
    second_out[...] = added(second[...], come[1])


def clip_swap(values, bits, count):
    return lax.ppermute(values, "clip", [(i, i ^ bits) for i in range(count)])


def core_swap(values):
    return lax.ppermute(values, "frame", [(0, 1), (1, 0)])


class Near:
    def __init__(self, clips, info):
        self.clips = clips
        self.info = info
        self.core = lax.axis_index("frame")

    def swap(self, values, bits):
        return clip_swap(values, bits, self.clips)

    def in_order(self, mine, far, axis):
        return jnp.where(
            self.core == 0, jnp.concatenate([mine, far], axis=axis), jnp.concatenate([far, mine], axis=axis)
        )

    def stack(self, pieces, deps):
        shape = (len(pieces),) + pieces[0].shape
        return call(
            stack_kernel, (1,), [(whole(v.shape), v) for v in pieces], [(whole(shape), sds(shape, BRAIN))],
            micros=3, deps=deps,
        )[0]

    def depth_direct(self, own, deps):
        return self.stack([own] + [self.swap(own, 4 * m) for m in (1, 2, 3)], deps)

    def depth_in_order(self, own, deps):
        pieces = [own] + [self.swap(own, 4 * m) for m in (1, 2, 3)]
        shape = (4,) + own.shape
        return call(
            stack_at_kernel, (1,), [(smem(), self.info)] + [(whole(v.shape), v) for v in pieces],
            [(whole(shape), sds(shape, BRAIN))], micros=3, deps=deps,
        )[0]

    def depth_near(self, own, deps):
        return self.stack([own, self.swap(own, 4)], deps)

    def depth_far(self, two, deps):
        come = self.swap(two, 8)
        return self.stack([two[0], two[1], come[0], come[1]], deps)

    def plane_step(self, o4, deps):
        rx = self.swap(o4, 1)
        ry = self.swap(o4, 2)
        half = (2,) + o4.shape[1:]
        first = pl.BlockSpec(half, lambda s: (0, 0, 0))
        second = pl.BlockSpec(half, lambda s: (1, 0, 0))
        sx, sy = call(
            halves_kernel, (1,), [(first, rx), (second, ry)], [(whole(half), sds(half, BRAIN))] * 2, deps=deps
        )
        return rx, ry, sx, sy

    def diagonal_step(self, o4, planes, deps):
        rx, ry, sx, sy = planes
        pieces = (o4, rx, ry, self.swap(sx, 2), self.swap(sy, 1))
        shape = (self.clips,) + o4.shape[1:]
        return call(
            assemble_kernel, (1,), [(smem(), self.info)] + [(whole(v.shape), v) for v in pieces],
            [(whole(shape), sds(shape, BRAIN))], micros=3, deps=deps,
        )[0]

    def reduce_first(self, mine, far, deps, micros=20):
        block = mine.shape[1:]
        four = (4, 4) + block
        view = pl.BlockSpec((1, 4) + block, lambda s: (s, 0, 0, 0))
        one = lambda pick: pl.BlockSpec((1,) + block, lambda s: (pick(s), 0, 0))
        each = (one(lambda s: s), sds((4,) + block, BRAIN))
        return call(
            reduce_first_kernel, (4,),
            [(smem(), self.info), (view, mine.reshape(four)), (view, far.reshape(four))],
            [
                (one(lambda s: jnp.minimum(s, 1)), sds((2,) + block, BRAIN)),
                (one(lambda s: jnp.maximum(s - 2, 0)), sds((2,) + block, BRAIN)),
                each, each, each,
            ],
            micros=micros, deps=deps,
        )

    def reduce_second(self, near_x, near_y, to_y, to_x, deps):
        from_y, from_x = self.swap(to_y, 2), self.swap(to_x, 1)
        block = near_x.shape[1:]
        one = lambda pick: pl.BlockSpec((1,) + block, lambda s: (pick(s), 0, 0))
        each = one(lambda s: s)
        return call(
            reduce_second_kernel, (4,),
            [
                (each, near_x), (each, near_y), (one(lambda s: jnp.minimum(s, 1)), from_y),
                (one(lambda s: jnp.maximum(s - 2, 0)), from_x),
            ],
            [(each, sds(near_x.shape, BRAIN))] * 2, micros=20, deps=deps,
        )

    def reduce_third(self, own, near_x, near_y, deps):
        from_x, from_y = self.swap(near_x, 1), self.swap(near_y, 2)
        block = own.shape[1:]
        return call(
            reduce_third_kernel, (1,),
            [(smem(), self.info)] + [(whole(v.shape), v) for v in (own, from_x, from_y)],
            [(whole(shape), sds(shape, BRAIN)) for shape in (block, block, (2,) + block)],
            micros=20, deps=deps,
        )

    def reduce_fourth(self, first, second, others, deps):
        come = self.swap(others, 8)
        inputs = [(whole(v.shape), v) for v in (first, second, come)]
        outs = [(whole(first.shape), sds(first.shape, kind)) for kind in (FLOAT, BRAIN)]
        return call(reduce_fourth_kernel, (1,), inputs, outs, micros=20, deps=deps)

    def reduce_end(self, first, second):
        return first + self.swap(second, 4).astype(FLOAT)

    def reduce_direct(self, first, second, others, deps=()):
        pieces = [first, self.swap(second, 4), self.swap(others[0], 8), self.swap(others[1], 12)]
        inputs = [(whole(v.shape), v) for v in pieces]
        return call(final_kernel, (1,), inputs, [(whole(first.shape), sds(first.shape, FLOAT))], deps=deps)[0]

    def owner_rows(self, value):
        rows = value.shape[0] // 2
        mine = lax.dynamic_slice_in_dim(value, self.core * rows, rows, 0)
        theirs = lax.dynamic_slice_in_dim(value, (1 - self.core) * rows, rows, 0)
        return self.in_order(mine, core_swap(theirs), 1)


AXES = ("clip", "frame")


def body(
    clips, cores, clip_tokens, clip_class, output_grad, class_grad, clip_count,
    time_qkv, time_proj, time_vec, space_qkv, space_proj, space_vec, mlp_up, mlp_down, mlp_vec, mlp_bias,
):
    _, own, places_here, width = clip_tokens.shape
    rows = -(-(places_here + 1) // 16) * 16
    frames = own * cores
    wide = mlp_up.shape[1]
    cut = width // BLOCKS
    core = lax.axis_index("frame")
    place = lax.axis_index("clip")
    shard = place * cores + core
    leader = (core == 0).astype(jnp.int32)
    alive = (jnp.arange(1, dtype=jnp.int32) < clip_count[0]).astype(FLOAT)
    is_near = clips == 16 and cores == 2
    slot = core if is_near else core * 0
    info = jnp.stack([slot, leader, place // 4, place % 4, shard]).astype(jnp.int32)
    near = Near(clips, info) if is_near else None
    my_slot = info[0:1]
    far_slot = 1 - my_slot

    class_block = jnp.broadcast_to(clip_class[0][None, None], (own, 1, width))
    blank = jnp.zeros((own, rows - places_here - 1, width), BRAIN)
    tokens = jnp.concatenate([clip_tokens[0], class_block, blank], axis=1)
    last = (jnp.arange(own) == own - 1)[:, None, None]
    class_rows = jnp.where(last, class_grad[0][None, None], jnp.zeros((), BRAIN))
    grads = jnp.concatenate([output_grad[0], class_rows, blank], axis=1)

    bias_rows = wide // width
    zeros = jnp.zeros((8, width), FLOAT)
    flat = lambda v: v.reshape((own * rows,) + v.shape[2:])

    if near is not None:
        packed = (
            time_qkv, space_qkv, space_proj, time_proj, mlp_up, time_vec, space_vec, mlp_vec,
            mlp_bias.reshape(-1, bias_rows).T,
        )
        line = sds((time_qkv.shape[0], 6 * width + LANES), BRAIN)
        send, keep = call(
            pack_kernel, (1,), [(smem(), info)] + [(whole(v.shape), v) for v in packed],
            [(whole(line.shape), line), (whole(line.shape), line)],
        )
        shapes = [(cut, 3 * width // 2 + LANES), (cut, 5 * width // 2), (4 * cut, width)]
        time_own, space_own, mlp_own = call(
            join_kernel, (1,),
            [(smem(), info)] + [(whole(v.shape), v) for v in (keep, core_swap(send), mlp_down)],
            [(whole(shape), sds(shape, BRAIN)) for shape in shapes],
        )
        join = lambda two: tuple(h.reshape(width, h.shape[-1]) for h in two)
        time_line = near.depth_direct(time_own, [])
        all_tokens = jnp.concatenate([tokens, core_swap(gate(tokens, [time_own]))], axis=0)
        space_own = gate(space_own, [time_line])
        space_line = near.depth_direct(space_own, [])
        time_mine = near.diagonal_step(time_line, near.plane_step(time_line, []), [grads, all_tokens, space_line])
        space_line = gate(space_line, [time_mine])
        time_far = core_swap(time_mine)
        time_w = join((time_mine, time_far))
        vec_block = pl.BlockSpec((width, LANES), lambda s: (0, time_w[0].shape[1] // LANES - 1))
        vectors = call(
            turn_kernel, (1,), [(vec_block, time_w[0])], [(whole((LANES, width)), sds((LANES, width), FLOAT))],
            deps=[space_line],
        )[0]
        n_vec = time_vec.shape[0] + space_vec.shape[0] + mlp_vec.shape[0]
        bias = vectors[n_vec : n_vec + bias_rows].T.reshape(bias_rows, width)
        mlp_own = gate(mlp_own, [time_mine])
        mix_deps = [space_line, mlp_own]
    else:
        everywhere = lax.all_gather(tokens, "frame", axis=0, tiled=True)
        all_tokens = jnp.roll(everywhere, -core * own, axis=0)
        vec_shard = jnp.concatenate([time_vec, space_vec, mlp_vec], axis=0)
        blank_rows = jnp.zeros((16 - vec_shard.shape[0], width), FLOAT)
        space_shard = jnp.concatenate([space_qkv, space_proj, time_proj], axis=1)
        vectors = lax.all_gather(vec_shard, AXES, axis=1, tiled=True).astype(FLOAT)
        bias = lax.all_gather(mlp_bias, AXES, axis=0, tiled=True).astype(FLOAT).reshape(bias_rows, width)
        vectors = jnp.concatenate([vectors, blank_rows], axis=0)

        def halves(value):
            full = lax.all_gather(value, AXES, axis=0, tiled=True)
            half = full.shape[1] // 2
            return full[:, :half], full[:, half:]

        time_w, space_w = halves(time_qkv), halves(space_shard)
        up = lax.all_gather(mlp_up, AXES, axis=0, tiled=True).reshape(BLOCKS, cut, 2, 2, width)
        up = jnp.transpose(up, (2, 0, 3, 1, 4)).reshape(2, BLOCKS, 2 * cut, width)
        down = lax.all_gather(mlp_down, AXES, axis=0, tiled=True).reshape(BLOCKS, 2, 2 * cut, width)
        mlp_w = tuple(
            (jnp.concatenate([up[n], down[:, n]], axis=1).reshape(4, BLOCKS // 4, 4 * cut, width),) for n in (0, 1)
        )
        mix_deps = []

    frame_shape = (own, rows, width)
    out_shape = (own, places_here, width)
    all_shape = (frames, rows, width)
    heads = width // HEAD_DIM
    prob_shape = (own, frames, rows, LANES)
    sprob_shape = (own, heads, rows, rows)
    mixed_shape = (own, rows, 3 * width)
    hidden_shape = (own, rows, wide)
    sum_out = (whole((8, width)), sds((8, width), FLOAT))
    row_bytes = own * rows * width
    square = 2 * own * rows * width * width
    group = 2 if own % 2 == 0 else 1
    frames_in = lambda array, first=0: (per_frame(array.shape, first, group), array)
    low_out = lambda shape, first=0: (per_frame(shape, first, group), sds(shape, BRAIN))
    wide_out = lambda shape, first=0: (per_frame(shape, first, group), sds(shape, FLOAT))
    vec_in = (whole(vectors.shape), vectors)
    pair = lambda two: [(hbm(), two[0]), (hbm(), two[1])]
    time_held = [pltpu.VMEM((width, 3 * width), BRAIN), pltpu.SemaphoreType.DMA((2,))]
    space_held = [pltpu.VMEM((width, 5 * width), BRAIN), pltpu.SemaphoreType.DMA((2,))]
    mlp_held = [
        pltpu.VMEM((wide // width, 4, BLOCKS // 4, cut, width), BRAIN),
        pltpu.VMEM((4, BLOCKS // 4, 2, 2 * cut, width), BRAIN),
        pltpu.SemaphoreType.DMA((2, 15)),
    ]

    own_map = pl.BlockSpec((group, rows, width), lambda s: (jnp.minimum(s, own // group - 1), 0, 0))
    queries, key_rows, value_rows, time_low = call(
        functools.partial(time_mix_kernel, own // group), (frames // group,),
        [(smem(), info), frames_in(all_tokens), vec_in] + pair(time_w),
        [(own_map, sds(frame_shape, BRAIN)), low_out(all_shape), low_out(all_shape), (own_map, sds(frame_shape, BRAIN))],
        time_held, micros=1, deps=mix_deps,
    )

    if near is not None:
        mlp_line = near.depth_in_order(mlp_own, [queries])
        space_mine = near.diagonal_step(space_line, near.plane_step(space_line, [queries]), [mlp_line])
        space_w = join((space_mine, core_swap(space_mine)))
        mlp_line = gate(mlp_line, [space_mine])

    parts = [(0, own)]
    deps = [] if near is None else [mlp_line]
    kept, class_own = (), zeros
    for first, count in parts:
        outs = call(
            functools.partial(attention_kernel, places_here), (count // group,),
            [
                (smem(), info), frames_in(tokens, first), vec_in, frames_in(queries, first),
                (whole(all_shape), key_rows), (whole(all_shape), value_rows), (whole((8, width)), class_own),
            ]
            + pair(space_w),
            [
                low_out(prob_shape, first), low_out(frame_shape, first), wide_out(frame_shape, first),
                low_out(frame_shape, first), low_out(mixed_shape, first), low_out(sprob_shape, first),
                low_out(frame_shape, first), wide_out(frame_shape, first), sum_out,
            ],
            space_held, micros=27 * count / own, deps=deps, previous=kept,
        )
        kept, class_own = tuple(outs[:-1]), outs[-1]
        if near is not None and first == 0:
            mlp_planes = near.plane_step(mlp_line, [class_own])
            deps = list(mlp_planes[2:])
    time_prob, time_att, after, space_low, space_mixed, space_prob, space_att, places = kept

    if near is not None:
        rx, ry, sx, sy = mlp_planes
        mlp_first = tuple(gate(v, [sx, sy]) for v in (mlp_line, rx, ry))
        mlp_last = (near.swap(sx, 2), near.swap(sy, 1))
        mlp_w = (mlp_first + mlp_last, tuple(core_swap(v) for v in mlp_first) + tuple(core_swap(v) for v in mlp_last))
        class_far = core_swap(class_own)
    else:
        class_far = lax.psum(class_own, "frame") - class_own
    class_row = jnp.broadcast_to(clip_class.astype(FLOAT), (8, width))
    small = whole((8, width))
    result, class_result, mlp_low, hidden, feed_grad, before_grad, rows_grad, mlp_sums = call(
        functools.partial(mlp_kernel, places_here, frames, len(mlp_w[0])), (own // group,),
        [
            (smem(), info), (smem(), alive), frames_in(places), frames_in(grads),
            (small, class_row), (small, class_own), (small, class_far), vec_in, (whole(bias.shape), bias),
        ]
        + [(hbm(), v) for v in mlp_w[0] + mlp_w[1]],
        [
            low_out(out_shape), sum_out, low_out(frame_shape), low_out(hidden_shape), low_out(frame_shape),
            low_out(hidden_shape), wide_out(frame_shape), sum_out,
        ],
        [pltpu.VMEM((wide // width, group * rows, width), FLOAT)] + mlp_held,
        micros=25,
    )

    mlp_mine, mlp_far = mlp_outer(my_slot, flat(mlp_low), flat(before_grad), flat(hidden), flat(feed_grad))
    class_block_at = places_here // 16
    class_spec = pl.BlockSpec((1, 16, width), lambda s: (own - 1, class_block_at, 0))

    def space_back(first, count, sums, deps, previous):
        return call(
            functools.partial(space_back_kernel, places_here, frames), (count // group,),
            [
                (smem(), info), frames_in(rows_grad, first), (class_spec, rows_grad), frames_in(after, first),
                frames_in(space_mixed, first), frames_in(space_prob, first), frames_in(space_att, first),
                vec_in, (small, sums),
            ]
            + pair(space_w),
            [
                low_out(frame_shape, first), low_out(mixed_shape, first), wide_out(frame_shape, first),
                low_out(frame_shape, first), low_out(frame_shape, first), sum_out,
            ],
            space_held, micros=30 * count / own, deps=deps, previous=previous,
        )

    half = own // 2
    if near is not None:
        outs = space_back(0, half, zeros, [mlp_far], ())
        mlp_a, mlp_b, mlp_x, mlp_y, mlp_own = near.reduce_first(mlp_mine, core_swap(mlp_far), [outs[0]])
        outs = space_back(half, own - half, outs[-1], [mlp_a, mlp_b], tuple(outs[:-1]))
        mlp_x, mlp_y = near.reduce_second(mlp_x, mlp_y, mlp_a, mlp_b, [outs[0]])
        time_deps = [mlp_x, mlp_y]
    else:
        outs = space_back(0, own, zeros, [], ())
        time_deps = []
    branch_grad, space_mixed_grad, after_grad, time_grad, time_att_grad, space_sums = outs

    space_mine, space_far = space_outer(
        my_slot, *[flat(v) for v in (space_low, space_mixed_grad, space_att, branch_grad, time_att, time_grad)],
        deps=time_deps,
    )
    time_deps = time_deps + [space_far]
    far_frames = frames - own
    lanes_of = lambda shape: pl.BlockSpec(shape[:-1] + (2 * LANES,), lambda s: (0,) * (len(shape) - 1) + (s,))
    lanes_in = lambda v: (lanes_of(v.shape), v)
    q_grad, own_grad, far_grad = call(
        time_back_kernel, (width // LANES // 2,),
        [
            lanes_in(queries), lanes_in(key_rows), lanes_in(value_rows), (whole(prob_shape), time_prob),
            lanes_in(time_att_grad),
        ],
        [
            (lanes_of(shape), sds(shape, BRAIN))
            for shape in (frame_shape, (2,) + frame_shape, (2, far_frames, rows, width))
        ],
        micros=19, deps=time_deps,
    )
    if near is not None:
        from_far = core_swap(far_grad)
        mlp_first, mlp_second, mlp_others = near.reduce_third(mlp_own, mlp_x, mlp_y, [q_grad])
        space_a, space_b, space_x, space_y, space_own = near.reduce_first(space_mine, core_swap(space_far), [mlp_second])
        mixed_deps = [space_own]
    else:
        mixed_deps = []
        padded = jnp.concatenate([jnp.zeros_like(own_grad), far_grad], axis=1)
        padded = jnp.roll(padded, core * own, axis=1)
        from_far = lax.psum_scatter(padded, "frame", scatter_dimension=1, tiled=True)
    pair_in = lambda v: (pl.BlockSpec((2, group, rows, width), lambda s: (0, s, 0, 0)), v)
    time_mixed_grad = call(
        mixed_grad_kernel, (own // group,), [frames_in(q_grad), pair_in(own_grad), pair_in(from_far)],
        [low_out(mixed_shape)], micros=3, deps=mixed_deps,
    )[0]
    outer = (flat(time_low), flat(time_mixed_grad))

    back_deps = [] if near is None else [mlp_second, space_a, space_b]
    token_grad, time_sums = call(
        time_mix_back_kernel, (own // group,),
        [(smem(), info), frames_in(tokens), vec_in, frames_in(time_mixed_grad), frames_in(after_grad)]
        + pair(time_w),
        [wide_out(out_shape), sum_out],
        time_held, micros=4, deps=back_deps,
    )
    bias_grad = mlp_sums[3 : 3 + bias_rows].reshape(width, bias_rows)
    n_sums = 13
    sums = call(
        sums_kernel, (1,), [(small, time_sums), (small, space_sums), (small, mlp_sums), (whole(bias_grad.shape), bias_grad)],
        [(whole((width, LANES)), sds((width, LANES), FLOAT))], [pltpu.VMEM((LANES, width), FLOAT)],
    )[0]

    if near is not None:
        space_x, space_y = near.reduce_second(space_x, space_y, space_a, space_b, [token_grad])
        mlp_grads = near.reduce_direct(mlp_first, mlp_second, mlp_others, [token_grad])
        time_mine, time_far = time_outer(my_slot, *outer, sums, deps=[space_x, space_y, mlp_grads])
        space_parts = near.reduce_third(space_own, space_x, space_y, [time_mine])
        time_a, time_b, time_x, time_y, time_own = near.reduce_first(
            time_mine, core_swap(time_far), [space_parts[1]]
        )
        time_x, time_y = near.reduce_second(time_x, time_y, time_a, time_b, [])
        time_parts = near.reduce_third(time_own, time_x, time_y, [])
        grad_space = near.reduce_direct(*space_parts)
        total = near.reduce_direct(*time_parts)
        grad_time, sums = total[:, : 3 * width], total[:, 3 * width :]
        grad_mlp_down = mlp_grads[2 * cut :]
        grad_mlp_up = near.owner_rows(jnp.concatenate([mlp_grads[:cut], mlp_grads[cut : 2 * cut]], axis=1))
        class_total = space_sums[6:7] + core_swap(space_sums)[6:7]
    else:
        send = lambda v: lax.psum_scatter(v, AXES, scatter_dimension=0, tiled=True).astype(FLOAT)
        spread = lambda mine, far: jnp.stack([mine, far], axis=1).reshape(width, mine.shape[2])
        time_mine, time_far = time_outer(my_slot, *outer, sums)
        up = jnp.stack([v[:, : 2 * cut].reshape(BLOCKS, 2, cut, width) for v in (mlp_mine, mlp_far)])
        grad_mlp_up = send(jnp.transpose(up, (1, 3, 0, 2, 4)).reshape(width, wide))
        grad_mlp_down = send(jnp.stack([v[:, 2 * cut :] for v in (mlp_mine, mlp_far)], axis=1).reshape(wide, width))
        grad_space = send(spread(space_mine, space_far))
        grad_time = send(spread(time_mine, time_far)[:, : 3 * width])
        class_total = lax.psum(space_sums[6:7], "frame")
        step = width // (clips * cores)
        sums = lax.dynamic_slice_in_dim(lax.psum(sums, AXES), shard * step, step, 0)
    class_in_grad = rows_grad[own - 1, places_here][None] + class_total
    lines = sums.T
    grad_time_vec, grad_space_vec, grad_mlp_vec = lines[:5], lines[5:10], lines[10:13]
    grad_mlp_bias = sums[:, n_sums : n_sums + bias_rows].reshape(-1)
    return (
        result[None],
        class_result[places_here % 8][None].astype(BRAIN),
        token_grad[None],
        class_in_grad,
        grad_time,
        grad_space[:, 4 * width :],
        grad_time_vec,
        grad_space[:, : 3 * width],
        grad_space[:, 3 * width : 4 * width],
        grad_space_vec,
        grad_mlp_up,
        grad_mlp_down,
        grad_mlp_vec,
        grad_mlp_bias,
    )


def solution(mesh):
    both = ("clip", "frame")
    rows = P(both, None)
    columns = P(None, both)
    weights = (rows, rows, columns, rows, rows, columns, rows, rows, columns, P(both))
    block = P("clip", "frame", None, None)
    classes = P("clip", None)
    return jax.shard_map(
        functools.partial(body, mesh.shape["clip"], mesh.shape["frame"]),
        mesh=mesh,
        in_specs=(block, classes, block, classes, P("clip")) + weights,
        out_specs=(block, classes, block, classes) + weights,
        check_vma=False,
    )
```

```python
import functools

import jax
import jax.numpy as jnp
from jax import lax
from jax.experimental import pallas as pl
from jax.experimental.pallas import tpu as pltpu
from jax.sharding import PartitionSpec as P

HEAD_DIM = 64
EPSILON = 1e-06
FLOAT = jnp.float32
BRAIN = jnp.bfloat16
LANES = 128
BLOCKS = 16
RATE = 1e9
VMEM_BYTES = 60 * 1024 * 1024


def nn(left, right):
    return lax.dot_general(left, right, (((1,), (0,)), ((), ())), preferred_element_type=FLOAT)


def nt(left, right):
    return lax.dot_general(left, right, (((1,), (1,)), ((), ())), preferred_element_type=FLOAT)


def tn(left, right):
    return lax.dot_general(left, right, (((0,), (0,)), ((), ())), preferred_element_type=FLOAT)


def unit_of(values):
    average = jnp.mean(values, axis=-1, keepdims=True)
    centred = values - average
    spread = jnp.mean(centred * centred, axis=-1, keepdims=True)
    inverse = lax.rsqrt(spread + EPSILON)
    return centred * inverse, inverse


def norm_back(unit, inverse, gain, upstream):
    scaled = upstream * gain
    inner = jnp.mean(scaled, axis=-1, keepdims=True)
    along = jnp.mean(scaled * unit, axis=-1, keepdims=True)
    return inverse * (scaled - inner - unit * along)


def column_sum(values):
    return jnp.sum(values, axis=0, keepdims=True)


def row_index(shape):
    return lax.broadcasted_iota(jnp.int32, shape, 0)


def head_map(width, first=0):
    lane = lax.broadcasted_iota(jnp.int32, (width, LANES), 0) // HEAD_DIM + first
    head = lax.broadcasted_iota(jnp.int32, (width, LANES), 1)
    return (lane == head).astype(FLOAT).astype(BRAIN)


def head_spread(width, first=0):
    head = lax.broadcasted_iota(jnp.int32, (LANES, width), 0)
    lane = lax.broadcasted_iota(jnp.int32, (LANES, width), 1) // HEAD_DIM + first
    return (lane == head).astype(FLOAT).astype(BRAIN)


def column_copies(core, mine, other, held, sems):
    half = held.shape[1] // 2
    copies = []
    for n, (source, slot) in enumerate(((mine, core), (other, 1 - core))):
        target = held.at[:, pl.ds(pl.multiple_of(slot * half, LANES), half)]
        copies.append(pltpu.make_async_copy(source.at[:, :half], target, sems.at[n]))
    return copies


def mlp_copies(core, plane, mine, other, up, down, sems):
    cut = up.shape[3]
    ups, downs = [], []
    for k, (sources, slot) in enumerate(((mine, core), (other, 1 - core))):
        for n, source in enumerate(sources):
            if len(sources) == 1:
                at, tail = (), (slice(None),)
            else:
                at, tail = ((slice(None), slice(0, 2), slice(2, 4))[max(n - 2, 0)], plane ^ min(n, 3)), ()
            rows = lambda low, high: source.at[(slice(None),) + tail + (slice(low, high),)]
            for t in (0, 1):
                part = up.at[(2 * slot + t,) + at]
                ups.append(pltpu.make_async_copy(rows(t * cut, (t + 1) * cut), part, sems.at[k, 3 * n + t]))
            part = down.at[at + (slot,)] if at else down.at[:, :, slot]
            downs.append(pltpu.make_async_copy(rows(2 * cut, 4 * cut), part, sems.at[k, 3 * n + 2]))
    return ups, downs


def start_first(copies):
    @pl.when(pl.program_id(0) == 0)
    def _():
        for copy in copies:
            copy.start()


def wait_first(copies):
    @pl.when(pl.program_id(0) == 0)
    def _():
        for copy in copies:
            copy.wait()


def merged(ref):
    return ref[...].reshape(ref.shape[0] * ref.shape[1], ref.shape[2])


def store(ref, value):
    ref[...] = value.astype(ref.dtype).reshape(ref.shape)


def marks(count, rows, low, high):
    index = row_index((count * rows, 1))
    found = (index >= low) & (index < high)
    for n in range(1, count):
        found = found | ((index >= n * rows + low) & (index < n * rows + high))
    return found


def time_mix_kernel(own_steps, info, tokens, vectors, w_mine, w_other, q_out, k_out, v_out, low_out, held, sems):
    step = pl.program_id(0)
    width = tokens.shape[-1]

    copies = column_copies(info[0], w_mine, w_other, held, sems)
    start_first(copies)
    unit, _ = unit_of(merged(tokens).astype(FLOAT))
    low = (unit * vectors[0:1] + vectors[1:2]).astype(BRAIN)
    wait_first(copies)
    store(k_out, nn(low, held[:, width : 2 * width]))
    store(v_out, nn(low, held[:, 2 * width :]) + vectors[3:4])

    @pl.when(step < own_steps)
    def _():
        queries = (nn(low, held[:, :width]) + vectors[2:3]).astype(BRAIN)
        store(q_out, queries * jnp.asarray(HEAD_DIM ** (-0.5), BRAIN))
        store(low_out, low)


def tree_sum(values):
    values = list(values)
    while len(values) > 1:
        values = [a + b for a, b in zip(values[::2], values[1::2])] + values[len(values) & ~1 :]
    return values[0]


def attention_kernel(
    places_here, info, tokens, vectors, q_in, k_in, v_in, begin, sw_mine, sw_other,
    prob_out, att_out, after_out, low_out, mixed_out, sprob_out, satt_out, places_out, class_out,
    held, sems,
):
    step = pl.program_id(0)
    frames = k_in.shape[0]
    count, rows, width = tokens.shape
    core = info[0]

    copies = column_copies(core, sw_mine, sw_other, held, sems)
    start_first(copies)
    mapping = head_map(width)
    spread = head_spread(width)
    for n in range(count):
        queries = q_in[n]
        scores = [nn(queries * k_in[g], mapping) for g in range(frames)]
        top = functools.reduce(jnp.maximum, scores)
        powers = [jnp.exp(s - top) for s in scores]
        scale = 1.0 / sum(powers)
        parts = []
        for g in range(frames):
            prob = (powers[g] * scale).astype(BRAIN)
            prob_out[n, g] = prob
            parts.append(nn(prob, spread).astype(BRAIN) * v_in[g])
        att_out[n] = tree_sum(parts)
    wait_first(copies)
    attended = merged(att_out)
    place = marks(count, rows, 0, places_here)
    base = merged(tokens).astype(FLOAT)
    after = jnp.where(place, base + (nn(attended, held[:, 4 * width :]) + vectors[4:5]), base)
    store(after_out, after)
    unit, _ = unit_of(after)
    low = (unit * vectors[5:6] + vectors[6:7]).astype(BRAIN)
    store(low_out, low)
    shape = (count, rows, width)
    queries = (nn(low, held[:, :width]) + vectors[7:8]).astype(BRAIN) * jnp.asarray(HEAD_DIM ** (-0.5), BRAIN)
    mixed_out[:, :, :width] = queries.reshape(shape)
    mixed_out[:, :, width : 2 * width] = nn(low, held[:, width : 2 * width]).astype(BRAIN).reshape(shape)
    mixed_out[:, :, 2 * width :] = (
        (nn(low, held[:, 2 * width : 3 * width]) + vectors[8:9]).astype(BRAIN).reshape(shape)
    )
    lane = lax.broadcasted_iota(jnp.int32, (1, LANES), 1)
    masks = [(lane // HEAD_DIM == e).astype(FLOAT).astype(BRAIN) for e in (0, 1)]
    key_ok = row_index((rows, 1)) <= places_here
    for n in range(count):
        for pair in range(width // LANES):
            at = pair * LANES
            q2 = mixed_out[n, :, at : at + LANES]
            k2 = mixed_out[n, :, width + at : width + at + LANES]
            v2 = mixed_out[n, :, 2 * width + at : 2 * width + at + LANES]
            result = []
            for e in (0, 1):
                logits = jnp.where(key_ok, nt(k2, q2 * masks[e]), -1e30)
                power = jnp.exp(logits - jnp.max(logits, axis=0, keepdims=True))
                prob = (power * (1.0 / jnp.sum(power, axis=0, keepdims=True))).astype(BRAIN)
                sprob_out[n, 2 * pair + e] = prob
                result.append(tn(prob, v2))
            satt_out[n, :, at : at + LANES] = jnp.where(lane < HEAD_DIM, result[0], result[1]).astype(BRAIN)
    spatial = nn(merged(satt_out), held[:, 3 * width : 4 * width]) + vectors[9:10]
    store(places_out, jnp.where(place, after, 0.0) + spatial)

    @pl.when(step == 0)
    def _():
        class_out[...] = begin[...]

    class_row = column_sum(jnp.where(marks(count, rows, places_here, places_here + 1), spatial, 0.0))
    class_out[0:1] = class_out[0:1] + class_row


def gelu_parts(values):
    half = 0.5 + 0.5 * lax.erf(values * (0.5 ** 0.5))
    density = jnp.exp(values * values * (-0.5)) * (0.5 / 3.141592653589793) ** 0.5
    return values * half, half + values * density


def mlp_kernel(
    places_here, all_frames, pieces, info, alive, places, grads, class_row, class_own, class_far, vectors, bias,
    *others,
):
    mine, other, others = others[:pieces], others[pieces : 2 * pieces], others[2 * pieces :]
    out, class_out, low_out, hidden_out, feed_out, before_out, rows_out, sums, slopes, up, down, sems = others
    step = pl.program_id(0)
    count, rows, width = places.shape
    core = info[0]

    ups, downs = mlp_copies(core, info[3], mine, other, up, down, sems)
    start_first(ups + downs)

    @pl.when(step == 0)
    def _():
        sums[...] = jnp.zeros_like(sums)

    class_mid = class_row[0:1] + (class_own[0:1] + class_far[0:1]) * all_frames ** (-0.5)
    last = (count - 1) * rows + places_here
    is_class = (row_index((count * rows, 1)) == last) & (step == pl.num_programs(0) - 1)
    kept = jnp.logical_not(marks(count, rows, places_here, places_here + 1) & (info[1] == 0))
    values = jnp.where(is_class, class_mid, merged(places))
    unit, inverse = unit_of(values)
    low = (unit * vectors[10:11] + vectors[11:12]).astype(BRAIN)
    store(low_out, low)
    feed = jnp.zeros((count * rows, width), FLOAT)
    chunks = hidden_out.shape[-1] // width
    wait_first(ups)
    for j in range(chunks):
        before = nn(low, up[j].reshape(width, width)) + bias[j : j + 1]
        hidden, slope = gelu_parts(before)
        hidden = hidden.astype(BRAIN)
        hidden_out[:, :, j * width : (j + 1) * width] = hidden.reshape(count, rows, width)
        slopes[j] = slope
        if j == 0:
            wait_first(downs)
        feed = feed + nn(hidden, down[j].reshape(width, width))
    result = ((values + (feed + vectors[12:13])) * alive[0]).reshape(count, rows, width)
    out[...] = result[:, :places_here].astype(BRAIN)
    class_out[...] = result[count - 1, places_here - places_here % 8 : places_here - places_here % 8 + 8]

    row_grad = merged(grads).astype(FLOAT) * alive[0]
    feed_grad = row_grad.astype(BRAIN)
    feed_kept = jnp.where(kept, row_grad, 0.0).astype(BRAIN)
    store(feed_out, feed_kept)
    sums[2:3] = sums[2:3] + column_sum(feed_kept.astype(FLOAT))
    upstream = jnp.zeros((count * rows, width), FLOAT)
    for j in range(chunks):
        hidden_grad = nt(feed_grad, down[j].reshape(width, width))
        before_grad = (hidden_grad * slopes[j]).astype(BRAIN)
        before_kept = jnp.where(kept, before_grad.astype(FLOAT), 0.0)
        before_out[:, :, j * width : (j + 1) * width] = before_kept.astype(BRAIN).reshape(count, rows, width)
        sums[3 + j : 4 + j] = sums[3 + j : 4 + j] + column_sum(before_kept)
        upstream = upstream + nt(before_grad, up[j].reshape(width, width))
    store(rows_out, row_grad + norm_back(unit, inverse, vectors[10:11], upstream))
    upstream = jnp.where(kept, upstream, 0.0)
    sums[0:1] = sums[0:1] + column_sum(upstream * unit)
    sums[1:2] = sums[1:2] + column_sum(upstream)


def space_back_kernel(
    places_here, all_frames, info, rows_grad, class_grad, after, mixed, sprob, satt, vectors, begin,
    sw_mine, sw_other,
    branch_out, mixed_out, after_out, time_out, att_out, sums, held, sems,
):
    step = pl.program_id(0)
    count, rows, width = after.shape
    core = info[0]

    copies = column_copies(core, sw_mine, sw_other, held, sems)
    start_first(copies)

    @pl.when(step == 0)
    def _():
        sums[...] = begin[...]

    place = marks(count, rows, 0, places_here)
    class_at = marks(count, rows, places_here, places_here + 1)
    offset = places_here % 16
    share = class_grad[0, offset : offset + 1] * all_frames ** (-0.5)
    direct = jnp.where(place, merged(rows_grad), 0.0)
    branch = jnp.where(class_at, share, direct).astype(BRAIN)
    store(branch_out, branch)
    sums[4:5] = sums[4:5] + column_sum(branch.astype(FLOAT))
    unit, inverse = unit_of(merged(after))
    wait_first(copies)
    att_grad = nt(branch, held[:, 3 * width : 4 * width]).astype(BRAIN)
    store(att_out, att_grad)
    spread = head_spread(width)
    lane = lax.broadcasted_iota(jnp.int32, (1, LANES), 1)
    masks = [(lane // HEAD_DIM == e).astype(FLOAT).astype(BRAIN) for e in (0, 1)]
    left = lane < HEAD_DIM
    for n in range(count):
        product = att_out[n].astype(FLOAT) * satt[n].astype(FLOAT)
        high = product.astype(BRAIN)
        rowdots = nt(spread, high) + nt(spread, (product - high.astype(FLOAT)).astype(BRAIN))
        for pair in range(width // LANES):
            at = pair * LANES
            a2 = att_out[n, :, at : at + LANES]
            q2 = mixed[n, :, at : at + LANES]
            k2 = mixed[n, :, width + at : width + at + LANES]
            v2 = mixed[n, :, 2 * width + at : 2 * width + at + LANES]
            queries, key_rows, value_rows = [], [], []
            for e in (0, 1):
                head = 2 * pair + e
                prob = sprob[n, head]
                prob_grad = nt(v2, a2 * masks[e])
                score = (prob.astype(FLOAT) * (prob_grad - rowdots[head : head + 1])).astype(BRAIN)
                queries.append(tn(score, k2))
                key_rows.append(nn(score, q2))
                value_rows.append(nn(prob, a2))
            q_grad = (jnp.where(left, queries[0], queries[1]) * HEAD_DIM ** (-0.5)).astype(BRAIN)
            k_grad = jnp.where(left, key_rows[0], key_rows[1]).astype(BRAIN)
            v_grad = jnp.where(left, value_rows[0], value_rows[1]).astype(BRAIN)
            mixed_out[n, :, at : at + LANES] = q_grad
            mixed_out[n, :, width + at : width + at + LANES] = k_grad
            mixed_out[n, :, 2 * width + at : 2 * width + at + LANES] = v_grad
    mixed_grad = merged(mixed_out)
    sums[2:3] = sums[2:3] + column_sum(mixed_grad[:, :width].astype(FLOAT))
    sums[3:4] = sums[3:4] + column_sum(mixed_grad[:, 2 * width :].astype(FLOAT))
    upstream = nt(mixed_grad, held[:, : 3 * width])
    inner = norm_back(unit, inverse, vectors[5:6], upstream)
    sums[0:1] = sums[0:1] + column_sum(upstream * unit)
    sums[1:2] = sums[1:2] + column_sum(upstream)
    sums[6:7] = sums[6:7] + column_sum(jnp.where(class_at, inner, 0.0))
    after_grad = jnp.where(place, direct + inner, 0.0)
    store(after_out, after_grad)
    low = after_grad.astype(BRAIN)
    store(time_out, low)
    sums[5:6] = sums[5:6] + column_sum(low.astype(FLOAT))
    store(att_out, nt(low, held[:, 4 * width :]))


def time_back_kernel(q_in, k_in, v_in, prob_in, att_in, q_out, own_out, far_out):
    own, rows, width = q_in.shape
    frames = k_in.shape[0]
    first = pl.program_id(0) * (width // HEAD_DIM)
    mapping = head_map(width, first)
    spread = head_spread(width, first)
    size = 16

    def chunk(index, carry):
        at = pl.ds(pl.multiple_of(index * size, size), size)
        values = [v_in[g, at] for g in range(frames)]
        att = [att_in[f, at] for f in range(own)]
        products = jnp.concatenate([att[f] * values[g] for f in range(own) for g in range(frames)], axis=0)
        prob_grad = nn(products, mapping)
        probs = [prob_in[f, g, at] for f in range(own) for g in range(frames)]
        scores = []
        for f in range(own):
            wide = [probs[f * frames + g].astype(FLOAT) for g in range(frames)]
            weighted = [
                wide[g] * prob_grad[(f * frames + g) * size : (f * frames + g + 1) * size] for g in range(frames)
            ]
            rowdot = sum(weighted)
            scores += [(weighted[g] - wide[g] * rowdot).astype(BRAIN) for g in range(frames)]
        score_wide = nn(jnp.concatenate(scores, axis=0), spread).astype(BRAIN)
        prob_wide = nn(jnp.concatenate(probs, axis=0), spread).astype(BRAIN)

        def part(array, f, g):
            return array[(f * frames + g) * size : (f * frames + g + 1) * size]

        keys = [k_in[g, at] for g in range(frames)]
        for f in range(own):
            total = tree_sum(part(score_wide, f, g) * keys[g] for g in range(frames))
            q_out[f, at] = total * jnp.asarray(HEAD_DIM ** (-0.5), BRAIN)
        queries = [q_in[f, at] for f in range(own)]
        for g in range(frames):
            key_grad = tree_sum(part(score_wide, f, g) * queries[f] for f in range(own))
            value_grad = tree_sum(part(prob_wide, f, g) * att[f] for f in range(own))
            if g < own:
                own_out[0, g, at] = key_grad
                own_out[1, g, at] = value_grad
            else:
                far_out[0, g - own, at] = key_grad
                far_out[1, g - own, at] = value_grad
        return carry

    lax.fori_loop(0, rows // size, chunk, 0, unroll=True)


def time_mix_back_kernel(info, tokens, vectors, mixed, after_grad, w_mine, w_other, token_out, sums, held, sems):
    step = pl.program_id(0)
    width = tokens.shape[-1]

    copies = column_copies(info[0], w_mine, w_other, held, sems)
    start_first(copies)

    @pl.when(step == 0)
    def _():
        sums[...] = jnp.zeros_like(sums)

    mixed_grad = merged(mixed)
    sums[2:3] = sums[2:3] + column_sum(mixed_grad[:, :width].astype(FLOAT))
    sums[3:4] = sums[3:4] + column_sum(mixed_grad[:, 2 * width :].astype(FLOAT))
    unit, inverse = unit_of(merged(tokens).astype(FLOAT))
    wait_first(copies)
    upstream = nt(mixed_grad, held[...])
    result = merged(after_grad) + norm_back(unit, inverse, vectors[0:1], upstream)
    token_out[...] = result.reshape(mixed.shape[:2] + (width,))[:, : token_out.shape[1]]
    sums[0:1] = sums[0:1] + column_sum(upstream * unit)
    sums[1:2] = sums[1:2] + column_sum(upstream)


def mixed_grad_kernel(queries, own, far, out):
    width = queries.shape[2]
    out[:, :, :width] = queries[...]
    out[:, :, width : 2 * width] = (own[0].astype(FLOAT) + far[0].astype(FLOAT)).astype(BRAIN)
    out[:, :, 2 * width :] = (own[1].astype(FLOAT) + far[1].astype(FLOAT)).astype(BRAIN)


def sums_kernel(time_sums, space_sums, mlp_sums, bias, out, lines):
    lines[...] = jnp.zeros_like(lines)
    lines[0:4] = time_sums[0:4]
    lines[4:5] = space_sums[5:6]
    lines[5:10] = space_sums[0:5]
    lines[10:13] = mlp_sums[0:3]
    count = bias.shape[1]
    place = lax.broadcasted_iota(jnp.int32, (count, LANES), 1) == row_index((count, LANES)) + 13
    spread = lax.dot_general(
        bias[...], place.astype(FLOAT), (((1,), (0,)), ((), ())), preferred_element_type=FLOAT,
        precision=lax.Precision.HIGHEST,
    )
    out[...] = lines[...].T + spread


def halves_kernel(left, right, left_out, right_out):
    left_out[...] = left[...]
    right_out[...] = right[...]


def share_rows(info, value, mine, other, at=slice(None)):
    value = value.reshape(mine.shape[0], 2, mine.shape[1], value.shape[-1])
    first = info[0] == 0
    mine[:, :, at] = jnp.where(first, value[:, 0], value[:, 1]).astype(BRAIN)
    other[:, :, at] = jnp.where(first, value[:, 1], value[:, 0]).astype(BRAIN)


def time_outer_kernel(info, left, right, sums, mine, other):
    step = pl.program_id(0)
    width = left.shape[1]

    for n in range(3):

        @pl.when(step == n)
        def _():
            share_rows(info, tn(left[...], right[...]), mine, other, slice(n * width, (n + 1) * width))

    @pl.when(step == 0)
    def _():
        share_rows(info, sums[...], mine, other, slice(3 * width, 3 * width + sums.shape[1]))


def space_outer_kernel(info, low, mixed, att, branch, time_att, time_grad, mine, other):
    step = pl.program_id(0)

    @pl.when(step < 3)
    def _():
        share_rows(info, tn(low[...], mixed[...]), mine, other)

    @pl.when(step == 3)
    def _():
        share_rows(info, tn(att[...], branch[...]), mine, other)

    @pl.when(step == 4)
    def _():
        share_rows(info, tn(time_att[...], time_grad[...]), mine, other)


def mlp_outer_kernel(info, low, before, hidden, feed, mine, other, turned, ups, downs, sems):
    step = pl.program_id(0)
    steps = ups.shape[0]
    blocks, cut, width = ups.shape[1:]
    per = downs.shape[2]

    @pl.when(step == 0)
    def _():
        turned[...] = low[...].T

    ups[step] = nn(turned[...], before[...]).astype(BRAIN).reshape(blocks, cut, width)
    value = tn(hidden[...], feed[...]).astype(BRAIN).reshape(per, 2, 2 * cut, width)
    downs[step, 0] = value[:, 0]
    downs[step, 1] = value[:, 1]

    for n in range(steps):
        targets = (mine, other)
        for k, slot in ((0, info[0]), (1, 1 - info[0])):
            up_copy = pltpu.make_async_copy(
                ups.at[n], targets[k].at[:, (n % 2) * cut : (n % 2 + 1) * cut], sems.at[0, n]
            )
            down_copy = pltpu.make_async_copy(
                downs.at[n, slot], targets[k].at[n * per : (n + 1) * per, 2 * cut :], sems.at[1 + k, n]
            )

            @pl.when((step == n) & (slot == n // 2))
            def _():
                up_copy.start()

            @pl.when(step == n)
            def _():
                down_copy.start()

            @pl.when((step == steps - 1) & (slot == n // 2))
            def _():
                up_copy.wait()

            @pl.when(step == steps - 1)
            def _():
                down_copy.wait()


def smem():
    return pl.BlockSpec(memory_space=pltpu.SMEM)


def hbm():
    return pl.BlockSpec(memory_space=pl.ANY)


def whole(shape):
    return pl.BlockSpec(shape, lambda *_: (0,) * len(shape))


def per_frame(shape, first=0, count=1):
    return pl.BlockSpec((count,) + shape[1:], lambda s: (s + first // count,) + (0,) * (len(shape) - 1))


def sds(shape, kind):
    return jax.ShapeDtypeStruct(shape, kind)


def call(kernel, grid, inputs, outputs, scratch=(), micros=2, deps=(), previous=(), prefetch=0):
    count = len(inputs)
    skip = len(previous) + len(deps)

    def inner(*refs):
        kernel(*refs[:count], *refs[count + skip :])

    specs = [spec for spec, _ in inputs[prefetch:]] + [hbm()] * skip
    common = dict(
        name=getattr(kernel, "func", kernel).__name__,
        out_shape=[shape for _, shape in outputs],
        compiler_params=pltpu.CompilerParams(vmem_limit_bytes=VMEM_BYTES),
        input_output_aliases={count + n: n for n in range(len(previous))},
        cost_estimate=pl.CostEstimate(flops=int(micros * RATE), bytes_accessed=1, transcendentals=0),
    )
    places = dict(grid=grid, in_specs=specs, out_specs=[spec for spec, _ in outputs], scratch_shapes=list(scratch))
    if prefetch:
        common["grid_spec"] = pltpu.PrefetchScalarGridSpec(num_scalar_prefetch=prefetch, **places)
    else:
        common.update(places)
    return pl.pallas_call(inner, **common)(*[array for _, array in inputs], *previous, *deps)


def time_outer(slot, left, right, sums, deps=()):
    rows, width = left.shape
    wide = right.shape[1]
    shape = (BLOCKS, width // (2 * BLOCKS), wide + sums.shape[1])
    return call(
        time_outer_kernel, (3,),
        [
            (smem(), slot), (whole(left.shape), left), (pl.BlockSpec((rows, width), lambda s: (0, s)), right),
            (whole(sums.shape), sums),
        ],
        [(whole(shape), sds(shape, BRAIN))] * 2, micros=8, deps=deps,
    )


def space_outer(slot, low, mixed, *others, deps=()):
    rows, width = low.shape
    shape = (BLOCKS, width // (2 * BLOCKS), width)
    moving = pl.BlockSpec((rows, width), lambda s: (0, jnp.minimum(s, 2)))
    return call(
        space_outer_kernel, (5,),
        [(smem(), slot), (whole(low.shape), low), (moving, mixed)] + [(whole(v.shape), v) for v in others],
        [(pl.BlockSpec(shape, lambda s: (0, 0, s)), sds(shape[:2] + (5 * width,), BRAIN))] * 2, micros=12, deps=deps,
    )


def mlp_outer(slot, low, before, hidden, feed, deps=()):
    rows, width = low.shape
    wide = hidden.shape[1]
    cut = width // BLOCKS
    shape = (BLOCKS, 4 * cut, width)
    fixed = pl.BlockSpec((rows, width), lambda s, info: (0, 0))
    moving = pl.BlockSpec((rows, width), lambda s, info: (0, s))
    return call(
        mlp_outer_kernel, (wide // width,),
        [(None, slot), (fixed, low), (moving, before), (moving, hidden), (fixed, feed)],
        [(hbm(), sds(shape, BRAIN))] * 2,
        [
            pltpu.VMEM((width, rows), BRAIN),
            pltpu.VMEM((wide // width, BLOCKS, cut, width), BRAIN),
            pltpu.VMEM((wide // width, 2, BLOCKS * width // wide, 2 * cut, width), BRAIN),
            pltpu.SemaphoreType.DMA((3, wide // width)),
        ],
        micros=21, deps=deps, prefetch=1,
    )


def gate(value, deps):
    return pl.pallas_call(
        lambda source, *refs: None,
        in_specs=[hbm()] * (1 + len(deps)),
        out_specs=hbm(),
        out_shape=sds(value.shape, value.dtype),
        input_output_aliases={0: 0},
    )(value, *deps)


def stack_at_kernel(info, *refs):
    for n, ref in enumerate(refs[:-1]):
        refs[-1][info[2] ^ n] = ref[...]


def stack_kernel(*refs):
    for n, ref in enumerate(refs[:-1]):
        refs[-1][n] = ref[...]


def add_kernel(left, right, out):
    out[...] = left[...] + right[...]


def add_after(left, right, deps):
    inputs = [(whole(left.shape), left), (whole(right.shape), right)]
    return call(add_kernel, (1,), inputs, [(whole(left.shape), sds(left.shape, left.dtype))], deps=deps)[0]


def assemble_kernel(info, o4, rx, ry, ra, rb, out):
    depth = info[2]
    plane = info[3]
    for m in range(4):
        for n in range(4):
            if n < 3:
                value = (o4, rx, ry)[n][m]
            else:
                value = ra[m] if m < 2 else rb[m - 2]
            out[(depth ^ m) * 4 + (plane ^ n)] = value


def pack_kernel(info, time_qkv, space_qkv, space_proj, time_proj, up, time_vec, space_vec, mlp_vec, bias, send, keep):
    width = time_proj.shape[1]
    half = width // 2
    pieces = [time_qkv[:, n * half : (n + 1) * half] for n in range(6)]
    pieces += [space_qkv[:, n * half : (n + 1) * half] for n in range(6)]
    pieces += [space_proj[:, :half], space_proj[:, half:], time_proj[:, :half], time_proj[:, half:]]
    pieces += [up[:, n * half : (n + 1) * half] for n in range(8)]
    first = info[0] == 0
    at = 0
    for begin, count in ((0, 3), (6, 5), (16, 4)):
        for n in range(count):
            low, high = pieces[begin + n], pieces[begin + count + n]
            keep[:, at : at + half] = jnp.where(first, low, high)
            send[:, at : at + half] = jnp.where(first, high, low)
            at += half
    line = 0
    total = jnp.zeros((keep.shape[0], LANES), FLOAT)
    for source in (time_vec, space_vec, mlp_vec, bias):
        count = source.shape[0]
        lane = lax.broadcasted_iota(jnp.int32, (count, LANES), 1)
        chosen = (lane == row_index((count, LANES)) + line).astype(FLOAT)
        total = total + lax.dot_general(
            source[...].astype(FLOAT), chosen, (((0,), (0,)), ((), ())), preferred_element_type=FLOAT
        )
        line += count
    keep[:, at:] = total.astype(BRAIN)
    send[:, at:] = total.astype(BRAIN)


def turn_kernel(source, out):
    out[...] = source[...].astype(FLOAT).T


def join_kernel(info, keep, come, down, time_out, space_out, mlp_out):
    first = info[0] == 0
    width = down.shape[1]
    mine, far = keep[...].astype(FLOAT), come[...].astype(FLOAT)
    both = jnp.concatenate([jnp.where(first, mine, far), jnp.where(first, far, mine)], axis=0).astype(BRAIN)
    cut = both.shape[0]
    end = time_out.shape[1] - LANES
    time_out[:, :end] = both[:, :end]
    time_out[:, end:] = both[:, both.shape[1] - LANES :]
    space_out[...] = both[:, end : end + space_out.shape[1]]
    at = end + space_out.shape[1]
    mlp_out[:cut] = both[:, at : at + width]
    mlp_out[cut : 2 * cut] = both[:, at + width : at + 2 * width]
    mlp_out[2 * cut :] = down[...]


def added(*values):
    return sum(v.astype(FLOAT) for v in values).astype(BRAIN)


def reduce_first_kernel(info, mine, far, to_y, to_x, near_x, near_y, own):
    step = pl.program_id(0)
    plane = info[3]
    own[0] = added(mine[0, plane], far[0, plane])
    near_x[0] = added(mine[0, plane ^ 1], far[0, plane ^ 1])
    near_y[0] = added(mine[0, plane ^ 2], far[0, plane ^ 2])
    diagonal = added(mine[0, plane ^ 3], far[0, plane ^ 3])

    @pl.when(step < 2)
    def _():
        to_y[0] = diagonal

    @pl.when(step >= 2)
    def _():
        to_x[0] = diagonal


def reduce_second_kernel(near_x, near_y, from_y, from_x, out_x, out_y):
    step = pl.program_id(0)

    @pl.when(step < 2)
    def _():
        out_x[0] = added(near_x[0], from_y[0])
        out_y[0] = near_y[0]

    @pl.when(step >= 2)
    def _():
        out_x[0] = near_x[0]
        out_y[0] = added(near_y[0], from_x[0])


def reduce_third_kernel(info, own, from_x, from_y, first, second, others):
    for m in range(4):
        at = info[2] ^ m
        value = added(own[at], from_x[at], from_y[at])
        if m == 0:
            first[...] = value
        elif m == 1:
            second[...] = value
        else:
            others[m - 2] = value


def final_kernel(first, second, third, fourth, *outs):
    at = 0
    for out in outs:
        part = slice(at, at + out.shape[1])
        out[...] = (first[:, part].astype(FLOAT) + second[:, part].astype(FLOAT)) + (
            third[:, part].astype(FLOAT) + fourth[:, part].astype(FLOAT)
        )
        at += out.shape[1]


def reduce_fourth_kernel(first, second, come, first_out, second_out):
    first_out[...] = first[...].astype(FLOAT) + come[0].astype(FLOAT)
    second_out[...] = added(second[...], come[1])


def clip_swap(values, bits, count):
    return lax.ppermute(values, "clip", [(i, i ^ bits) for i in range(count)])


def core_swap(values):
    return lax.ppermute(values, "frame", [(0, 1), (1, 0)])


class Near:
    def __init__(self, clips, info):
        self.clips = clips
        self.info = info
        self.core = lax.axis_index("frame")

    def swap(self, values, bits):
        return clip_swap(values, bits, self.clips)

    def in_order(self, mine, far, axis):
        return jnp.where(
            self.core == 0, jnp.concatenate([mine, far], axis=axis), jnp.concatenate([far, mine], axis=axis)
        )

    def stack(self, pieces, deps):
        shape = (len(pieces),) + pieces[0].shape
        return call(
            stack_kernel, (1,), [(whole(v.shape), v) for v in pieces], [(whole(shape), sds(shape, BRAIN))],
            micros=3, deps=deps,
        )[0]

    def depth_direct(self, own, deps):
        return self.stack([own] + [self.swap(own, 4 * m) for m in (1, 2, 3)], deps)

    def depth_in_order(self, own, deps):
        pieces = [own] + [self.swap(own, 4 * m) for m in (1, 2, 3)]
        shape = (4,) + own.shape
        return call(
            stack_at_kernel, (1,), [(smem(), self.info)] + [(whole(v.shape), v) for v in pieces],
            [(whole(shape), sds(shape, BRAIN))], micros=3, deps=deps,
        )[0]

    def depth_near(self, own, deps):
        return self.stack([own, self.swap(own, 4)], deps)

    def depth_far(self, two, deps):
        come = self.swap(two, 8)
        return self.stack([two[0], two[1], come[0], come[1]], deps)

    def plane_step(self, o4, deps):
        rx = self.swap(o4, 1)
        ry = self.swap(o4, 2)
        half = (2,) + o4.shape[1:]
        first = pl.BlockSpec(half, lambda s: (0, 0, 0))
        second = pl.BlockSpec(half, lambda s: (1, 0, 0))
        sx, sy = call(
            halves_kernel, (1,), [(first, rx), (second, ry)], [(whole(half), sds(half, BRAIN))] * 2, deps=deps
        )
        return rx, ry, sx, sy

    def diagonal_step(self, o4, planes, deps):
        rx, ry, sx, sy = planes
        pieces = (o4, rx, ry, self.swap(sx, 2), self.swap(sy, 1))
        shape = (self.clips,) + o4.shape[1:]
        return call(
            assemble_kernel, (1,), [(smem(), self.info)] + [(whole(v.shape), v) for v in pieces],
            [(whole(shape), sds(shape, BRAIN))], micros=3, deps=deps,
        )[0]

    def reduce_first(self, mine, far, deps, micros=20):
        block = mine.shape[1:]
        four = (4, 4) + block
        view = pl.BlockSpec((1, 4) + block, lambda s: (s, 0, 0, 0))
        one = lambda pick: pl.BlockSpec((1,) + block, lambda s: (pick(s), 0, 0))
        each = (one(lambda s: s), sds((4,) + block, BRAIN))
        return call(
            reduce_first_kernel, (4,),
            [(smem(), self.info), (view, mine.reshape(four)), (view, far.reshape(four))],
            [
                (one(lambda s: jnp.minimum(s, 1)), sds((2,) + block, BRAIN)),
                (one(lambda s: jnp.maximum(s - 2, 0)), sds((2,) + block, BRAIN)),
                each, each, each,
            ],
            micros=micros, deps=deps,
        )

    def reduce_second(self, near_x, near_y, to_y, to_x, deps):
        from_y, from_x = self.swap(to_y, 2), self.swap(to_x, 1)
        block = near_x.shape[1:]
        one = lambda pick: pl.BlockSpec((1,) + block, lambda s: (pick(s), 0, 0))
        each = one(lambda s: s)
        return call(
            reduce_second_kernel, (4,),
            [
                (each, near_x), (each, near_y), (one(lambda s: jnp.minimum(s, 1)), from_y),
                (one(lambda s: jnp.maximum(s - 2, 0)), from_x),
            ],
            [(each, sds(near_x.shape, BRAIN))] * 2, micros=20, deps=deps,
        )

    def reduce_third(self, own, near_x, near_y, deps):
        from_x, from_y = self.swap(near_x, 1), self.swap(near_y, 2)
        block = own.shape[1:]
        return call(
            reduce_third_kernel, (1,),
            [(smem(), self.info)] + [(whole(v.shape), v) for v in (own, from_x, from_y)],
            [(whole(shape), sds(shape, BRAIN)) for shape in (block, block, (2,) + block)],
            micros=20, deps=deps,
        )

    def reduce_fourth(self, first, second, others, deps):
        come = self.swap(others, 8)
        inputs = [(whole(v.shape), v) for v in (first, second, come)]
        outs = [(whole(first.shape), sds(first.shape, kind)) for kind in (FLOAT, BRAIN)]
        return call(reduce_fourth_kernel, (1,), inputs, outs, micros=20, deps=deps)

    def reduce_end(self, first, second):
        return first + self.swap(second, 4).astype(FLOAT)

    def reduce_direct(self, first, second, others, deps=(), widths=None):
        pieces = [first, self.swap(second, 4), self.swap(others[0], 8), self.swap(others[1], 12)]
        inputs = [(whole(v.shape), v) for v in pieces]
        shapes = [(first.shape[0], n) for n in (widths or first.shape[1:])]
        return call(final_kernel, (1,), inputs, [(whole(n), sds(n, FLOAT)) for n in shapes], deps=deps)

    def owner_rows(self, value):
        rows = value.shape[0] // 2
        mine = lax.dynamic_slice_in_dim(value, self.core * rows, rows, 0)
        theirs = lax.dynamic_slice_in_dim(value, (1 - self.core) * rows, rows, 0)
        return self.in_order(mine, core_swap(theirs), 1)


AXES = ("clip", "frame")


def body(
    clips, cores, clip_tokens, clip_class, output_grad, class_grad, clip_count,
    time_qkv, time_proj, time_vec, space_qkv, space_proj, space_vec, mlp_up, mlp_down, mlp_vec, mlp_bias,
):
    _, own, places_here, width = clip_tokens.shape
    rows = -(-(places_here + 1) // 16) * 16
    frames = own * cores
    wide = mlp_up.shape[1]
    cut = width // BLOCKS
    core = lax.axis_index("frame")
    place = lax.axis_index("clip")
    shard = place * cores + core
    leader = (core == 0).astype(jnp.int32)
    alive = (jnp.arange(1, dtype=jnp.int32) < clip_count[0]).astype(FLOAT)
    is_near = clips == 16 and cores == 2
    slot = core if is_near else core * 0
    info = jnp.stack([slot, leader, place // 4, place % 4, shard]).astype(jnp.int32)
    near = Near(clips, info) if is_near else None
    my_slot = info[0:1]
    far_slot = 1 - my_slot

    class_block = jnp.broadcast_to(clip_class[0][None, None], (own, 1, width))
    blank = jnp.zeros((own, rows - places_here - 1, width), BRAIN)
    tokens = jnp.concatenate([clip_tokens[0], class_block, blank], axis=1)
    last = (jnp.arange(own) == own - 1)[:, None, None]
    class_rows = jnp.where(last, class_grad[0][None, None], jnp.zeros((), BRAIN))
    grads = jnp.concatenate([output_grad[0], class_rows, blank], axis=1)

    bias_rows = wide // width
    zeros = jnp.zeros((8, width), FLOAT)
    flat = lambda v: v.reshape((own * rows,) + v.shape[2:])

    if near is not None:
        packed = (
            time_qkv, space_qkv, space_proj, time_proj, mlp_up, time_vec, space_vec, mlp_vec,
            mlp_bias.reshape(-1, bias_rows).T,
        )
        line = sds((time_qkv.shape[0], 6 * width + LANES), BRAIN)
        send, keep = call(
            pack_kernel, (1,), [(smem(), info)] + [(whole(v.shape), v) for v in packed],
            [(whole(line.shape), line), (whole(line.shape), line)],
        )
        shapes = [(cut, 3 * width // 2 + LANES), (cut, 5 * width // 2), (4 * cut, width)]
        time_own, space_own, mlp_own = call(
            join_kernel, (1,),
            [(smem(), info)] + [(whole(v.shape), v) for v in (keep, core_swap(send), mlp_down)],
            [(whole(shape), sds(shape, BRAIN)) for shape in shapes],
        )
        join = lambda two: tuple(h.reshape(width, h.shape[-1]) for h in two)
        time_line = near.depth_direct(time_own, [])
        all_tokens = jnp.concatenate([tokens, core_swap(gate(tokens, [time_own]))], axis=0)
        space_own = gate(space_own, [time_line])
        space_line = near.depth_direct(space_own, [])
        time_mine = near.diagonal_step(time_line, near.plane_step(time_line, []), [grads, all_tokens, space_line])
        space_line = gate(space_line, [time_mine])
        time_far = core_swap(time_mine)
        time_w = join((time_mine, time_far))
        vec_block = pl.BlockSpec((width, LANES), lambda s: (0, time_w[0].shape[1] // LANES - 1))
        vectors = call(
            turn_kernel, (1,), [(vec_block, time_w[0])], [(whole((LANES, width)), sds((LANES, width), FLOAT))],
            deps=[space_line],
        )[0]
        n_vec = time_vec.shape[0] + space_vec.shape[0] + mlp_vec.shape[0]
        bias = vectors[n_vec : n_vec + bias_rows].T.reshape(bias_rows, width)
        mlp_own = gate(mlp_own, [time_mine])
        mix_deps = [space_line, mlp_own]
    else:
        everywhere = lax.all_gather(tokens, "frame", axis=0, tiled=True)
        all_tokens = jnp.roll(everywhere, -core * own, axis=0)
        vec_shard = jnp.concatenate([time_vec, space_vec, mlp_vec], axis=0)
        blank_rows = jnp.zeros((16 - vec_shard.shape[0], width), FLOAT)
        space_shard = jnp.concatenate([space_qkv, space_proj, time_proj], axis=1)
        vectors = lax.all_gather(vec_shard, AXES, axis=1, tiled=True).astype(FLOAT)
        bias = lax.all_gather(mlp_bias, AXES, axis=0, tiled=True).astype(FLOAT).reshape(bias_rows, width)
        vectors = jnp.concatenate([vectors, blank_rows], axis=0)

        def halves(value):
            full = lax.all_gather(value, AXES, axis=0, tiled=True)
            half = full.shape[1] // 2
            return full[:, :half], full[:, half:]

        time_w, space_w = halves(time_qkv), halves(space_shard)
        up = lax.all_gather(mlp_up, AXES, axis=0, tiled=True).reshape(BLOCKS, cut, 2, 2, width)
        up = jnp.transpose(up, (2, 0, 3, 1, 4)).reshape(2, BLOCKS, 2 * cut, width)
        down = lax.all_gather(mlp_down, AXES, axis=0, tiled=True).reshape(BLOCKS, 2, 2 * cut, width)
        mlp_w = tuple(
            (jnp.concatenate([up[n], down[:, n]], axis=1).reshape(4, BLOCKS // 4, 4 * cut, width),) for n in (0, 1)
        )
        mix_deps = []

    frame_shape = (own, rows, width)
    out_shape = (own, places_here, width)
    all_shape = (frames, rows, width)
    heads = width // HEAD_DIM
    prob_shape = (own, frames, rows, LANES)
    sprob_shape = (own, heads, rows, rows)
    mixed_shape = (own, rows, 3 * width)
    hidden_shape = (own, rows, wide)
    sum_out = (whole((8, width)), sds((8, width), FLOAT))
    row_bytes = own * rows * width
    square = 2 * own * rows * width * width
    group = 2 if own % 2 == 0 else 1
    frames_in = lambda array, first=0: (per_frame(array.shape, first, group), array)
    low_out = lambda shape, first=0: (per_frame(shape, first, group), sds(shape, BRAIN))
    wide_out = lambda shape, first=0: (per_frame(shape, first, group), sds(shape, FLOAT))
    vec_in = (whole(vectors.shape), vectors)
    pair = lambda two: [(hbm(), two[0]), (hbm(), two[1])]
    time_held = [pltpu.VMEM((width, 3 * width), BRAIN), pltpu.SemaphoreType.DMA((2,))]
    space_held = [pltpu.VMEM((width, 5 * width), BRAIN), pltpu.SemaphoreType.DMA((2,))]
    mlp_held = [
        pltpu.VMEM((wide // width, 4, BLOCKS // 4, cut, width), BRAIN),
        pltpu.VMEM((4, BLOCKS // 4, 2, 2 * cut, width), BRAIN),
        pltpu.SemaphoreType.DMA((2, 15)),
    ]

    own_map = pl.BlockSpec((group, rows, width), lambda s: (jnp.minimum(s, own // group - 1), 0, 0))
    queries, key_rows, value_rows, time_low = call(
        functools.partial(time_mix_kernel, own // group), (frames // group,),
        [(smem(), info), frames_in(all_tokens), vec_in] + pair(time_w),
        [(own_map, sds(frame_shape, BRAIN)), low_out(all_shape), low_out(all_shape), (own_map, sds(frame_shape, BRAIN))],
        time_held, micros=1, deps=mix_deps,
    )

    if near is not None:
        mlp_line = near.depth_in_order(mlp_own, [queries])
        space_mine = near.diagonal_step(space_line, near.plane_step(space_line, [queries]), [mlp_line])
        space_w = join((space_mine, core_swap(space_mine)))
        mlp_line = gate(mlp_line, [space_mine])

    parts = [(0, own)]
    deps = [] if near is None else [mlp_line]
    kept, class_own = (), zeros
    for first, count in parts:
        outs = call(
            functools.partial(attention_kernel, places_here), (count // group,),
            [
                (smem(), info), frames_in(tokens, first), vec_in, frames_in(queries, first),
                (whole(all_shape), key_rows), (whole(all_shape), value_rows), (whole((8, width)), class_own),
            ]
            + pair(space_w),
            [
                low_out(prob_shape, first), low_out(frame_shape, first), wide_out(frame_shape, first),
                low_out(frame_shape, first), low_out(mixed_shape, first), low_out(sprob_shape, first),
                low_out(frame_shape, first), wide_out(frame_shape, first), sum_out,
            ],
            space_held, micros=27 * count / own, deps=deps, previous=kept,
        )
        kept, class_own = tuple(outs[:-1]), outs[-1]
        if near is not None and first == 0:
            mlp_planes = near.plane_step(mlp_line, [class_own])
            deps = list(mlp_planes[2:])
    time_prob, time_att, after, space_low, space_mixed, space_prob, space_att, places = kept

    if near is not None:
        rx, ry, sx, sy = mlp_planes
        mlp_first = tuple(gate(v, [sx, sy]) for v in (mlp_line, rx, ry))
        mlp_last = (near.swap(sx, 2), near.swap(sy, 1))
        mlp_w = (mlp_first + mlp_last, tuple(core_swap(v) for v in mlp_first) + tuple(core_swap(v) for v in mlp_last))
        class_far = core_swap(class_own)
    else:
        class_far = lax.psum(class_own, "frame") - class_own
    class_row = jnp.broadcast_to(clip_class.astype(FLOAT), (8, width))
    small = whole((8, width))
    result, class_result, mlp_low, hidden, feed_grad, before_grad, rows_grad, mlp_sums = call(
        functools.partial(mlp_kernel, places_here, frames, len(mlp_w[0])), (own // group,),
        [
            (smem(), info), (smem(), alive), frames_in(places), frames_in(grads),
            (small, class_row), (small, class_own), (small, class_far), vec_in, (whole(bias.shape), bias),
        ]
        + [(hbm(), v) for v in mlp_w[0] + mlp_w[1]],
        [
            low_out(out_shape), sum_out, low_out(frame_shape), low_out(hidden_shape), low_out(frame_shape),
            low_out(hidden_shape), wide_out(frame_shape), sum_out,
        ],
        [pltpu.VMEM((wide // width, group * rows, width), FLOAT)] + mlp_held,
        micros=25,
    )

    mlp_mine, mlp_far = mlp_outer(my_slot, flat(mlp_low), flat(before_grad), flat(hidden), flat(feed_grad))
    class_block_at = places_here // 16
    class_spec = pl.BlockSpec((1, 16, width), lambda s: (own - 1, class_block_at, 0))

    def space_back(first, count, sums, deps, previous):
        return call(
            functools.partial(space_back_kernel, places_here, frames), (count // group,),
            [
                (smem(), info), frames_in(rows_grad, first), (class_spec, rows_grad), frames_in(after, first),
                frames_in(space_mixed, first), frames_in(space_prob, first), frames_in(space_att, first),
                vec_in, (small, sums),
            ]
            + pair(space_w),
            [
                low_out(frame_shape, first), low_out(mixed_shape, first), wide_out(frame_shape, first),
                low_out(frame_shape, first), low_out(frame_shape, first), sum_out,
            ],
            space_held, micros=30 * count / own, deps=deps, previous=previous,
        )

    half = own // 2
    if near is not None:
        outs = space_back(0, half, zeros, [mlp_far], ())
        mlp_a, mlp_b, mlp_x, mlp_y, mlp_own = near.reduce_first(mlp_mine, core_swap(mlp_far), [outs[0]])
        outs = space_back(half, own - half, outs[-1], [mlp_a, mlp_b], tuple(outs[:-1]))
        mlp_x, mlp_y = near.reduce_second(mlp_x, mlp_y, mlp_a, mlp_b, [outs[0]])
        time_deps = [mlp_x, mlp_y]
    else:
        outs = space_back(0, own, zeros, [], ())
        time_deps = []
    branch_grad, space_mixed_grad, after_grad, time_grad, time_att_grad, space_sums = outs

    space_mine, space_far = space_outer(
        my_slot, *[flat(v) for v in (space_low, space_mixed_grad, space_att, branch_grad, time_att, time_grad)],
        deps=time_deps,
    )
    time_deps = time_deps + [space_far]
    far_frames = frames - own
    lanes_of = lambda shape: pl.BlockSpec(shape[:-1] + (2 * LANES,), lambda s: (0,) * (len(shape) - 1) + (s,))
    lanes_in = lambda v: (lanes_of(v.shape), v)
    q_grad, own_grad, far_grad = call(
        time_back_kernel, (width // LANES // 2,),
        [
            lanes_in(queries), lanes_in(key_rows), lanes_in(value_rows), (whole(prob_shape), time_prob),
            lanes_in(time_att_grad),
        ],
        [
            (lanes_of(shape), sds(shape, BRAIN))
            for shape in (frame_shape, (2,) + frame_shape, (2, far_frames, rows, width))
        ],
        micros=19, deps=time_deps,
    )
    if near is not None:
        from_far = core_swap(far_grad)
        mlp_first, mlp_second, mlp_others = near.reduce_third(mlp_own, mlp_x, mlp_y, [q_grad])
        space_a, space_b, space_x, space_y, space_own = near.reduce_first(space_mine, core_swap(space_far), [mlp_second])
        mixed_deps = [space_own]
    else:
        mixed_deps = []
        padded = jnp.concatenate([jnp.zeros_like(own_grad), far_grad], axis=1)
        padded = jnp.roll(padded, core * own, axis=1)
        from_far = lax.psum_scatter(padded, "frame", scatter_dimension=1, tiled=True)
    pair_in = lambda v: (pl.BlockSpec((2, group, rows, width), lambda s: (0, s, 0, 0)), v)
    time_mixed_grad = call(
        mixed_grad_kernel, (own // group,), [frames_in(q_grad), pair_in(own_grad), pair_in(from_far)],
        [low_out(mixed_shape)], micros=3, deps=mixed_deps,
    )[0]
    outer = (flat(time_low), flat(time_mixed_grad))

    back_deps = []
    if near is not None:
        space_x, space_y = near.reduce_second(space_x, space_y, space_a, space_b, [time_mixed_grad])
        back_deps = [mlp_second, space_x, space_y]
    token_grad, time_sums = call(
        time_mix_back_kernel, (own // group,),
        [(smem(), info), frames_in(tokens), vec_in, frames_in(time_mixed_grad), frames_in(after_grad)]
        + pair(time_w),
        [wide_out(out_shape), sum_out],
        time_held, micros=4, deps=back_deps,
    )
    bias_grad = mlp_sums[3 : 3 + bias_rows].reshape(width, bias_rows)
    n_sums = 13
    sums = call(
        sums_kernel, (1,), [(small, time_sums), (small, space_sums), (small, mlp_sums), (whole(bias_grad.shape), bias_grad)],
        [(whole((width, LANES)), sds((width, LANES), FLOAT))], [pltpu.VMEM((LANES, width), FLOAT)],
    )[0]

    if near is not None:
        mlp_grads = near.reduce_direct(mlp_first, mlp_second, mlp_others, [token_grad])[0]
        space_parts = near.reduce_third(space_own, space_x, space_y, [mlp_grads])
        time_mine, time_far = time_outer(my_slot, *outer, sums, deps=[space_parts[1]])
        time_a, time_b, time_x, time_y, time_own = near.reduce_first(time_mine, core_swap(time_far), [])
        time_x, time_y = near.reduce_second(time_x, time_y, time_a, time_b, [])
        time_parts = near.reduce_third(time_own, time_x, time_y, [])
        space_grads = near.reduce_direct(*space_parts, widths=[3 * width, width, width])
        grad_time, sums = near.reduce_direct(*time_parts, widths=[3 * width, LANES])
        grad_mlp_down = mlp_grads[2 * cut :]
        grad_mlp_up = near.owner_rows(jnp.concatenate([mlp_grads[:cut], mlp_grads[cut : 2 * cut]], axis=1))
        class_total = space_sums[6:7] + core_swap(space_sums)[6:7]
    else:
        send = lambda v: lax.psum_scatter(v, AXES, scatter_dimension=0, tiled=True).astype(FLOAT)
        spread = lambda mine, far: jnp.stack([mine, far], axis=1).reshape(width, mine.shape[2])
        time_mine, time_far = time_outer(my_slot, *outer, sums)
        up = jnp.stack([v[:, : 2 * cut].reshape(BLOCKS, 2, cut, width) for v in (mlp_mine, mlp_far)])
        grad_mlp_up = send(jnp.transpose(up, (1, 3, 0, 2, 4)).reshape(width, wide))
        grad_mlp_down = send(jnp.stack([v[:, 2 * cut :] for v in (mlp_mine, mlp_far)], axis=1).reshape(wide, width))
        grad_space = send(spread(space_mine, space_far))
        space_grads = (grad_space[:, : 3 * width], grad_space[:, 3 * width : 4 * width], grad_space[:, 4 * width :])
        grad_time = send(spread(time_mine, time_far)[:, : 3 * width])
        class_total = lax.psum(space_sums[6:7], "frame")
        step = width // (clips * cores)
        sums = lax.dynamic_slice_in_dim(lax.psum(sums, AXES), shard * step, step, 0)
    class_in_grad = rows_grad[own - 1, places_here][None] + class_total
    lines = sums.T
    grad_time_vec, grad_space_vec, grad_mlp_vec = lines[:5], lines[5:10], lines[10:13]
    grad_mlp_bias = sums[:, n_sums : n_sums + bias_rows].reshape(-1)
    return (
        result[None],
        class_result[places_here % 8][None].astype(BRAIN),
        token_grad[None],
        class_in_grad,
        grad_time,
        space_grads[2],
        grad_time_vec,
        space_grads[0],
        space_grads[1],
        grad_space_vec,
        grad_mlp_up,
        grad_mlp_down,
        grad_mlp_vec,
        grad_mlp_bias,
    )


def solution(mesh):
    both = ("clip", "frame")
    rows = P(both, None)
    columns = P(None, both)
    weights = (rows, rows, columns, rows, rows, columns, rows, rows, columns, P(both))
    block = P("clip", "frame", None, None)
    classes = P("clip", None)
    return jax.shard_map(
        functools.partial(body, mesh.shape["clip"], mesh.shape["frame"]),
        mesh=mesh,
        in_specs=(block, classes, block, classes, P("clip")) + weights,
        out_specs=(block, classes, block, classes) + weights,
        check_vma=False,
    )
```

```python
import functools

import jax
import jax.numpy as jnp
from jax import lax
from jax.experimental import pallas as pl
from jax.experimental.pallas import tpu as pltpu
from jax.sharding import PartitionSpec as P

HEAD_DIM = 64
EPSILON = 1e-06
FLOAT = jnp.float32
BRAIN = jnp.bfloat16
LANES = 128
BLOCKS = 16
RATE = 1e9
VMEM_BYTES = 60 * 1024 * 1024


def nn(left, right):
    return lax.dot_general(left, right, (((1,), (0,)), ((), ())), preferred_element_type=FLOAT)


def nt(left, right):
    return lax.dot_general(left, right, (((1,), (1,)), ((), ())), preferred_element_type=FLOAT)


def tn(left, right):
    return lax.dot_general(left, right, (((0,), (0,)), ((), ())), preferred_element_type=FLOAT)


def unit_of(values):
    average = jnp.mean(values, axis=-1, keepdims=True)
    centred = values - average
    spread = jnp.mean(centred * centred, axis=-1, keepdims=True)
    inverse = lax.rsqrt(spread + EPSILON)
    return centred * inverse, inverse


def norm_back(unit, inverse, gain, upstream):
    scaled = upstream * gain
    inner = jnp.mean(scaled, axis=-1, keepdims=True)
    along = jnp.mean(scaled * unit, axis=-1, keepdims=True)
    return inverse * (scaled - inner - unit * along)


def column_sum(values):
    return jnp.sum(values, axis=0, keepdims=True)


def row_index(shape):
    return lax.broadcasted_iota(jnp.int32, shape, 0)


def head_map(width, first=0):
    lane = lax.broadcasted_iota(jnp.int32, (width, LANES), 0) // HEAD_DIM + first
    head = lax.broadcasted_iota(jnp.int32, (width, LANES), 1)
    return (lane == head).astype(FLOAT).astype(BRAIN)


def head_spread(width, first=0):
    head = lax.broadcasted_iota(jnp.int32, (LANES, width), 0)
    lane = lax.broadcasted_iota(jnp.int32, (LANES, width), 1) // HEAD_DIM + first
    return (lane == head).astype(FLOAT).astype(BRAIN)


def column_copies(core, mine, other, held, sems):
    half = held.shape[1] // 2
    copies = []
    for n, (source, slot) in enumerate(((mine, core), (other, 1 - core))):
        target = held.at[:, pl.ds(pl.multiple_of(slot * half, LANES), half)]
        copies.append(pltpu.make_async_copy(source.at[:, :half], target, sems.at[n]))
    return copies


def mlp_copies(core, plane, mine, other, up, down, sems):
    cut = up.shape[3]
    ups, downs = [], []
    for k, (sources, slot) in enumerate(((mine, core), (other, 1 - core))):
        for n, source in enumerate(sources):
            if len(sources) == 1:
                at, tail = (), (slice(None),)
            else:
                at, tail = ((slice(None), slice(0, 2), slice(2, 4))[max(n - 2, 0)], plane ^ min(n, 3)), ()
            rows = lambda low, high: source.at[(slice(None),) + tail + (slice(low, high),)]
            for t in (0, 1):
                part = up.at[(2 * slot + t,) + at]
                ups.append(pltpu.make_async_copy(rows(t * cut, (t + 1) * cut), part, sems.at[k, 3 * n + t]))
            part = down.at[at + (slot,)] if at else down.at[:, :, slot]
            downs.append(pltpu.make_async_copy(rows(2 * cut, 4 * cut), part, sems.at[k, 3 * n + 2]))
    return ups, downs


def start_first(copies):
    @pl.when(pl.program_id(0) == 0)
    def _():
        for copy in copies:
            copy.start()


def wait_first(copies):
    @pl.when(pl.program_id(0) == 0)
    def _():
        for copy in copies:
            copy.wait()


def merged(ref):
    return ref[...].reshape(ref.shape[0] * ref.shape[1], ref.shape[2])


def store(ref, value):
    ref[...] = value.astype(ref.dtype).reshape(ref.shape)


def marks(count, rows, low, high):
    index = row_index((count * rows, 1))
    found = (index >= low) & (index < high)
    for n in range(1, count):
        found = found | ((index >= n * rows + low) & (index < n * rows + high))
    return found


def time_mix_kernel(own_steps, info, tokens, far_tokens, vectors, w_mine, w_other, q_out, k_out, v_out, low_out, held, sems):
    step = pl.program_id(0)
    width = tokens.shape[-1]

    copies = column_copies(info[0], w_mine, w_other, held, sems)
    start_first(copies)
    unit, _ = unit_of(jnp.where(step < own_steps, merged(tokens).astype(FLOAT), merged(far_tokens).astype(FLOAT)))
    low = (unit * vectors[0:1] + vectors[1:2]).astype(BRAIN)
    wait_first(copies)
    store(k_out, nn(low, held[:, width : 2 * width]))
    store(v_out, nn(low, held[:, 2 * width :]) + vectors[3:4])

    @pl.when(step < own_steps)
    def _():
        queries = (nn(low, held[:, :width]) + vectors[2:3]).astype(BRAIN)
        store(q_out, queries * jnp.asarray(HEAD_DIM ** (-0.5), BRAIN))
        store(low_out, low)


def tree_sum(values):
    values = list(values)
    while len(values) > 1:
        values = [a + b for a, b in zip(values[::2], values[1::2])] + values[len(values) & ~1 :]
    return values[0]


def attention_kernel(
    places_here, info, tokens, vectors, q_in, k_in, v_in, begin, sw_mine, sw_other,
    prob_out, att_out, after_out, low_out, mixed_out, sprob_out, satt_out, places_out, class_out,
    held, sems,
):
    step = pl.program_id(0)
    frames = k_in.shape[0]
    count, rows, width = tokens.shape
    core = info[0]

    copies = column_copies(core, sw_mine, sw_other, held, sems)
    start_first(copies)
    mapping = head_map(width)
    spread = head_spread(width)
    for n in range(count):
        queries = q_in[n]
        scores = [nn(queries * k_in[g], mapping) for g in range(frames)]
        top = functools.reduce(jnp.maximum, scores)
        powers = [jnp.exp(s - top) for s in scores]
        scale = 1.0 / sum(powers)
        parts = []
        for g in range(frames):
            prob = (powers[g] * scale).astype(BRAIN)
            prob_out[n, g] = prob
            parts.append(nn(prob, spread).astype(BRAIN) * v_in[g])
        att_out[n] = tree_sum(parts)
    wait_first(copies)
    attended = merged(att_out)
    place = marks(count, rows, 0, places_here)
    base = merged(tokens).astype(FLOAT)
    after = jnp.where(place, base + (nn(attended, held[:, 4 * width :]) + vectors[4:5]), base)
    store(after_out, after)
    unit, _ = unit_of(after)
    low = (unit * vectors[5:6] + vectors[6:7]).astype(BRAIN)
    store(low_out, low)
    shape = (count, rows, width)
    queries = (nn(low, held[:, :width]) + vectors[7:8]).astype(BRAIN) * jnp.asarray(HEAD_DIM ** (-0.5), BRAIN)
    mixed_out[:, :, :width] = queries.reshape(shape)
    mixed_out[:, :, width : 2 * width] = nn(low, held[:, width : 2 * width]).astype(BRAIN).reshape(shape)
    mixed_out[:, :, 2 * width :] = (
        (nn(low, held[:, 2 * width : 3 * width]) + vectors[8:9]).astype(BRAIN).reshape(shape)
    )
    lane = lax.broadcasted_iota(jnp.int32, (1, LANES), 1)
    masks = [(lane // HEAD_DIM == e).astype(FLOAT).astype(BRAIN) for e in (0, 1)]
    key_ok = row_index((rows, 1)) <= places_here
    for n in range(count):
        for pair in range(width // LANES):
            at = pair * LANES
            q2 = mixed_out[n, :, at : at + LANES]
            k2 = mixed_out[n, :, width + at : width + at + LANES]
            v2 = mixed_out[n, :, 2 * width + at : 2 * width + at + LANES]
            result = []
            for e in (0, 1):
                logits = jnp.where(key_ok, nt(k2, q2 * masks[e]), -1e30)
                power = jnp.exp(logits - jnp.max(logits, axis=0, keepdims=True))
                prob = (power * (1.0 / jnp.sum(power, axis=0, keepdims=True))).astype(BRAIN)
                sprob_out[n, 2 * pair + e] = prob
                result.append(tn(prob, v2))
            satt_out[n, :, at : at + LANES] = jnp.where(lane < HEAD_DIM, result[0], result[1]).astype(BRAIN)
    spatial = nn(merged(satt_out), held[:, 3 * width : 4 * width]) + vectors[9:10]
    store(places_out, jnp.where(place, after, 0.0) + spatial)

    @pl.when(step == 0)
    def _():
        class_out[...] = begin[...]

    class_row = column_sum(jnp.where(marks(count, rows, places_here, places_here + 1), spatial, 0.0))
    class_out[0:1] = class_out[0:1] + class_row


def gelu_parts(values):
    half = 0.5 + 0.5 * lax.erf(values * (0.5 ** 0.5))
    density = jnp.exp(values * values * (-0.5)) * (0.5 / 3.141592653589793) ** 0.5
    return values * half, half + values * density


def mlp_kernel(
    places_here, all_frames, pieces, info, alive, places, grads, class_row, class_own, class_far, vectors, bias,
    *others,
):
    mine, other, others = others[:pieces], others[pieces : 2 * pieces], others[2 * pieces :]
    out, class_out, low_out, hidden_out, feed_out, before_out, rows_out, sums, slopes, up, down, sems = others
    step = pl.program_id(0)
    count, rows, width = places.shape
    core = info[0]

    ups, downs = mlp_copies(core, info[3], mine, other, up, down, sems)
    start_first(ups + downs)

    @pl.when(step == 0)
    def _():
        sums[...] = jnp.zeros_like(sums)

    class_mid = class_row[0:1] + (class_own[0:1] + class_far[0:1]) * all_frames ** (-0.5)
    last = (count - 1) * rows + places_here
    is_class = (row_index((count * rows, 1)) == last) & (step == pl.num_programs(0) - 1)
    kept = jnp.logical_not(marks(count, rows, places_here, places_here + 1) & (info[1] == 0))
    values = jnp.where(is_class, class_mid, merged(places))
    unit, inverse = unit_of(values)
    low = (unit * vectors[10:11] + vectors[11:12]).astype(BRAIN)
    store(low_out, low)
    feed = jnp.zeros((count * rows, width), FLOAT)
    chunks = hidden_out.shape[-1] // width
    wait_first(ups)
    for j in range(chunks):
        before = nn(low, up[j].reshape(width, width)) + bias[j : j + 1]
        hidden, slope = gelu_parts(before)
        hidden = hidden.astype(BRAIN)
        hidden_out[:, :, j * width : (j + 1) * width] = hidden.reshape(count, rows, width)
        slopes[j] = slope
        if j == 0:
            wait_first(downs)
        feed = feed + nn(hidden, down[j].reshape(width, width))
    result = ((values + (feed + vectors[12:13])) * alive[0]).reshape(count, rows, width)
    out[...] = result[:, :places_here].astype(BRAIN)
    class_out[...] = result[count - 1, places_here - places_here % 8 : places_here - places_here % 8 + 8]

    row_grad = merged(grads).astype(FLOAT) * alive[0]
    feed_grad = row_grad.astype(BRAIN)
    feed_kept = jnp.where(kept, row_grad, 0.0).astype(BRAIN)
    store(feed_out, feed_kept)
    sums[2:3] = sums[2:3] + column_sum(feed_kept.astype(FLOAT))
    upstream = jnp.zeros((count * rows, width), FLOAT)
    for j in range(chunks):
        hidden_grad = nt(feed_grad, down[j].reshape(width, width))
        before_grad = (hidden_grad * slopes[j]).astype(BRAIN)
        before_kept = jnp.where(kept, before_grad.astype(FLOAT), 0.0)
        before_out[:, :, j * width : (j + 1) * width] = before_kept.astype(BRAIN).reshape(count, rows, width)
        sums[3 + j : 4 + j] = sums[3 + j : 4 + j] + column_sum(before_kept)
        upstream = upstream + nt(before_grad, up[j].reshape(width, width))
    store(rows_out, row_grad + norm_back(unit, inverse, vectors[10:11], upstream))
    upstream = jnp.where(kept, upstream, 0.0)
    sums[0:1] = sums[0:1] + column_sum(upstream * unit)
    sums[1:2] = sums[1:2] + column_sum(upstream)


def space_back_kernel(
    places_here, all_frames, info, rows_grad, class_grad, after, mixed, sprob, satt, vectors, begin,
    sw_mine, sw_other,
    branch_out, mixed_out, after_out, time_out, att_out, sums, held, sems,
):
    step = pl.program_id(0)
    count, rows, width = after.shape
    core = info[0]

    copies = column_copies(core, sw_mine, sw_other, held, sems)
    start_first(copies)

    @pl.when(step == 0)
    def _():
        sums[...] = begin[...]

    place = marks(count, rows, 0, places_here)
    class_at = marks(count, rows, places_here, places_here + 1)
    offset = places_here % 16
    share = class_grad[0, offset : offset + 1] * all_frames ** (-0.5)
    direct = jnp.where(place, merged(rows_grad), 0.0)
    branch = jnp.where(class_at, share, direct).astype(BRAIN)
    store(branch_out, branch)
    sums[4:5] = sums[4:5] + column_sum(branch.astype(FLOAT))
    unit, inverse = unit_of(merged(after))
    wait_first(copies)
    att_grad = nt(branch, held[:, 3 * width : 4 * width]).astype(BRAIN)
    store(att_out, att_grad)
    spread = head_spread(width)
    lane = lax.broadcasted_iota(jnp.int32, (1, LANES), 1)
    masks = [(lane // HEAD_DIM == e).astype(FLOAT).astype(BRAIN) for e in (0, 1)]
    left = lane < HEAD_DIM
    for n in range(count):
        product = att_out[n].astype(FLOAT) * satt[n].astype(FLOAT)
        high = product.astype(BRAIN)
        rowdots = nt(spread, high) + nt(spread, (product - high.astype(FLOAT)).astype(BRAIN))
        for pair in range(width // LANES):
            at = pair * LANES
            a2 = att_out[n, :, at : at + LANES]
            q2 = mixed[n, :, at : at + LANES]
            k2 = mixed[n, :, width + at : width + at + LANES]
            v2 = mixed[n, :, 2 * width + at : 2 * width + at + LANES]
            queries, key_rows, value_rows = [], [], []
            for e in (0, 1):
                head = 2 * pair + e
                prob = sprob[n, head]
                prob_grad = nt(v2, a2 * masks[e])
                score = (prob.astype(FLOAT) * (prob_grad - rowdots[head : head + 1])).astype(BRAIN)
                queries.append(tn(score, k2))
                key_rows.append(nn(score, q2))
                value_rows.append(nn(prob, a2))
            q_grad = (jnp.where(left, queries[0], queries[1]) * HEAD_DIM ** (-0.5)).astype(BRAIN)
            k_grad = jnp.where(left, key_rows[0], key_rows[1]).astype(BRAIN)
            v_grad = jnp.where(left, value_rows[0], value_rows[1]).astype(BRAIN)
            mixed_out[n, :, at : at + LANES] = q_grad
            mixed_out[n, :, width + at : width + at + LANES] = k_grad
            mixed_out[n, :, 2 * width + at : 2 * width + at + LANES] = v_grad
    mixed_grad = merged(mixed_out)
    sums[2:3] = sums[2:3] + column_sum(mixed_grad[:, :width].astype(FLOAT))
    sums[3:4] = sums[3:4] + column_sum(mixed_grad[:, 2 * width :].astype(FLOAT))
    upstream = nt(mixed_grad, held[:, : 3 * width])
    inner = norm_back(unit, inverse, vectors[5:6], upstream)
    sums[0:1] = sums[0:1] + column_sum(upstream * unit)
    sums[1:2] = sums[1:2] + column_sum(upstream)
    sums[6:7] = sums[6:7] + column_sum(jnp.where(class_at, inner, 0.0))
    after_grad = jnp.where(place, direct + inner, 0.0)
    store(after_out, after_grad)
    low = after_grad.astype(BRAIN)
    store(time_out, low)
    sums[5:6] = sums[5:6] + column_sum(low.astype(FLOAT))
    store(att_out, nt(low, held[:, 4 * width :]))


def time_back_kernel(q_in, k_in, v_in, prob_in, att_in, q_out, own_out, far_out):
    own, rows, width = q_in.shape
    frames = k_in.shape[0]
    first = pl.program_id(0) * (width // HEAD_DIM)
    mapping = head_map(width, first)
    spread = head_spread(width, first)
    size = 16

    def chunk(index, carry):
        at = pl.ds(pl.multiple_of(index * size, size), size)
        values = [v_in[g, at] for g in range(frames)]
        att = [att_in[f, at] for f in range(own)]
        products = jnp.concatenate([att[f] * values[g] for f in range(own) for g in range(frames)], axis=0)
        prob_grad = nn(products, mapping)
        probs = [prob_in[f, g, at] for f in range(own) for g in range(frames)]
        scores = []
        for f in range(own):
            wide = [probs[f * frames + g].astype(FLOAT) for g in range(frames)]
            weighted = [
                wide[g] * prob_grad[(f * frames + g) * size : (f * frames + g + 1) * size] for g in range(frames)
            ]
            rowdot = sum(weighted)
            scores += [(weighted[g] - wide[g] * rowdot).astype(BRAIN) for g in range(frames)]
        score_wide = nn(jnp.concatenate(scores, axis=0), spread).astype(BRAIN)
        prob_wide = nn(jnp.concatenate(probs, axis=0), spread).astype(BRAIN)

        def part(array, f, g):
            return array[(f * frames + g) * size : (f * frames + g + 1) * size]

        keys = [k_in[g, at] for g in range(frames)]
        for f in range(own):
            total = tree_sum(part(score_wide, f, g) * keys[g] for g in range(frames))
            q_out[f, at] = total * jnp.asarray(HEAD_DIM ** (-0.5), BRAIN)
        queries = [q_in[f, at] for f in range(own)]
        for g in range(frames):
            key_grad = tree_sum(part(score_wide, f, g) * queries[f] for f in range(own))
            value_grad = tree_sum(part(prob_wide, f, g) * att[f] for f in range(own))
            if g < own:
                own_out[0, g, at] = key_grad
                own_out[1, g, at] = value_grad
            else:
                far_out[0, g - own, at] = key_grad
                far_out[1, g - own, at] = value_grad
        return carry

    lax.fori_loop(0, rows // size, chunk, 0, unroll=True)


def time_mix_back_kernel(info, tokens, vectors, mixed, after_grad, w_mine, w_other, token_out, sums, held, sems):
    step = pl.program_id(0)
    width = tokens.shape[-1]

    copies = column_copies(info[0], w_mine, w_other, held, sems)
    start_first(copies)

    @pl.when(step == 0)
    def _():
        sums[...] = jnp.zeros_like(sums)

    mixed_grad = merged(mixed)
    sums[2:3] = sums[2:3] + column_sum(mixed_grad[:, :width].astype(FLOAT))
    sums[3:4] = sums[3:4] + column_sum(mixed_grad[:, 2 * width :].astype(FLOAT))
    unit, inverse = unit_of(merged(tokens).astype(FLOAT))
    wait_first(copies)
    upstream = nt(mixed_grad, held[...])
    result = merged(after_grad) + norm_back(unit, inverse, vectors[0:1], upstream)
    token_out[...] = result.reshape(mixed.shape[:2] + (width,))[:, : token_out.shape[1]]
    sums[0:1] = sums[0:1] + column_sum(upstream * unit)
    sums[1:2] = sums[1:2] + column_sum(upstream)


def mixed_grad_kernel(queries, own, far, out):
    width = queries.shape[2]
    out[:, :, :width] = queries[...]
    out[:, :, width : 2 * width] = (own[0].astype(FLOAT) + far[0].astype(FLOAT)).astype(BRAIN)
    out[:, :, 2 * width :] = (own[1].astype(FLOAT) + far[1].astype(FLOAT)).astype(BRAIN)


def sums_kernel(time_sums, space_sums, mlp_sums, bias, out, lines):
    lines[...] = jnp.zeros_like(lines)
    lines[0:4] = time_sums[0:4]
    lines[4:5] = space_sums[5:6]
    lines[5:10] = space_sums[0:5]
    lines[10:13] = mlp_sums[0:3]
    count = bias.shape[1]
    place = lax.broadcasted_iota(jnp.int32, (count, LANES), 1) == row_index((count, LANES)) + 13
    spread = lax.dot_general(
        bias[...], place.astype(FLOAT), (((1,), (0,)), ((), ())), preferred_element_type=FLOAT,
        precision=lax.Precision.HIGHEST,
    )
    out[...] = lines[...].T + spread


def halves_kernel(left, right, left_out, right_out):
    left_out[...] = left[...]
    right_out[...] = right[...]


def share_rows(info, value, mine, other, at=slice(None)):
    value = value.reshape(mine.shape[0], 2, mine.shape[1], value.shape[-1])
    first = info[0] == 0
    mine[:, :, at] = jnp.where(first, value[:, 0], value[:, 1]).astype(BRAIN)
    other[:, :, at] = jnp.where(first, value[:, 1], value[:, 0]).astype(BRAIN)


def time_outer_kernel(info, left, right, sums, mine, other):
    step = pl.program_id(0)
    width = left.shape[1]

    for n in range(3):

        @pl.when(step == n)
        def _():
            share_rows(info, tn(left[...], right[...]), mine, other, slice(n * width, (n + 1) * width))

    @pl.when(step == 0)
    def _():
        share_rows(info, sums[...], mine, other, slice(3 * width, 3 * width + sums.shape[1]))


def space_outer_kernel(info, low, mixed, att, branch, time_att, time_grad, mine, other):
    step = pl.program_id(0)

    @pl.when(step < 3)
    def _():
        share_rows(info, tn(low[...], mixed[...]), mine, other)

    @pl.when(step == 3)
    def _():
        share_rows(info, tn(att[...], branch[...]), mine, other)

    @pl.when(step == 4)
    def _():
        share_rows(info, tn(time_att[...], time_grad[...]), mine, other)


def mlp_outer_kernel(info, low, before, hidden, feed, mine, other, turned, ups, downs, sems):
    step = pl.program_id(0)
    steps = ups.shape[0]
    blocks, cut, width = ups.shape[1:]
    per = downs.shape[2]

    @pl.when(step == 0)
    def _():
        turned[...] = low[...].T

    ups[step] = nn(turned[...], before[...]).astype(BRAIN).reshape(blocks, cut, width)
    value = tn(hidden[...], feed[...]).astype(BRAIN).reshape(per, 2, 2 * cut, width)
    downs[step, 0] = value[:, 0]
    downs[step, 1] = value[:, 1]

    for n in range(steps):
        targets = (mine, other)
        for k, slot in ((0, info[0]), (1, 1 - info[0])):
            up_copy = pltpu.make_async_copy(
                ups.at[n], targets[k].at[:, (n % 2) * cut : (n % 2 + 1) * cut], sems.at[0, n]
            )
            down_copy = pltpu.make_async_copy(
                downs.at[n, slot], targets[k].at[n * per : (n + 1) * per, 2 * cut :], sems.at[1 + k, n]
            )

            @pl.when((step == n) & (slot == n // 2))
            def _():
                up_copy.start()

            @pl.when(step == n)
            def _():
                down_copy.start()

            @pl.when((step == steps - 1) & (slot == n // 2))
            def _():
                up_copy.wait()

            @pl.when(step == steps - 1)
            def _():
                down_copy.wait()


def smem():
    return pl.BlockSpec(memory_space=pltpu.SMEM)


def hbm():
    return pl.BlockSpec(memory_space=pl.ANY)


def whole(shape):
    return pl.BlockSpec(shape, lambda *_: (0,) * len(shape))


def per_frame(shape, first=0, count=1):
    return pl.BlockSpec((count,) + shape[1:], lambda s: (s + first // count,) + (0,) * (len(shape) - 1))


def sds(shape, kind):
    return jax.ShapeDtypeStruct(shape, kind)


def call(kernel, grid, inputs, outputs, scratch=(), micros=2, deps=(), previous=(), prefetch=0):
    count = len(inputs)
    skip = len(previous) + len(deps)

    def inner(*refs):
        kernel(*refs[:count], *refs[count + skip :])

    specs = [spec for spec, _ in inputs[prefetch:]] + [hbm()] * skip
    common = dict(
        name=getattr(kernel, "func", kernel).__name__,
        out_shape=[shape for _, shape in outputs],
        compiler_params=pltpu.CompilerParams(vmem_limit_bytes=VMEM_BYTES),
        input_output_aliases={count + n: n for n in range(len(previous))},
        cost_estimate=pl.CostEstimate(flops=int(micros * RATE), bytes_accessed=1, transcendentals=0),
    )
    places = dict(grid=grid, in_specs=specs, out_specs=[spec for spec, _ in outputs], scratch_shapes=list(scratch))
    if prefetch:
        common["grid_spec"] = pltpu.PrefetchScalarGridSpec(num_scalar_prefetch=prefetch, **places)
    else:
        common.update(places)
    return pl.pallas_call(inner, **common)(*[array for _, array in inputs], *previous, *deps)


def time_outer(slot, left, right, sums, deps=()):
    rows, width = left.shape
    wide = right.shape[1]
    shape = (BLOCKS, width // (2 * BLOCKS), wide + sums.shape[1])
    return call(
        time_outer_kernel, (3,),
        [
            (smem(), slot), (whole(left.shape), left), (pl.BlockSpec((rows, width), lambda s: (0, s)), right),
            (whole(sums.shape), sums),
        ],
        [(whole(shape), sds(shape, BRAIN))] * 2, micros=8, deps=deps,
    )


def space_outer(slot, low, mixed, *others, deps=()):
    rows, width = low.shape
    shape = (BLOCKS, width // (2 * BLOCKS), width)
    moving = pl.BlockSpec((rows, width), lambda s: (0, jnp.minimum(s, 2)))
    return call(
        space_outer_kernel, (5,),
        [(smem(), slot), (whole(low.shape), low), (moving, mixed)] + [(whole(v.shape), v) for v in others],
        [(pl.BlockSpec(shape, lambda s: (0, 0, s)), sds(shape[:2] + (5 * width,), BRAIN))] * 2, micros=12, deps=deps,
    )


def mlp_outer(slot, low, before, hidden, feed, deps=()):
    rows, width = low.shape
    wide = hidden.shape[1]
    cut = width // BLOCKS
    shape = (BLOCKS, 4 * cut, width)
    fixed = pl.BlockSpec((rows, width), lambda s, info: (0, 0))
    moving = pl.BlockSpec((rows, width), lambda s, info: (0, s))
    return call(
        mlp_outer_kernel, (wide // width,),
        [(None, slot), (fixed, low), (moving, before), (moving, hidden), (fixed, feed)],
        [(hbm(), sds(shape, BRAIN))] * 2,
        [
            pltpu.VMEM((width, rows), BRAIN),
            pltpu.VMEM((wide // width, BLOCKS, cut, width), BRAIN),
            pltpu.VMEM((wide // width, 2, BLOCKS * width // wide, 2 * cut, width), BRAIN),
            pltpu.SemaphoreType.DMA((3, wide // width)),
        ],
        micros=21, deps=deps, prefetch=1,
    )


def gate(value, deps):
    return pl.pallas_call(
        lambda source, *refs: None,
        in_specs=[hbm()] * (1 + len(deps)),
        out_specs=hbm(),
        out_shape=sds(value.shape, value.dtype),
        input_output_aliases={0: 0},
    )(value, *deps)


def stack_at_kernel(info, *refs):
    for n, ref in enumerate(refs[:-1]):
        refs[-1][info[2] ^ n] = ref[...]


def stack_kernel(*refs):
    for n, ref in enumerate(refs[:-1]):
        refs[-1][n] = ref[...]


def add_kernel(left, right, out):
    out[...] = left[...] + right[...]


def add_after(left, right, deps):
    inputs = [(whole(left.shape), left), (whole(right.shape), right)]
    return call(add_kernel, (1,), inputs, [(whole(left.shape), sds(left.shape, left.dtype))], deps=deps)[0]


def assemble_kernel(info, o4, rx, ry, ra, rb, out):
    depth = info[2]
    plane = info[3]
    for m in range(4):
        for n in range(4):
            if n < 3:
                value = (o4, rx, ry)[n][m]
            else:
                value = ra[m] if m < 2 else rb[m - 2]
            out[(depth ^ m) * 4 + (plane ^ n)] = value


def pack_kernel(info, time_qkv, space_qkv, space_proj, time_proj, up, time_vec, space_vec, mlp_vec, bias, send, keep):
    width = time_proj.shape[1]
    half = width // 2
    pieces = [time_qkv[:, n * half : (n + 1) * half] for n in range(6)]
    pieces += [space_qkv[:, n * half : (n + 1) * half] for n in range(6)]
    pieces += [space_proj[:, :half], space_proj[:, half:], time_proj[:, :half], time_proj[:, half:]]
    pieces += [up[:, n * half : (n + 1) * half] for n in range(8)]
    first = info[0] == 0
    at = 0
    for begin, count in ((0, 3), (6, 5), (16, 4)):
        for n in range(count):
            low, high = pieces[begin + n], pieces[begin + count + n]
            keep[:, at : at + half] = jnp.where(first, low, high)
            send[:, at : at + half] = jnp.where(first, high, low)
            at += half
    line = 0
    total = jnp.zeros((keep.shape[0], LANES), FLOAT)
    for source in (time_vec, space_vec, mlp_vec, bias):
        count = source.shape[0]
        lane = lax.broadcasted_iota(jnp.int32, (count, LANES), 1)
        chosen = (lane == row_index((count, LANES)) + line).astype(FLOAT)
        total = total + lax.dot_general(
            source[...].astype(FLOAT), chosen, (((0,), (0,)), ((), ())), preferred_element_type=FLOAT
        )
        line += count
    keep[:, at:] = total.astype(BRAIN)
    send[:, at:] = total.astype(BRAIN)


def turn_kernel(source, out):
    out[...] = source[...].astype(FLOAT).T


def join_kernel(info, keep, come, down, time_out, space_out, mlp_out):
    first = info[0] == 0
    width = down.shape[1]
    mine, far = keep[...].astype(FLOAT), come[...].astype(FLOAT)
    both = jnp.concatenate([jnp.where(first, mine, far), jnp.where(first, far, mine)], axis=0).astype(BRAIN)
    cut = both.shape[0]
    end = time_out.shape[1] - LANES
    time_out[:, :end] = both[:, :end]
    time_out[:, end:] = both[:, both.shape[1] - LANES :]
    space_out[...] = both[:, end : end + space_out.shape[1]]
    at = end + space_out.shape[1]
    mlp_out[:cut] = both[:, at : at + width]
    mlp_out[cut : 2 * cut] = both[:, at + width : at + 2 * width]
    mlp_out[2 * cut :] = down[...]


def added(*values):
    return sum(v.astype(FLOAT) for v in values).astype(BRAIN)


def reduce_first_kernel(info, mine, far, to_y, to_x, near_x, near_y, own):
    step = pl.program_id(0)
    plane = info[3]
    own[0] = added(mine[0, plane], far[0, plane])
    near_x[0] = added(mine[0, plane ^ 1], far[0, plane ^ 1])
    near_y[0] = added(mine[0, plane ^ 2], far[0, plane ^ 2])
    diagonal = added(mine[0, plane ^ 3], far[0, plane ^ 3])

    @pl.when(step < 2)
    def _():
        to_y[0] = diagonal

    @pl.when(step >= 2)
    def _():
        to_x[0] = diagonal


def reduce_second_kernel(near_x, near_y, from_y, from_x, out_x, out_y):
    step = pl.program_id(0)

    @pl.when(step < 2)
    def _():
        out_x[0] = added(near_x[0], from_y[0])
        out_y[0] = near_y[0]

    @pl.when(step >= 2)
    def _():
        out_x[0] = near_x[0]
        out_y[0] = added(near_y[0], from_x[0])


def reduce_third_kernel(info, own, from_x, from_y, *outs):
    for m, out in enumerate(outs):
        at = info[2] ^ m
        out[...] = added(own[at], from_x[at], from_y[at])


def final_kernel(first, second, third, fourth, *outs):
    at = 0
    for out in outs:
        part = slice(at, at + out.shape[1])
        out[...] = (first[:, part].astype(FLOAT) + second[:, part].astype(FLOAT)) + (
            third[:, part].astype(FLOAT) + fourth[:, part].astype(FLOAT)
        )
        at += out.shape[1]


def final_mlp_kernel(first, second, third, fourth, up, down):
    cut, width = up.shape[0], down.shape[1]
    total = (first[...].astype(FLOAT) + second[...].astype(FLOAT)) + (
        third[...].astype(FLOAT) + fourth[...].astype(FLOAT)
    )
    up[:, :width] = total[:cut]
    up[:, width:] = total[cut : 2 * cut]
    down[...] = total[2 * cut :]


def exact(left, right, sides):
    return lax.dot_general(
        left, right, ((sides[:1], sides[1:]), ((), ())), preferred_element_type=FLOAT, precision=lax.Precision.HIGHEST
    )


def final_time_kernel(first, second, third, fourth, out, time_vec, space_vec, mlp_vec, bias):
    total = (first[...].astype(FLOAT) + second[...].astype(FLOAT)) + (
        third[...].astype(FLOAT) + fourth[...].astype(FLOAT)
    )
    end = out.shape[1]
    out[...] = total[:, :end]
    sums = total[:, end:]
    rows = sums.shape[0]
    same = row_index((rows, rows)) == lax.broadcasted_iota(jnp.int32, (rows, rows), 1)
    lines = exact(sums, same.astype(FLOAT), (0, 0))
    at = 0
    for ref in (time_vec, space_vec, mlp_vec):
        ref[...] = lines[at : at + ref.shape[0]]
        at += ref.shape[0]
    count = bias.shape[1]
    chosen = row_index((LANES, count)) == lax.broadcasted_iota(jnp.int32, (LANES, count), 1) + at
    bias[...] = exact(sums, chosen.astype(FLOAT), (1, 0))


def reduce_fourth_kernel(first, second, come, first_out, second_out):
    first_out[...] = first[...].astype(FLOAT) + come[0].astype(FLOAT)
    second_out[...] = added(second[...], come[1])


def clip_swap(values, bits, count):
    return lax.ppermute(values, "clip", [(i, i ^ bits) for i in range(count)])


def core_swap(values):
    return lax.ppermute(values, "frame", [(0, 1), (1, 0)])


class Near:
    def __init__(self, clips, info):
        self.clips = clips
        self.info = info
        self.core = lax.axis_index("frame")

    def swap(self, values, bits):
        return clip_swap(values, bits, self.clips)

    def in_order(self, mine, far, axis):
        return jnp.where(
            self.core == 0, jnp.concatenate([mine, far], axis=axis), jnp.concatenate([far, mine], axis=axis)
        )

    def stack(self, pieces, deps):
        shape = (len(pieces),) + pieces[0].shape
        return call(
            stack_kernel, (1,), [(whole(v.shape), v) for v in pieces], [(whole(shape), sds(shape, BRAIN))],
            micros=3, deps=deps,
        )[0]

    def depth_direct(self, own, deps):
        return self.stack([own] + [self.swap(own, 4 * m) for m in (1, 2, 3)], deps)

    def depth_in_order(self, own, deps):
        pieces = [own] + [self.swap(own, 4 * m) for m in (1, 2, 3)]
        shape = (4,) + own.shape
        return call(
            stack_at_kernel, (1,), [(smem(), self.info)] + [(whole(v.shape), v) for v in pieces],
            [(whole(shape), sds(shape, BRAIN))], micros=3, deps=deps,
        )[0]

    def depth_near(self, own, deps):
        return self.stack([own, self.swap(own, 4)], deps)

    def depth_far(self, two, deps):
        come = self.swap(two, 8)
        return self.stack([two[0], two[1], come[0], come[1]], deps)

    def plane_step(self, o4, deps):
        rx = self.swap(o4, 1)
        ry = self.swap(o4, 2)
        half = (2,) + o4.shape[1:]
        first = pl.BlockSpec(half, lambda s: (0, 0, 0))
        second = pl.BlockSpec(half, lambda s: (1, 0, 0))
        sx, sy = call(
            halves_kernel, (1,), [(first, rx), (second, ry)], [(whole(half), sds(half, BRAIN))] * 2, deps=deps
        )
        return rx, ry, sx, sy

    def diagonal_step(self, o4, planes, deps):
        rx, ry, sx, sy = planes
        pieces = (o4, rx, ry, self.swap(sx, 2), self.swap(sy, 1))
        shape = (self.clips,) + o4.shape[1:]
        return call(
            assemble_kernel, (1,), [(smem(), self.info)] + [(whole(v.shape), v) for v in pieces],
            [(whole(shape), sds(shape, BRAIN))], micros=3, deps=deps,
        )[0]

    def reduce_first(self, mine, far, deps, micros=20):
        block = mine.shape[1:]
        four = (4, 4) + block
        view = pl.BlockSpec((1, 4) + block, lambda s: (s, 0, 0, 0))
        one = lambda pick: pl.BlockSpec((1,) + block, lambda s: (pick(s), 0, 0))
        each = (one(lambda s: s), sds((4,) + block, BRAIN))
        return call(
            reduce_first_kernel, (4,),
            [(smem(), self.info), (view, mine.reshape(four)), (view, far.reshape(four))],
            [
                (one(lambda s: jnp.minimum(s, 1)), sds((2,) + block, BRAIN)),
                (one(lambda s: jnp.maximum(s - 2, 0)), sds((2,) + block, BRAIN)),
                each, each, each,
            ],
            micros=micros, deps=deps,
        )

    def reduce_second(self, near_x, near_y, to_y, to_x, deps):
        from_y, from_x = self.swap(to_y, 2), self.swap(to_x, 1)
        block = near_x.shape[1:]
        one = lambda pick: pl.BlockSpec((1,) + block, lambda s: (pick(s), 0, 0))
        each = one(lambda s: s)
        return call(
            reduce_second_kernel, (4,),
            [
                (each, near_x), (each, near_y), (one(lambda s: jnp.minimum(s, 1)), from_y),
                (one(lambda s: jnp.maximum(s - 2, 0)), from_x),
            ],
            [(each, sds(near_x.shape, BRAIN))] * 2, micros=20, deps=deps,
        )

    def reduce_third(self, own, near_x, near_y, deps):
        from_x, from_y = self.swap(near_x, 1), self.swap(near_y, 2)
        block = own.shape[1:]
        return call(
            reduce_third_kernel, (1,),
            [(smem(), self.info)] + [(whole(v.shape), v) for v in (own, from_x, from_y)],
            [(whole(block), sds(block, BRAIN))] * 4,
            micros=20, deps=deps,
        )

    def reduce_fourth(self, first, second, others, deps):
        come = self.swap(others, 8)
        inputs = [(whole(v.shape), v) for v in (first, second, come)]
        outs = [(whole(first.shape), sds(first.shape, kind)) for kind in (FLOAT, BRAIN)]
        return call(reduce_fourth_kernel, (1,), inputs, outs, micros=20, deps=deps)

    def reduce_end(self, first, second):
        return first + self.swap(second, 4).astype(FLOAT)

    def reduce_direct(self, first, second, third, fourth, shapes, kernel=final_kernel, deps=()):
        pieces = [first, self.swap(second, 4), self.swap(third, 8), self.swap(fourth, 12)]
        inputs = [(whole(v.shape), v) for v in pieces]
        return call(kernel, (1,), inputs, [(whole(n), sds(n, FLOAT)) for n in shapes], deps=deps)

    def owner_rows(self, value):
        rows = value.shape[0] // 2
        mine = lax.dynamic_slice_in_dim(value, self.core * rows, rows, 0)
        theirs = lax.dynamic_slice_in_dim(value, (1 - self.core) * rows, rows, 0)
        return self.in_order(mine, core_swap(theirs), 1)


AXES = ("clip", "frame")


def body(
    clips, cores, clip_tokens, clip_class, output_grad, class_grad, clip_count,
    time_qkv, time_proj, time_vec, space_qkv, space_proj, space_vec, mlp_up, mlp_down, mlp_vec, mlp_bias,
):
    _, own, places_here, width = clip_tokens.shape
    rows = -(-(places_here + 1) // 16) * 16
    frames = own * cores
    wide = mlp_up.shape[1]
    cut = width // BLOCKS
    core = lax.axis_index("frame")
    place = lax.axis_index("clip")
    shard = place * cores + core
    leader = (core == 0).astype(jnp.int32)
    alive = (jnp.arange(1, dtype=jnp.int32) < clip_count[0]).astype(FLOAT)
    is_near = clips == 16 and cores == 2
    slot = core if is_near else core * 0
    info = jnp.stack([slot, leader, place // 4, place % 4, shard]).astype(jnp.int32)
    near = Near(clips, info) if is_near else None
    my_slot = info[0:1]
    far_slot = 1 - my_slot

    class_block = jnp.broadcast_to(clip_class[0][None, None], (own, 1, width))
    blank = jnp.zeros((own, rows - places_here - 1, width), BRAIN)
    tokens = jnp.concatenate([clip_tokens[0], class_block, blank], axis=1)
    last = (jnp.arange(own) == own - 1)[:, None, None]
    class_rows = jnp.where(last, class_grad[0][None, None], jnp.zeros((), BRAIN))
    grads = jnp.concatenate([output_grad[0], class_rows, blank], axis=1)

    bias_rows = wide // width
    zeros = jnp.zeros((8, width), FLOAT)
    flat = lambda v: v.reshape((own * rows,) + v.shape[2:])

    if near is not None:
        packed = (
            time_qkv, space_qkv, space_proj, time_proj, mlp_up, time_vec, space_vec, mlp_vec,
            mlp_bias.reshape(-1, bias_rows).T,
        )
        line = sds((time_qkv.shape[0], 6 * width + LANES), BRAIN)
        send, keep = call(
            pack_kernel, (1,), [(smem(), info)] + [(whole(v.shape), v) for v in packed],
            [(whole(line.shape), line), (whole(line.shape), line)],
        )
        shapes = [(cut, 3 * width // 2 + LANES), (cut, 5 * width // 2), (4 * cut, width)]
        time_own, space_own, mlp_own = call(
            join_kernel, (1,),
            [(smem(), info)] + [(whole(v.shape), v) for v in (keep, core_swap(send), mlp_down)],
            [(whole(shape), sds(shape, BRAIN)) for shape in shapes],
        )
        join = lambda two: tuple(h.reshape(width, h.shape[-1]) for h in two)
        time_line = near.depth_direct(time_own, [])
        far_tokens = core_swap(gate(tokens, [time_own]))
        space_own = gate(space_own, [time_line])
        space_line = near.depth_direct(space_own, [])
        time_mine = near.diagonal_step(time_line, near.plane_step(time_line, []), [grads, far_tokens, space_line])
        space_line = gate(space_line, [time_mine])
        time_far = core_swap(time_mine)
        time_w = join((time_mine, time_far))
        vec_block = pl.BlockSpec((width, LANES), lambda s: (0, time_w[0].shape[1] // LANES - 1))
        vectors = call(
            turn_kernel, (1,), [(vec_block, time_w[0])], [(whole((LANES, width)), sds((LANES, width), FLOAT))],
            deps=[space_line],
        )[0]
        n_vec = time_vec.shape[0] + space_vec.shape[0] + mlp_vec.shape[0]
        bias = vectors[n_vec : n_vec + bias_rows].T.reshape(bias_rows, width)
        mlp_own = gate(mlp_own, [time_mine])
        mix_deps = [space_line, mlp_own]
    else:
        everywhere = lax.all_gather(tokens, "frame", axis=0, tiled=True)
        far_tokens = jnp.roll(everywhere, -core * own, axis=0)[own:]
        vec_shard = jnp.concatenate([time_vec, space_vec, mlp_vec], axis=0)
        blank_rows = jnp.zeros((16 - vec_shard.shape[0], width), FLOAT)
        space_shard = jnp.concatenate([space_qkv, space_proj, time_proj], axis=1)
        vectors = lax.all_gather(vec_shard, AXES, axis=1, tiled=True).astype(FLOAT)
        bias = lax.all_gather(mlp_bias, AXES, axis=0, tiled=True).astype(FLOAT).reshape(bias_rows, width)
        vectors = jnp.concatenate([vectors, blank_rows], axis=0)

        def halves(value):
            full = lax.all_gather(value, AXES, axis=0, tiled=True)
            half = full.shape[1] // 2
            return full[:, :half], full[:, half:]

        time_w, space_w = halves(time_qkv), halves(space_shard)
        up = lax.all_gather(mlp_up, AXES, axis=0, tiled=True).reshape(BLOCKS, cut, 2, 2, width)
        up = jnp.transpose(up, (2, 0, 3, 1, 4)).reshape(2, BLOCKS, 2 * cut, width)
        down = lax.all_gather(mlp_down, AXES, axis=0, tiled=True).reshape(BLOCKS, 2, 2 * cut, width)
        mlp_w = tuple(
            (jnp.concatenate([up[n], down[:, n]], axis=1).reshape(4, BLOCKS // 4, 4 * cut, width),) for n in (0, 1)
        )
        mix_deps = []

    frame_shape = (own, rows, width)
    out_shape = (own, places_here, width)
    all_shape = (frames, rows, width)
    heads = width // HEAD_DIM
    prob_shape = (own, frames, rows, LANES)
    sprob_shape = (own, heads, rows, rows)
    mixed_shape = (own, rows, 3 * width)
    hidden_shape = (own, rows, wide)
    sum_out = (whole((8, width)), sds((8, width), FLOAT))
    row_bytes = own * rows * width
    square = 2 * own * rows * width * width
    group = 2 if own % 2 == 0 else 1
    frames_in = lambda array, first=0: (per_frame(array.shape, first, group), array)
    low_out = lambda shape, first=0: (per_frame(shape, first, group), sds(shape, BRAIN))
    wide_out = lambda shape, first=0: (per_frame(shape, first, group), sds(shape, FLOAT))
    vec_in = (whole(vectors.shape), vectors)
    pair = lambda two: [(hbm(), two[0]), (hbm(), two[1])]
    time_held = [pltpu.VMEM((width, 3 * width), BRAIN), pltpu.SemaphoreType.DMA((2,))]
    space_held = [pltpu.VMEM((width, 5 * width), BRAIN), pltpu.SemaphoreType.DMA((2,))]
    mlp_held = [
        pltpu.VMEM((wide // width, 4, BLOCKS // 4, cut, width), BRAIN),
        pltpu.VMEM((4, BLOCKS // 4, 2, 2 * cut, width), BRAIN),
        pltpu.SemaphoreType.DMA((2, 15)),
    ]

    own_map = pl.BlockSpec((group, rows, width), lambda s: (jnp.minimum(s, own // group - 1), 0, 0))
    far_map = pl.BlockSpec((group, rows, width), lambda s: (jnp.maximum(s - own // group, 0), 0, 0))
    queries, key_rows, value_rows, time_low = call(
        functools.partial(time_mix_kernel, own // group), (frames // group,),
        [(smem(), info), (own_map, tokens), (far_map, far_tokens), vec_in] + pair(time_w),
        [(own_map, sds(frame_shape, BRAIN)), low_out(all_shape), low_out(all_shape), (own_map, sds(frame_shape, BRAIN))],
        time_held, micros=1, deps=mix_deps,
    )

    if near is not None:
        mlp_line = near.depth_in_order(mlp_own, [queries])
        space_mine = near.diagonal_step(space_line, near.plane_step(space_line, [queries]), [mlp_line])
        space_w = join((space_mine, core_swap(space_mine)))
        mlp_line = gate(mlp_line, [space_mine])

    parts = [(0, own)]
    deps = [] if near is None else [mlp_line]
    kept, class_own = (), zeros
    for first, count in parts:
        outs = call(
            functools.partial(attention_kernel, places_here), (count // group,),
            [
                (smem(), info), frames_in(tokens, first), vec_in, frames_in(queries, first),
                (whole(all_shape), key_rows), (whole(all_shape), value_rows), (whole((8, width)), class_own),
            ]
            + pair(space_w),
            [
                low_out(prob_shape, first), low_out(frame_shape, first), wide_out(frame_shape, first),
                low_out(frame_shape, first), low_out(mixed_shape, first), low_out(sprob_shape, first),
                low_out(frame_shape, first), wide_out(frame_shape, first), sum_out,
            ],
            space_held, micros=27 * count / own, deps=deps, previous=kept,
        )
        kept, class_own = tuple(outs[:-1]), outs[-1]
        if near is not None and first == 0:
            mlp_planes = near.plane_step(mlp_line, [class_own])
            deps = list(mlp_planes[2:])
    time_prob, time_att, after, space_low, space_mixed, space_prob, space_att, places = kept

    if near is not None:
        rx, ry, sx, sy = mlp_planes
        mlp_first = tuple(gate(v, [sx, sy]) for v in (mlp_line, rx, ry))
        mlp_last = (near.swap(sx, 2), near.swap(sy, 1))
        mlp_w = (mlp_first + mlp_last, tuple(core_swap(v) for v in mlp_first) + tuple(core_swap(v) for v in mlp_last))
        class_far = core_swap(class_own)
    else:
        class_far = lax.psum(class_own, "frame") - class_own
    class_row = jnp.broadcast_to(clip_class.astype(FLOAT), (8, width))
    small = whole((8, width))
    result, class_result, mlp_low, hidden, feed_grad, before_grad, rows_grad, mlp_sums = call(
        functools.partial(mlp_kernel, places_here, frames, len(mlp_w[0])), (own // group,),
        [
            (smem(), info), (smem(), alive), frames_in(places), frames_in(grads),
            (small, class_row), (small, class_own), (small, class_far), vec_in, (whole(bias.shape), bias),
        ]
        + [(hbm(), v) for v in mlp_w[0] + mlp_w[1]],
        [
            low_out(out_shape), sum_out, low_out(frame_shape), low_out(hidden_shape), low_out(frame_shape),
            low_out(hidden_shape), wide_out(frame_shape), sum_out,
        ],
        [pltpu.VMEM((wide // width, group * rows, width), FLOAT)] + mlp_held,
        micros=25,
    )

    mlp_mine, mlp_far = mlp_outer(my_slot, flat(mlp_low), flat(before_grad), flat(hidden), flat(feed_grad))
    class_block_at = places_here // 16
    class_spec = pl.BlockSpec((1, 16, width), lambda s: (own - 1, class_block_at, 0))

    def space_back(first, count, sums, deps, previous):
        return call(
            functools.partial(space_back_kernel, places_here, frames), (count // group,),
            [
                (smem(), info), frames_in(rows_grad, first), (class_spec, rows_grad), frames_in(after, first),
                frames_in(space_mixed, first), frames_in(space_prob, first), frames_in(space_att, first),
                vec_in, (small, sums),
            ]
            + pair(space_w),
            [
                low_out(frame_shape, first), low_out(mixed_shape, first), wide_out(frame_shape, first),
                low_out(frame_shape, first), low_out(frame_shape, first), sum_out,
            ],
            space_held, micros=30 * count / own, deps=deps, previous=previous,
        )

    half = own // 2
    if near is not None:
        outs = space_back(0, half, zeros, [mlp_far], ())
        mlp_a, mlp_b, mlp_x, mlp_y, mlp_own = near.reduce_first(mlp_mine, core_swap(mlp_far), [outs[0]])
        outs = space_back(half, own - half, outs[-1], [mlp_a, mlp_b], tuple(outs[:-1]))
        mlp_x, mlp_y = near.reduce_second(mlp_x, mlp_y, mlp_a, mlp_b, [outs[0]])
        time_deps = [mlp_x, mlp_y]
    else:
        outs = space_back(0, own, zeros, [], ())
        time_deps = []
    branch_grad, space_mixed_grad, after_grad, time_grad, time_att_grad, space_sums = outs

    space_mine, space_far = space_outer(
        my_slot, *[flat(v) for v in (space_low, space_mixed_grad, space_att, branch_grad, time_att, time_grad)],
        deps=time_deps,
    )
    time_deps = time_deps + [space_far]
    far_frames = frames - own
    lanes_of = lambda shape: pl.BlockSpec(shape[:-1] + (2 * LANES,), lambda s: (0,) * (len(shape) - 1) + (s,))
    lanes_in = lambda v: (lanes_of(v.shape), v)
    q_grad, own_grad, far_grad = call(
        time_back_kernel, (width // LANES // 2,),
        [
            lanes_in(queries), lanes_in(key_rows), lanes_in(value_rows), (whole(prob_shape), time_prob),
            lanes_in(time_att_grad),
        ],
        [
            (lanes_of(shape), sds(shape, BRAIN))
            for shape in (frame_shape, (2,) + frame_shape, (2, far_frames, rows, width))
        ],
        micros=19, deps=time_deps,
    )
    if near is not None:
        from_far = core_swap(far_grad)
        mlp_first, mlp_second, *mlp_others = near.reduce_third(mlp_own, mlp_x, mlp_y, [q_grad])
        space_a, space_b, space_x, space_y, space_own = near.reduce_first(space_mine, core_swap(space_far), [mlp_second])
        mixed_deps = [space_own]
    else:
        mixed_deps = []
        padded = jnp.concatenate([jnp.zeros_like(own_grad), far_grad], axis=1)
        padded = jnp.roll(padded, core * own, axis=1)
        from_far = lax.psum_scatter(padded, "frame", scatter_dimension=1, tiled=True)
    pair_in = lambda v: (pl.BlockSpec((2, group, rows, width), lambda s: (0, s, 0, 0)), v)
    time_mixed_grad = call(
        mixed_grad_kernel, (own // group,), [frames_in(q_grad), pair_in(own_grad), pair_in(from_far)],
        [low_out(mixed_shape)], micros=3, deps=mixed_deps,
    )[0]
    outer = (flat(time_low), flat(time_mixed_grad))

    back_deps = []
    if near is not None:
        space_x, space_y = near.reduce_second(space_x, space_y, space_a, space_b, [time_mixed_grad])
        back_deps = [mlp_second, space_x, space_y]
    token_grad, time_sums = call(
        time_mix_back_kernel, (own // group,),
        [(smem(), info), frames_in(tokens), vec_in, frames_in(time_mixed_grad), frames_in(after_grad)]
        + pair(time_w),
        [wide_out(out_shape), sum_out],
        time_held, micros=4, deps=back_deps,
    )
    bias_grad = mlp_sums[3 : 3 + bias_rows].reshape(width, bias_rows)
    n_sums = 13
    sums = call(
        sums_kernel, (1,), [(small, time_sums), (small, space_sums), (small, mlp_sums), (whole(bias_grad.shape), bias_grad)],
        [(whole((width, LANES)), sds((width, LANES), FLOAT))], [pltpu.VMEM((LANES, width), FLOAT)],
    )[0]

    if near is not None:
        up_rows, grad_mlp_down = near.reduce_direct(
            mlp_first, mlp_second, *mlp_others, [(cut, 2 * width), (2 * cut, width)], final_mlp_kernel, [token_grad]
        )
        space_parts = near.reduce_third(space_own, space_x, space_y, [up_rows])
        time_mine, time_far = time_outer(my_slot, *outer, sums, deps=[space_parts[1]])
        time_a, time_b, time_x, time_y, time_own = near.reduce_first(time_mine, core_swap(time_far), [])
        time_x, time_y = near.reduce_second(time_x, time_y, time_a, time_b, [])
        time_parts = near.reduce_third(time_own, time_x, time_y, [])
        half = cut // 2
        space_grads = near.reduce_direct(*space_parts, [(half, 3 * width), (half, width), (half, width)])
        vec_shapes = [(v.shape[0], half) for v in (time_vec, space_vec, mlp_vec)]
        grad_time, grad_time_vec, grad_space_vec, grad_mlp_vec, bias_rows_grad = near.reduce_direct(
            *time_parts, [(half, 3 * width)] + vec_shapes + [(half, bias_rows)], final_time_kernel
        )
        grad_mlp_bias = bias_rows_grad.reshape(-1)
        grad_mlp_up = near.owner_rows(up_rows)
        class_total = space_sums[6:7] + core_swap(space_sums)[6:7]
    else:
        send = lambda v: lax.psum_scatter(v, AXES, scatter_dimension=0, tiled=True).astype(FLOAT)
        spread = lambda mine, far: jnp.stack([mine, far], axis=1).reshape(width, mine.shape[2])
        time_mine, time_far = time_outer(my_slot, *outer, sums)
        up = jnp.stack([v[:, : 2 * cut].reshape(BLOCKS, 2, cut, width) for v in (mlp_mine, mlp_far)])
        grad_mlp_up = send(jnp.transpose(up, (1, 3, 0, 2, 4)).reshape(width, wide))
        grad_mlp_down = send(jnp.stack([v[:, 2 * cut :] for v in (mlp_mine, mlp_far)], axis=1).reshape(wide, width))
        grad_space = send(spread(space_mine, space_far))
        space_grads = (grad_space[:, : 3 * width], grad_space[:, 3 * width : 4 * width], grad_space[:, 4 * width :])
        grad_time = send(spread(time_mine, time_far)[:, : 3 * width])
        class_total = lax.psum(space_sums[6:7], "frame")
        step = width // (clips * cores)
        sums = lax.dynamic_slice_in_dim(lax.psum(sums, AXES), shard * step, step, 0)
        lines = sums.T
        grad_time_vec, grad_space_vec, grad_mlp_vec = lines[:5], lines[5:10], lines[10:13]
        grad_mlp_bias = sums[:, n_sums : n_sums + bias_rows].reshape(-1)
    class_in_grad = rows_grad[own - 1, places_here][None] + class_total
    return (
        result[None],
        class_result[places_here % 8][None].astype(BRAIN),
        token_grad[None],
        class_in_grad,
        grad_time,
        space_grads[2],
        grad_time_vec,
        space_grads[0],
        space_grads[1],
        grad_space_vec,
        grad_mlp_up,
        grad_mlp_down,
        grad_mlp_vec,
        grad_mlp_bias,
    )


def solution(mesh):
    both = ("clip", "frame")
    rows = P(both, None)
    columns = P(None, both)
    weights = (rows, rows, columns, rows, rows, columns, rows, rows, columns, P(both))
    block = P("clip", "frame", None, None)
    classes = P("clip", None)
    return jax.shard_map(
        functools.partial(body, mesh.shape["clip"], mesh.shape["frame"]),
        mesh=mesh,
        in_specs=(block, classes, block, classes, P("clip")) + weights,
        out_specs=(block, classes, block, classes) + weights,
        check_vma=False,
    )
```

```python
import functools

import jax
import jax.numpy as jnp
from jax import lax
from jax.experimental import pallas as pl
from jax.experimental.pallas import tpu as pltpu
from jax.sharding import PartitionSpec as P

HEAD_DIM = 64
EPSILON = 1e-06
FLOAT = jnp.float32
BRAIN = jnp.bfloat16
LANES = 128
BLOCKS = 16
RATE = 1e9
VMEM_BYTES = 63 * 1024 * 1024


def nn(left, right):
    return lax.dot_general(left, right, (((1,), (0,)), ((), ())), preferred_element_type=FLOAT)


def nt(left, right):
    return lax.dot_general(left, right, (((1,), (1,)), ((), ())), preferred_element_type=FLOAT)


def tn(left, right):
    return lax.dot_general(left, right, (((0,), (0,)), ((), ())), preferred_element_type=FLOAT)


def unit_of(values):
    average = jnp.mean(values, axis=-1, keepdims=True)
    centred = values - average
    spread = jnp.mean(centred * centred, axis=-1, keepdims=True)
    inverse = lax.rsqrt(spread + EPSILON)
    return centred * inverse, inverse


def norm_back(unit, inverse, gain, upstream):
    scaled = upstream * gain
    inner = jnp.mean(scaled, axis=-1, keepdims=True)
    along = jnp.mean(scaled * unit, axis=-1, keepdims=True)
    return inverse * (scaled - inner - unit * along)


def column_sum(values):
    return jnp.sum(values, axis=0, keepdims=True)


def row_index(shape):
    return lax.broadcasted_iota(jnp.int32, shape, 0)


def head_map(width, first=0):
    lane = lax.broadcasted_iota(jnp.int32, (width, LANES), 0) // HEAD_DIM + first
    head = lax.broadcasted_iota(jnp.int32, (width, LANES), 1)
    return (lane == head).astype(FLOAT).astype(BRAIN)


def head_spread(width, first=0):
    head = lax.broadcasted_iota(jnp.int32, (LANES, width), 0)
    lane = lax.broadcasted_iota(jnp.int32, (LANES, width), 1) // HEAD_DIM + first
    return (lane == head).astype(FLOAT).astype(BRAIN)


def column_copies(core, mine, other, held, sems):
    half = held.shape[1] // 2
    copies = []
    for n, (source, slot) in enumerate(((mine, core), (other, 1 - core))):
        target = held.at[:, pl.ds(pl.multiple_of(slot * half, LANES), half)]
        copies.append(pltpu.make_async_copy(source.at[:, :half], target, sems.at[n]))
    return copies


def mlp_copies(core, plane, mine, other, up, down, sems):
    cut = up.shape[3]
    ups, downs = [], []
    for k, (sources, slot) in enumerate(((mine, core), (other, 1 - core))):
        for n, source in enumerate(sources):
            if len(sources) == 1:
                at, tail = (), (slice(None),)
            else:
                at, tail = ((slice(None), slice(0, 2), slice(2, 4))[max(n - 2, 0)], plane ^ min(n, 3)), ()
            rows = lambda low, high: source.at[(slice(None),) + tail + (slice(low, high),)]
            for t in (0, 1):
                part = up.at[(2 * slot + t,) + at]
                ups.append(pltpu.make_async_copy(rows(t * cut, (t + 1) * cut), part, sems.at[k, 3 * n + t]))
            part = down.at[at + (slot,)] if at else down.at[:, :, slot]
            downs.append(pltpu.make_async_copy(rows(2 * cut, 4 * cut), part, sems.at[k, 3 * n + 2]))
    return ups, downs


def start_first(copies):
    @pl.when(pl.program_id(0) == 0)
    def _():
        for copy in copies:
            copy.start()


def wait_first(copies):
    @pl.when(pl.program_id(0) == 0)
    def _():
        for copy in copies:
            copy.wait()


def merged(ref):
    return ref[...].reshape(ref.shape[0] * ref.shape[1], ref.shape[2])


def store(ref, value):
    ref[...] = value.astype(ref.dtype).reshape(ref.shape)


def marks(count, rows, low, high):
    index = row_index((count * rows, 1))
    found = (index >= low) & (index < high)
    for n in range(1, count):
        found = found | ((index >= n * rows + low) & (index < n * rows + high))
    return found


def time_mix_kernel(own_steps, info, tokens, far_tokens, vectors, w_mine, w_other, q_out, k_out, v_out, low_out, held, sems):
    step = pl.program_id(0)
    width = tokens.shape[-1]

    copies = column_copies(info[0], w_mine, w_other, held, sems)
    start_first(copies)
    unit, _ = unit_of(jnp.where(step < own_steps, merged(tokens).astype(FLOAT), merged(far_tokens).astype(FLOAT)))
    low = (unit * vectors[0:1] + vectors[1:2]).astype(BRAIN)
    wait_first(copies)
    store(k_out, nn(low, held[:, width : 2 * width]))
    store(v_out, nn(low, held[:, 2 * width :]) + vectors[3:4])

    @pl.when(step < own_steps)
    def _():
        queries = (nn(low, held[:, :width]) + vectors[2:3]).astype(BRAIN)
        store(q_out, queries * jnp.asarray(HEAD_DIM ** (-0.5), BRAIN))
        store(low_out, low)


def tree_sum(values):
    values = list(values)
    while len(values) > 1:
        values = [a + b for a, b in zip(values[::2], values[1::2])] + values[len(values) & ~1 :]
    return values[0]


def attention_kernel(
    places_here, info, tokens, vectors, q_in, k_in, v_in, begin, sw_mine, sw_other,
    prob_out, att_out, after_out, low_out, mixed_out, sprob_out, satt_out, places_out, class_out,
    held, sems,
):
    step = pl.program_id(0)
    frames = k_in.shape[0]
    count, rows, width = tokens.shape
    core = info[0]

    copies = column_copies(core, sw_mine, sw_other, held, sems)
    start_first(copies)
    mapping = head_map(width)
    spread = head_spread(width)
    for n in range(count):
        queries = q_in[n]
        scores = [nn(queries * k_in[g], mapping) for g in range(frames)]
        top = functools.reduce(jnp.maximum, scores)
        powers = [jnp.exp(s - top) for s in scores]
        scale = 1.0 / sum(powers)
        parts = []
        for g in range(frames):
            prob = (powers[g] * scale).astype(BRAIN)
            prob_out[n, g] = prob
            parts.append(nn(prob, spread).astype(BRAIN) * v_in[g])
        att_out[n] = tree_sum(parts)
    wait_first(copies)
    attended = merged(att_out)
    place = marks(count, rows, 0, places_here)
    base = merged(tokens).astype(FLOAT)
    after = jnp.where(place, base + (nn(attended, held[:, 4 * width :]) + vectors[4:5]), base)
    store(after_out, after)
    unit, _ = unit_of(after)
    low = (unit * vectors[5:6] + vectors[6:7]).astype(BRAIN)
    store(low_out, low)
    shape = (count, rows, width)
    queries = (nn(low, held[:, :width]) + vectors[7:8]).astype(BRAIN) * jnp.asarray(HEAD_DIM ** (-0.5), BRAIN)
    mixed_out[:, :, :width] = queries.reshape(shape)
    mixed_out[:, :, width : 2 * width] = nn(low, held[:, width : 2 * width]).astype(BRAIN).reshape(shape)
    mixed_out[:, :, 2 * width :] = (
        (nn(low, held[:, 2 * width : 3 * width]) + vectors[8:9]).astype(BRAIN).reshape(shape)
    )
    lane = lax.broadcasted_iota(jnp.int32, (1, LANES), 1)
    masks = [(lane // HEAD_DIM == e).astype(FLOAT).astype(BRAIN) for e in (0, 1)]
    key_ok = row_index((rows, 1)) <= places_here
    for n in range(count):
        for pair in range(width // LANES):
            at = pair * LANES
            q2 = mixed_out[n, :, at : at + LANES]
            k2 = mixed_out[n, :, width + at : width + at + LANES]
            v2 = mixed_out[n, :, 2 * width + at : 2 * width + at + LANES]
            result = []
            for e in (0, 1):
                logits = jnp.where(key_ok, nt(k2, q2 * masks[e]), -1e30)
                power = jnp.exp(logits - jnp.max(logits, axis=0, keepdims=True))
                prob = (power * (1.0 / jnp.sum(power, axis=0, keepdims=True))).astype(BRAIN)
                sprob_out[n, 2 * pair + e] = prob
                result.append(tn(prob, v2))
            satt_out[n, :, at : at + LANES] = jnp.where(lane < HEAD_DIM, result[0], result[1]).astype(BRAIN)
    spatial = nn(merged(satt_out), held[:, 3 * width : 4 * width]) + vectors[9:10]
    store(places_out, jnp.where(place, after, 0.0) + spatial)

    @pl.when(step == 0)
    def _():
        class_out[...] = begin[...]

    class_row = column_sum(jnp.where(marks(count, rows, places_here, places_here + 1), spatial, 0.0))
    class_out[0:1] = class_out[0:1] + class_row


def gelu_parts(values):
    half = 0.5 + 0.5 * lax.erf(values * (0.5 ** 0.5))
    density = jnp.exp(values * values * (-0.5)) * (0.5 / 3.141592653589793) ** 0.5
    return values * half, half + values * density


def mlp_kernel(
    places_here, all_frames, pieces, info, alive, places, grads, class_row, class_own, class_far, vectors, bias,
    *others,
):
    mine, other, others = others[:pieces], others[pieces : 2 * pieces], others[2 * pieces :]
    out, class_out, low_out, hidden_out, feed_out, before_out, rows_out, sums, slopes, up, down, sems = others
    step = pl.program_id(0)
    count, rows, width = places.shape
    core = info[0]

    ups, downs = mlp_copies(core, info[3], mine, other, up, down, sems)
    start_first(ups + downs)

    @pl.when(step == 0)
    def _():
        sums[...] = jnp.zeros_like(sums)

    class_mid = class_row[0:1] + (class_own[0:1] + class_far[0:1]) * all_frames ** (-0.5)
    last = (count - 1) * rows + places_here
    is_class = (row_index((count * rows, 1)) == last) & (step == pl.num_programs(0) - 1)
    kept = jnp.logical_not(marks(count, rows, places_here, places_here + 1) & (info[1] == 0))
    values = jnp.where(is_class, class_mid, merged(places))
    unit, inverse = unit_of(values)
    low = (unit * vectors[10:11] + vectors[11:12]).astype(BRAIN)
    store(low_out, low)
    feed = jnp.zeros((count * rows, width), FLOAT)
    chunks = hidden_out.shape[-1] // width
    wait_first(ups)
    for j in range(chunks):
        before = nn(low, up[j].reshape(width, width)) + bias[j : j + 1]
        hidden, slope = gelu_parts(before)
        hidden = hidden.astype(BRAIN)
        hidden_out[:, :, j * width : (j + 1) * width] = hidden.reshape(count, rows, width)
        slopes[j] = slope
        if j == 0:
            wait_first(downs)
        feed = feed + nn(hidden, down[j].reshape(width, width))
    result = ((values + (feed + vectors[12:13])) * alive[0]).reshape(count, rows, width)
    out[...] = result[:, :places_here].astype(BRAIN)
    class_out[...] = result[count - 1, places_here - places_here % 8 : places_here - places_here % 8 + 8]

    row_grad = merged(grads).astype(FLOAT) * alive[0]
    feed_grad = row_grad.astype(BRAIN)
    feed_kept = jnp.where(kept, row_grad, 0.0).astype(BRAIN)
    store(feed_out, feed_kept)
    sums[2:3] = sums[2:3] + column_sum(feed_kept.astype(FLOAT))
    upstream = jnp.zeros((count * rows, width), FLOAT)
    for j in range(chunks):
        hidden_grad = nt(feed_grad, down[j].reshape(width, width))
        before_grad = (hidden_grad * slopes[j]).astype(BRAIN)
        before_kept = jnp.where(kept, before_grad.astype(FLOAT), 0.0)
        before_out[:, :, j * width : (j + 1) * width] = before_kept.astype(BRAIN).reshape(count, rows, width)
        sums[3 + j : 4 + j] = sums[3 + j : 4 + j] + column_sum(before_kept)
        upstream = upstream + nt(before_grad, up[j].reshape(width, width))
    store(rows_out, row_grad + norm_back(unit, inverse, vectors[10:11], upstream))
    upstream = jnp.where(kept, upstream, 0.0)
    sums[0:1] = sums[0:1] + column_sum(upstream * unit)
    sums[1:2] = sums[1:2] + column_sum(upstream)


def space_back_kernel(
    places_here, all_frames, info, rows_grad, class_grad, after, mixed, sprob, satt, vectors, begin,
    sw_mine, sw_other,
    branch_out, mixed_out, after_out, time_out, att_out, sums, held, sems,
):
    step = pl.program_id(0)
    count, rows, width = after.shape
    core = info[0]

    copies = column_copies(core, sw_mine, sw_other, held, sems)
    start_first(copies)

    @pl.when(step == 0)
    def _():
        sums[...] = begin[...]

    place = marks(count, rows, 0, places_here)
    class_at = marks(count, rows, places_here, places_here + 1)
    offset = places_here % 16
    share = class_grad[0, offset : offset + 1] * all_frames ** (-0.5)
    direct = jnp.where(place, merged(rows_grad), 0.0)
    branch = jnp.where(class_at, share, direct).astype(BRAIN)
    store(branch_out, branch)
    sums[4:5] = sums[4:5] + column_sum(branch.astype(FLOAT))
    unit, inverse = unit_of(merged(after))
    wait_first(copies)
    att_grad = nt(branch, held[:, 3 * width : 4 * width]).astype(BRAIN)
    store(att_out, att_grad)
    spread = head_spread(width)
    lane = lax.broadcasted_iota(jnp.int32, (1, LANES), 1)
    masks = [(lane // HEAD_DIM == e).astype(FLOAT).astype(BRAIN) for e in (0, 1)]
    left = lane < HEAD_DIM
    for n in range(count):
        product = att_out[n].astype(FLOAT) * satt[n].astype(FLOAT)
        high = product.astype(BRAIN)
        rowdots = nt(spread, high) + nt(spread, (product - high.astype(FLOAT)).astype(BRAIN))
        for pair in range(width // LANES):
            at = pair * LANES
            a2 = att_out[n, :, at : at + LANES]
            q2 = mixed[n, :, at : at + LANES]
            k2 = mixed[n, :, width + at : width + at + LANES]
            v2 = mixed[n, :, 2 * width + at : 2 * width + at + LANES]
            queries, key_rows, value_rows = [], [], []
            for e in (0, 1):
                head = 2 * pair + e
                prob = sprob[n, head]
                prob_grad = nt(v2, a2 * masks[e])
                score = (prob.astype(FLOAT) * (prob_grad - rowdots[head : head + 1])).astype(BRAIN)
                queries.append(tn(score, k2))
                key_rows.append(nn(score, q2))
                value_rows.append(nn(prob, a2))
            q_grad = (jnp.where(left, queries[0], queries[1]) * HEAD_DIM ** (-0.5)).astype(BRAIN)
            k_grad = jnp.where(left, key_rows[0], key_rows[1]).astype(BRAIN)
            v_grad = jnp.where(left, value_rows[0], value_rows[1]).astype(BRAIN)
            mixed_out[n, :, at : at + LANES] = q_grad
            mixed_out[n, :, width + at : width + at + LANES] = k_grad
            mixed_out[n, :, 2 * width + at : 2 * width + at + LANES] = v_grad
    mixed_grad = merged(mixed_out)
    sums[2:3] = sums[2:3] + column_sum(mixed_grad[:, :width].astype(FLOAT))
    sums[3:4] = sums[3:4] + column_sum(mixed_grad[:, 2 * width :].astype(FLOAT))
    upstream = nt(mixed_grad, held[:, : 3 * width])
    inner = norm_back(unit, inverse, vectors[5:6], upstream)
    sums[0:1] = sums[0:1] + column_sum(upstream * unit)
    sums[1:2] = sums[1:2] + column_sum(upstream)
    sums[6:7] = sums[6:7] + column_sum(jnp.where(class_at, inner, 0.0))
    after_grad = jnp.where(place, direct + inner, 0.0)
    store(after_out, after_grad)
    low = after_grad.astype(BRAIN)
    store(time_out, low)
    sums[5:6] = sums[5:6] + column_sum(low.astype(FLOAT))
    store(att_out, nt(low, held[:, 4 * width :]))


def time_back_kernel(q_in, k_in, v_in, prob_in, att_in, q_out, own_out, far_out):
    own, rows, width = q_in.shape
    frames = k_in.shape[0]
    first = pl.program_id(0) * (width // HEAD_DIM)
    mapping = head_map(width, first)
    spread = head_spread(width, first)
    size = 16

    def chunk(index, carry):
        at = pl.ds(pl.multiple_of(index * size, size), size)
        values = [v_in[g, at] for g in range(frames)]
        att = [att_in[f, at] for f in range(own)]
        products = jnp.concatenate([att[f] * values[g] for f in range(own) for g in range(frames)], axis=0)
        prob_grad = nn(products, mapping)
        probs = [prob_in[f, g, at] for f in range(own) for g in range(frames)]
        scores = []
        for f in range(own):
            wide = [probs[f * frames + g].astype(FLOAT) for g in range(frames)]
            weighted = [
                wide[g] * prob_grad[(f * frames + g) * size : (f * frames + g + 1) * size] for g in range(frames)
            ]
            rowdot = sum(weighted)
            scores += [(weighted[g] - wide[g] * rowdot).astype(BRAIN) for g in range(frames)]
        score_wide = nn(jnp.concatenate(scores, axis=0), spread).astype(BRAIN)
        prob_wide = nn(jnp.concatenate(probs, axis=0), spread).astype(BRAIN)

        def part(array, f, g):
            return array[(f * frames + g) * size : (f * frames + g + 1) * size]

        keys = [k_in[g, at] for g in range(frames)]
        for f in range(own):
            total = tree_sum(part(score_wide, f, g) * keys[g] for g in range(frames))
            q_out[f, at] = total * jnp.asarray(HEAD_DIM ** (-0.5), BRAIN)
        queries = [q_in[f, at] for f in range(own)]
        for g in range(frames):
            key_grad = tree_sum(part(score_wide, f, g) * queries[f] for f in range(own))
            value_grad = tree_sum(part(prob_wide, f, g) * att[f] for f in range(own))
            if g < own:
                own_out[0, g, at] = key_grad
                own_out[1, g, at] = value_grad
            else:
                far_out[0, g - own, at] = key_grad
                far_out[1, g - own, at] = value_grad
        return carry

    lax.fori_loop(0, rows // size, chunk, 0, unroll=True)


def time_mix_back_kernel(info, tokens, vectors, mixed, after_grad, w_mine, w_other, token_out, sums, held, sems):
    step = pl.program_id(0)
    width = tokens.shape[-1]

    copies = column_copies(info[0], w_mine, w_other, held, sems)
    start_first(copies)

    @pl.when(step == 0)
    def _():
        sums[...] = jnp.zeros_like(sums)

    mixed_grad = merged(mixed)
    sums[2:3] = sums[2:3] + column_sum(mixed_grad[:, :width].astype(FLOAT))
    sums[3:4] = sums[3:4] + column_sum(mixed_grad[:, 2 * width :].astype(FLOAT))
    unit, inverse = unit_of(merged(tokens).astype(FLOAT))
    wait_first(copies)
    upstream = nt(mixed_grad, held[...])
    result = merged(after_grad) + norm_back(unit, inverse, vectors[0:1], upstream)
    token_out[...] = result.reshape(mixed.shape[:2] + (width,))[:, : token_out.shape[1]]
    sums[0:1] = sums[0:1] + column_sum(upstream * unit)
    sums[1:2] = sums[1:2] + column_sum(upstream)


def mixed_grad_kernel(queries, own, far, out):
    width = queries.shape[2]
    out[:, :, :width] = queries[...]
    out[:, :, width : 2 * width] = (own[0].astype(FLOAT) + far[0].astype(FLOAT)).astype(BRAIN)
    out[:, :, 2 * width :] = (own[1].astype(FLOAT) + far[1].astype(FLOAT)).astype(BRAIN)


def sums_kernel(time_sums, space_sums, mlp_sums, bias, out, lines):
    lines[...] = jnp.zeros_like(lines)
    lines[0:4] = time_sums[0:4]
    lines[4:5] = space_sums[5:6]
    lines[5:10] = space_sums[0:5]
    lines[10:13] = mlp_sums[0:3]
    count = bias.shape[1]
    place = lax.broadcasted_iota(jnp.int32, (count, LANES), 1) == row_index((count, LANES)) + 13
    spread = lax.dot_general(
        bias[...], place.astype(FLOAT), (((1,), (0,)), ((), ())), preferred_element_type=FLOAT,
        precision=lax.Precision.HIGHEST,
    )
    out[...] = lines[...].T + spread


def halves_kernel(left, right, left_out, right_out):
    left_out[...] = left[...]
    right_out[...] = right[...]


def share_rows(info, value, mine, other, at=slice(None)):
    value = value.reshape(mine.shape[0], 2, mine.shape[1], value.shape[-1])
    first = info[0] == 0
    mine[:, :, at] = jnp.where(first, value[:, 0], value[:, 1]).astype(BRAIN)
    other[:, :, at] = jnp.where(first, value[:, 1], value[:, 0]).astype(BRAIN)


def time_outer_kernel(info, left, right, sums, mine, other):
    step = pl.program_id(0)
    width = left.shape[1]

    for n in range(3):

        @pl.when(step == n)
        def _():
            share_rows(info, tn(left[...], right[...]), mine, other, slice(n * width, (n + 1) * width))

    @pl.when(step == 0)
    def _():
        share_rows(info, sums[...], mine, other, slice(3 * width, 3 * width + sums.shape[1]))


def space_outer_kernel(info, low, mixed, att, branch, time_att, time_grad, mine, other):
    step = pl.program_id(0)

    @pl.when(step < 3)
    def _():
        share_rows(info, tn(low[...], mixed[...]), mine, other)

    @pl.when(step == 3)
    def _():
        share_rows(info, tn(att[...], branch[...]), mine, other)

    @pl.when(step == 4)
    def _():
        share_rows(info, tn(time_att[...], time_grad[...]), mine, other)


def mlp_outer_kernel(info, low, before, hidden, feed, mine, other, turned, ups, downs, sems):
    step = pl.program_id(0)
    steps = ups.shape[0]
    blocks, cut, width = ups.shape[1:]
    per = downs.shape[2]

    @pl.when(step == 0)
    def _():
        turned[...] = low[...].T

    ups[step] = nn(turned[...], before[...]).astype(BRAIN).reshape(blocks, cut, width)
    value = tn(hidden[...], feed[...]).astype(BRAIN).reshape(per, 2, 2 * cut, width)
    downs[step, 0] = value[:, 0]
    downs[step, 1] = value[:, 1]

    for n in range(steps):
        targets = (mine, other)
        for k, slot in ((0, info[0]), (1, 1 - info[0])):
            up_copy = pltpu.make_async_copy(
                ups.at[n], targets[k].at[:, (n % 2) * cut : (n % 2 + 1) * cut], sems.at[0, n]
            )
            down_copy = pltpu.make_async_copy(
                downs.at[n, slot], targets[k].at[n * per : (n + 1) * per, 2 * cut :], sems.at[1 + k, n]
            )

            @pl.when((step == n) & (slot == n // 2))
            def _():
                up_copy.start()

            @pl.when(step == n)
            def _():
                down_copy.start()

            @pl.when((step == steps - 1) & (slot == n // 2))
            def _():
                up_copy.wait()

            @pl.when(step == steps - 1)
            def _():
                down_copy.wait()


def smem():
    return pl.BlockSpec(memory_space=pltpu.SMEM)


def hbm():
    return pl.BlockSpec(memory_space=pl.ANY)


def whole(shape):
    return pl.BlockSpec(shape, lambda *_: (0,) * len(shape))


def per_frame(shape, first=0, count=1):
    return pl.BlockSpec((count,) + shape[1:], lambda s: (s + first // count,) + (0,) * (len(shape) - 1))


def sds(shape, kind):
    return jax.ShapeDtypeStruct(shape, kind)


def call(kernel, grid, inputs, outputs, scratch=(), micros=2, deps=(), previous=(), prefetch=0):
    count = len(inputs)
    skip = len(previous) + len(deps)

    def inner(*refs):
        kernel(*refs[:count], *refs[count + skip :])

    specs = [spec for spec, _ in inputs[prefetch:]] + [hbm()] * skip
    common = dict(
        name=getattr(kernel, "func", kernel).__name__,
        out_shape=[shape for _, shape in outputs],
        compiler_params=pltpu.CompilerParams(vmem_limit_bytes=VMEM_BYTES),
        input_output_aliases={count + n: n for n in range(len(previous))},
        cost_estimate=pl.CostEstimate(flops=int(micros * RATE), bytes_accessed=1, transcendentals=0),
    )
    places = dict(grid=grid, in_specs=specs, out_specs=[spec for spec, _ in outputs], scratch_shapes=list(scratch))
    if prefetch:
        common["grid_spec"] = pltpu.PrefetchScalarGridSpec(num_scalar_prefetch=prefetch, **places)
    else:
        common.update(places)
    return pl.pallas_call(inner, **common)(*[array for _, array in inputs], *previous, *deps)


def time_outer(slot, left, right, sums, deps=()):
    rows, width = left.shape
    wide = right.shape[1]
    shape = (BLOCKS, width // (2 * BLOCKS), wide + sums.shape[1])
    return call(
        time_outer_kernel, (3,),
        [
            (smem(), slot), (whole(left.shape), left), (pl.BlockSpec((rows, width), lambda s: (0, s)), right),
            (whole(sums.shape), sums),
        ],
        [(whole(shape), sds(shape, BRAIN))] * 2, micros=8, deps=deps,
    )


def space_outer(slot, low, mixed, *others, deps=()):
    rows, width = low.shape
    shape = (BLOCKS, width // (2 * BLOCKS), width)
    moving = pl.BlockSpec((rows, width), lambda s: (0, jnp.minimum(s, 2)))
    return call(
        space_outer_kernel, (5,),
        [(smem(), slot), (whole(low.shape), low), (moving, mixed)] + [(whole(v.shape), v) for v in others],
        [(pl.BlockSpec(shape, lambda s: (0, 0, s)), sds(shape[:2] + (5 * width,), BRAIN))] * 2, micros=12, deps=deps,
    )


def mlp_outer(slot, low, before, hidden, feed, deps=()):
    rows, width = low.shape
    wide = hidden.shape[1]
    cut = width // BLOCKS
    shape = (BLOCKS, 4 * cut, width)
    fixed = pl.BlockSpec((rows, width), lambda s, info: (0, 0))
    moving = pl.BlockSpec((rows, width), lambda s, info: (0, s))
    return call(
        mlp_outer_kernel, (wide // width,),
        [(None, slot), (fixed, low), (moving, before), (moving, hidden), (fixed, feed)],
        [(hbm(), sds(shape, BRAIN))] * 2,
        [
            pltpu.VMEM((width, rows), BRAIN),
            pltpu.VMEM((wide // width, BLOCKS, cut, width), BRAIN),
            pltpu.VMEM((wide // width, 2, BLOCKS * width // wide, 2 * cut, width), BRAIN),
            pltpu.SemaphoreType.DMA((3, wide // width)),
        ],
        micros=21, deps=deps, prefetch=1,
    )


def gate(value, deps):
    return pl.pallas_call(
        lambda source, *refs: None,
        in_specs=[hbm()] * (1 + len(deps)),
        out_specs=hbm(),
        out_shape=sds(value.shape, value.dtype),
        input_output_aliases={0: 0},
    )(value, *deps)


def stack_at_kernel(info, *refs):
    for n, ref in enumerate(refs[:-1]):
        refs[-1][info[2] ^ n] = ref[...]


def stack_kernel(*refs):
    for n, ref in enumerate(refs[:-1]):
        refs[-1][n] = ref[...]


def add_kernel(left, right, out):
    out[...] = left[...] + right[...]


def add_after(left, right, deps):
    inputs = [(whole(left.shape), left), (whole(right.shape), right)]
    return call(add_kernel, (1,), inputs, [(whole(left.shape), sds(left.shape, left.dtype))], deps=deps)[0]


def assemble_kernel(info, o4, rx, ry, ra, rb, out):
    depth = info[2]
    plane = info[3]
    for m in range(4):
        for n in range(4):
            if n < 3:
                value = (o4, rx, ry)[n][m]
            else:
                value = ra[m] if m < 2 else rb[m - 2]
            out[(depth ^ m) * 4 + (plane ^ n)] = value


def pack_kernel(info, time_qkv, space_qkv, space_proj, time_proj, up, time_vec, space_vec, mlp_vec, bias, send, keep):
    width = time_proj.shape[1]
    half = width // 2
    pieces = [time_qkv[:, n * half : (n + 1) * half] for n in range(6)]
    pieces += [space_qkv[:, n * half : (n + 1) * half] for n in range(6)]
    pieces += [space_proj[:, :half], space_proj[:, half:], time_proj[:, :half], time_proj[:, half:]]
    pieces += [up[:, n * half : (n + 1) * half] for n in range(8)]
    first = info[0] == 0
    at = 0
    for begin, count in ((0, 3), (6, 5), (16, 4)):
        for n in range(count):
            low, high = pieces[begin + n], pieces[begin + count + n]
            keep[:, at : at + half] = jnp.where(first, low, high)
            send[:, at : at + half] = jnp.where(first, high, low)
            at += half
    line = 0
    total = jnp.zeros((keep.shape[0], LANES), FLOAT)
    for source in (time_vec, space_vec, mlp_vec, bias):
        count = source.shape[0]
        lane = lax.broadcasted_iota(jnp.int32, (count, LANES), 1)
        chosen = (lane == row_index((count, LANES)) + line).astype(FLOAT)
        total = total + lax.dot_general(
            source[...].astype(FLOAT), chosen, (((0,), (0,)), ((), ())), preferred_element_type=FLOAT
        )
        line += count
    keep[:, at:] = total.astype(BRAIN)
    send[:, at:] = total.astype(BRAIN)


def turn_kernel(source, out):
    out[...] = source[...].astype(FLOAT).T


def join_kernel(info, keep, come, down, time_out, space_out, mlp_out):
    first = info[0] == 0
    width = down.shape[1]
    mine, far = keep[...].astype(FLOAT), come[...].astype(FLOAT)
    both = jnp.concatenate([jnp.where(first, mine, far), jnp.where(first, far, mine)], axis=0).astype(BRAIN)
    cut = both.shape[0]
    end = time_out.shape[1] - LANES
    time_out[:, :end] = both[:, :end]
    time_out[:, end:] = both[:, both.shape[1] - LANES :]
    space_out[...] = both[:, end : end + space_out.shape[1]]
    at = end + space_out.shape[1]
    mlp_out[:cut] = both[:, at : at + width]
    mlp_out[cut : 2 * cut] = both[:, at + width : at + 2 * width]
    mlp_out[2 * cut :] = down[...]


def added(*values):
    return sum(v.astype(FLOAT) for v in values).astype(BRAIN)


def reduce_first_kernel(info, mine, far, to_y, to_x, near_x, near_y, own):
    step = pl.program_id(0)
    plane = info[3]
    own[0] = added(mine[0, plane], far[0, plane])
    near_x[0] = added(mine[0, plane ^ 1], far[0, plane ^ 1])
    near_y[0] = added(mine[0, plane ^ 2], far[0, plane ^ 2])
    diagonal = added(mine[0, plane ^ 3], far[0, plane ^ 3])

    @pl.when(step < 2)
    def _():
        to_y[0] = diagonal

    @pl.when(step >= 2)
    def _():
        to_x[0] = diagonal


def reduce_second_kernel(near_x, near_y, from_y, from_x, out_x, out_y):
    step = pl.program_id(0)

    @pl.when(step < 2)
    def _():
        out_x[0] = added(near_x[0], from_y[0])
        out_y[0] = near_y[0]

    @pl.when(step >= 2)
    def _():
        out_x[0] = near_x[0]
        out_y[0] = added(near_y[0], from_x[0])


def reduce_third_kernel(info, own, from_x, from_y, *outs):
    for m, out in enumerate(outs):
        at = info[2] ^ m
        out[...] = added(own[at], from_x[at], from_y[at])


def final_kernel(first, second, third, fourth, *outs):
    at = 0
    for out in outs:
        part = slice(at, at + out.shape[1])
        out[...] = (first[:, part].astype(FLOAT) + second[:, part].astype(FLOAT)) + (
            third[:, part].astype(FLOAT) + fourth[:, part].astype(FLOAT)
        )
        at += out.shape[1]


def final_mlp_kernel(first, second, third, fourth, up, down):
    cut, width = up.shape[0], down.shape[1]
    total = (first[...].astype(FLOAT) + second[...].astype(FLOAT)) + (
        third[...].astype(FLOAT) + fourth[...].astype(FLOAT)
    )
    up[:, :width] = total[:cut]
    up[:, width:] = total[cut : 2 * cut]
    down[...] = total[2 * cut :]


def exact(left, right, sides):
    return lax.dot_general(
        left, right, ((sides[:1], sides[1:]), ((), ())), preferred_element_type=FLOAT, precision=lax.Precision.HIGHEST
    )


def final_time_kernel(first, second, third, fourth, out, time_vec, space_vec, mlp_vec, bias):
    total = (first[...].astype(FLOAT) + second[...].astype(FLOAT)) + (
        third[...].astype(FLOAT) + fourth[...].astype(FLOAT)
    )
    end = out.shape[1]
    out[...] = total[:, :end]
    sums = total[:, end:]
    rows = sums.shape[0]
    same = row_index((rows, rows)) == lax.broadcasted_iota(jnp.int32, (rows, rows), 1)
    lines = exact(sums, same.astype(FLOAT), (0, 0))
    at = 0
    for ref in (time_vec, space_vec, mlp_vec):
        ref[...] = lines[at : at + ref.shape[0]]
        at += ref.shape[0]
    count = bias.shape[1]
    chosen = row_index((LANES, count)) == lax.broadcasted_iota(jnp.int32, (LANES, count), 1) + at
    bias[...] = exact(sums, chosen.astype(FLOAT), (1, 0))


def reduce_fourth_kernel(first, second, come, first_out, second_out):
    first_out[...] = first[...].astype(FLOAT) + come[0].astype(FLOAT)
    second_out[...] = added(second[...], come[1])


def clip_swap(values, bits, count):
    return lax.ppermute(values, "clip", [(i, i ^ bits) for i in range(count)])


def core_swap(values):
    return lax.ppermute(values, "frame", [(0, 1), (1, 0)])


class Near:
    def __init__(self, clips, info):
        self.clips = clips
        self.info = info
        self.core = lax.axis_index("frame")

    def swap(self, values, bits):
        return clip_swap(values, bits, self.clips)

    def in_order(self, mine, far, axis):
        return jnp.where(
            self.core == 0, jnp.concatenate([mine, far], axis=axis), jnp.concatenate([far, mine], axis=axis)
        )

    def stack(self, pieces, deps):
        shape = (len(pieces),) + pieces[0].shape
        return call(
            stack_kernel, (1,), [(whole(v.shape), v) for v in pieces], [(whole(shape), sds(shape, BRAIN))],
            micros=3, deps=deps,
        )[0]

    def depth_direct(self, own, deps):
        return self.stack([own] + [self.swap(own, 4 * m) for m in (1, 2, 3)], deps)

    def depth_in_order(self, own, deps):
        pieces = [own] + [self.swap(own, 4 * m) for m in (1, 2, 3)]
        shape = (4,) + own.shape
        return call(
            stack_at_kernel, (1,), [(smem(), self.info)] + [(whole(v.shape), v) for v in pieces],
            [(whole(shape), sds(shape, BRAIN))], micros=3, deps=deps,
        )[0]

    def depth_near(self, own, deps):
        return self.stack([own, self.swap(own, 4)], deps)

    def depth_far(self, two, deps):
        come = self.swap(two, 8)
        return self.stack([two[0], two[1], come[0], come[1]], deps)

    def plane_step(self, o4, deps):
        rx = self.swap(o4, 1)
        ry = self.swap(o4, 2)
        half = (2,) + o4.shape[1:]
        first = pl.BlockSpec(half, lambda s: (0, 0, 0))
        second = pl.BlockSpec(half, lambda s: (1, 0, 0))
        sx, sy = call(
            halves_kernel, (1,), [(first, rx), (second, ry)], [(whole(half), sds(half, BRAIN))] * 2, deps=deps
        )
        return rx, ry, sx, sy

    def diagonal_step(self, o4, planes, deps):
        rx, ry, sx, sy = planes
        pieces = (o4, rx, ry, self.swap(sx, 2), self.swap(sy, 1))
        shape = (self.clips,) + o4.shape[1:]
        return call(
            assemble_kernel, (1,), [(smem(), self.info)] + [(whole(v.shape), v) for v in pieces],
            [(whole(shape), sds(shape, BRAIN))], micros=3, deps=deps,
        )[0]

    def reduce_first(self, mine, far, deps, micros=20):
        block = mine.shape[1:]
        four = (4, 4) + block
        view = pl.BlockSpec((1, 4) + block, lambda s: (s, 0, 0, 0))
        one = lambda pick: pl.BlockSpec((1,) + block, lambda s: (pick(s), 0, 0))
        each = (one(lambda s: s), sds((4,) + block, BRAIN))
        return call(
            reduce_first_kernel, (4,),
            [(smem(), self.info), (view, mine.reshape(four)), (view, far.reshape(four))],
            [
                (one(lambda s: jnp.minimum(s, 1)), sds((2,) + block, BRAIN)),
                (one(lambda s: jnp.maximum(s - 2, 0)), sds((2,) + block, BRAIN)),
                each, each, each,
            ],
            micros=micros, deps=deps,
        )

    def reduce_second(self, near_x, near_y, to_y, to_x, deps):
        from_y, from_x = self.swap(to_y, 2), self.swap(to_x, 1)
        block = near_x.shape[1:]
        one = lambda pick: pl.BlockSpec((1,) + block, lambda s: (pick(s), 0, 0))
        each = one(lambda s: s)
        return call(
            reduce_second_kernel, (4,),
            [
                (each, near_x), (each, near_y), (one(lambda s: jnp.minimum(s, 1)), from_y),
                (one(lambda s: jnp.maximum(s - 2, 0)), from_x),
            ],
            [(each, sds(near_x.shape, BRAIN))] * 2, micros=20, deps=deps,
        )

    def reduce_third(self, own, near_x, near_y, deps):
        from_x, from_y = self.swap(near_x, 1), self.swap(near_y, 2)
        block = own.shape[1:]
        return call(
            reduce_third_kernel, (1,),
            [(smem(), self.info)] + [(whole(v.shape), v) for v in (own, from_x, from_y)],
            [(whole(block), sds(block, BRAIN))] * 4,
            micros=20, deps=deps,
        )

    def reduce_fourth(self, first, second, others, deps):
        come = self.swap(others, 8)
        inputs = [(whole(v.shape), v) for v in (first, second, come)]
        outs = [(whole(first.shape), sds(first.shape, kind)) for kind in (FLOAT, BRAIN)]
        return call(reduce_fourth_kernel, (1,), inputs, outs, micros=20, deps=deps)

    def reduce_end(self, first, second):
        return first + self.swap(second, 4).astype(FLOAT)

    def reduce_direct(self, first, second, third, fourth, shapes, kernel=final_kernel, deps=()):
        pieces = [first, self.swap(second, 4), self.swap(third, 8), self.swap(fourth, 12)]
        inputs = [(whole(v.shape), v) for v in pieces]
        return call(kernel, (1,), inputs, [(whole(n), sds(n, FLOAT)) for n in shapes], deps=deps)

    def owner_rows(self, value):
        rows = value.shape[0] // 2
        mine = lax.dynamic_slice_in_dim(value, self.core * rows, rows, 0)
        theirs = lax.dynamic_slice_in_dim(value, (1 - self.core) * rows, rows, 0)
        return self.in_order(mine, core_swap(theirs), 1)


AXES = ("clip", "frame")


def body(
    clips, cores, clip_tokens, clip_class, output_grad, class_grad, clip_count,
    time_qkv, time_proj, time_vec, space_qkv, space_proj, space_vec, mlp_up, mlp_down, mlp_vec, mlp_bias,
):
    _, own, places_here, width = clip_tokens.shape
    rows = -(-(places_here + 1) // 16) * 16
    frames = own * cores
    wide = mlp_up.shape[1]
    cut = width // BLOCKS
    core = lax.axis_index("frame")
    place = lax.axis_index("clip")
    shard = place * cores + core
    leader = (core == 0).astype(jnp.int32)
    alive = (jnp.arange(1, dtype=jnp.int32) < clip_count[0]).astype(FLOAT)
    is_near = clips == 16 and cores == 2
    slot = core if is_near else core * 0
    info = jnp.stack([slot, leader, place // 4, place % 4, shard]).astype(jnp.int32)
    near = Near(clips, info) if is_near else None
    my_slot = info[0:1]
    far_slot = 1 - my_slot

    class_block = jnp.broadcast_to(clip_class[0][None, None], (own, 1, width))
    blank = jnp.zeros((own, rows - places_here - 1, width), BRAIN)
    tokens = jnp.concatenate([clip_tokens[0], class_block, blank], axis=1)
    last = (jnp.arange(own) == own - 1)[:, None, None]
    class_rows = jnp.where(last, class_grad[0][None, None], jnp.zeros((), BRAIN))
    grads = jnp.concatenate([output_grad[0], class_rows, blank], axis=1)

    bias_rows = wide // width
    zeros = jnp.zeros((8, width), FLOAT)
    flat = lambda v: v.reshape((own * rows,) + v.shape[2:])

    if near is not None:
        packed = (
            time_qkv, space_qkv, space_proj, time_proj, mlp_up, time_vec, space_vec, mlp_vec,
            mlp_bias.reshape(-1, bias_rows).T,
        )
        line = sds((time_qkv.shape[0], 6 * width + LANES), BRAIN)
        send, keep = call(
            pack_kernel, (1,), [(smem(), info)] + [(whole(v.shape), v) for v in packed],
            [(whole(line.shape), line), (whole(line.shape), line)],
        )
        shapes = [(cut, 3 * width // 2 + LANES), (cut, 5 * width // 2), (4 * cut, width)]
        time_own, space_own, mlp_own = call(
            join_kernel, (1,),
            [(smem(), info)] + [(whole(v.shape), v) for v in (keep, core_swap(send), mlp_down)],
            [(whole(shape), sds(shape, BRAIN)) for shape in shapes],
        )
        join = lambda two: tuple(h.reshape(width, h.shape[-1]) for h in two)
        time_line = near.depth_direct(time_own, [])
        far_tokens = core_swap(gate(tokens, [time_own]))
        space_own = gate(space_own, [time_line])
        space_line = near.depth_direct(space_own, [])
        time_mine = near.diagonal_step(time_line, near.plane_step(time_line, []), [grads, far_tokens, space_line])
        space_line = gate(space_line, [time_mine])
        time_far = core_swap(time_mine)
        time_w = join((time_mine, time_far))
        vec_block = pl.BlockSpec((width, LANES), lambda s: (0, time_w[0].shape[1] // LANES - 1))
        vectors = call(
            turn_kernel, (1,), [(vec_block, time_w[0])], [(whole((LANES, width)), sds((LANES, width), FLOAT))],
            deps=[space_line],
        )[0]
        n_vec = time_vec.shape[0] + space_vec.shape[0] + mlp_vec.shape[0]
        bias = vectors[n_vec : n_vec + bias_rows].T.reshape(bias_rows, width)
        mlp_own = gate(mlp_own, [time_mine])
        mix_deps = [space_line, mlp_own]
    else:
        everywhere = lax.all_gather(tokens, "frame", axis=0, tiled=True)
        far_tokens = jnp.roll(everywhere, -core * own, axis=0)[own:]
        vec_shard = jnp.concatenate([time_vec, space_vec, mlp_vec], axis=0)
        blank_rows = jnp.zeros((16 - vec_shard.shape[0], width), FLOAT)
        space_shard = jnp.concatenate([space_qkv, space_proj, time_proj], axis=1)
        vectors = lax.all_gather(vec_shard, AXES, axis=1, tiled=True).astype(FLOAT)
        bias = lax.all_gather(mlp_bias, AXES, axis=0, tiled=True).astype(FLOAT).reshape(bias_rows, width)
        vectors = jnp.concatenate([vectors, blank_rows], axis=0)

        def halves(value):
            full = lax.all_gather(value, AXES, axis=0, tiled=True)
            half = full.shape[1] // 2
            return full[:, :half], full[:, half:]

        time_w, space_w = halves(time_qkv), halves(space_shard)
        up = lax.all_gather(mlp_up, AXES, axis=0, tiled=True).reshape(BLOCKS, cut, 2, 2, width)
        up = jnp.transpose(up, (2, 0, 3, 1, 4)).reshape(2, BLOCKS, 2 * cut, width)
        down = lax.all_gather(mlp_down, AXES, axis=0, tiled=True).reshape(BLOCKS, 2, 2 * cut, width)
        mlp_w = tuple(
            (jnp.concatenate([up[n], down[:, n]], axis=1).reshape(4, BLOCKS // 4, 4 * cut, width),) for n in (0, 1)
        )
        mix_deps = []

    frame_shape = (own, rows, width)
    out_shape = (own, places_here, width)
    all_shape = (frames, rows, width)
    heads = width // HEAD_DIM
    prob_shape = (own, frames, rows, LANES)
    sprob_shape = (own, heads, rows, rows)
    mixed_shape = (own, rows, 3 * width)
    hidden_shape = (own, rows, wide)
    sum_out = (whole((8, width)), sds((8, width), FLOAT))
    row_bytes = own * rows * width
    square = 2 * own * rows * width * width
    group = 2 if own % 2 == 0 else 1
    frames_in = lambda array, first=0: (per_frame(array.shape, first, group), array)
    low_out = lambda shape, first=0: (per_frame(shape, first, group), sds(shape, BRAIN))
    wide_out = lambda shape, first=0: (per_frame(shape, first, group), sds(shape, FLOAT))
    vec_in = (whole(vectors.shape), vectors)
    pair = lambda two: [(hbm(), two[0]), (hbm(), two[1])]
    time_held = [pltpu.VMEM((width, 3 * width), BRAIN), pltpu.SemaphoreType.DMA((2,))]
    space_held = [pltpu.VMEM((width, 5 * width), BRAIN), pltpu.SemaphoreType.DMA((2,))]
    mlp_held = [
        pltpu.VMEM((wide // width, 4, BLOCKS // 4, cut, width), BRAIN),
        pltpu.VMEM((4, BLOCKS // 4, 2, 2 * cut, width), BRAIN),
        pltpu.SemaphoreType.DMA((2, 15)),
    ]

    own_map = pl.BlockSpec((group, rows, width), lambda s: (jnp.minimum(s, own // group - 1), 0, 0))
    far_map = pl.BlockSpec((group, rows, width), lambda s: (jnp.maximum(s - own // group, 0), 0, 0))
    queries, key_rows, value_rows, time_low = call(
        functools.partial(time_mix_kernel, own // group), (frames // group,),
        [(smem(), info), (own_map, tokens), (far_map, far_tokens), vec_in] + pair(time_w),
        [(own_map, sds(frame_shape, BRAIN)), low_out(all_shape), low_out(all_shape), (own_map, sds(frame_shape, BRAIN))],
        time_held, micros=1, deps=mix_deps,
    )

    if near is not None:
        mlp_line = near.depth_in_order(mlp_own, [queries])
        space_mine = near.diagonal_step(space_line, near.plane_step(space_line, [queries]), [mlp_line])
        space_w = join((space_mine, core_swap(space_mine)))
        mlp_line = gate(mlp_line, [space_mine])

    parts = [(0, own)]
    deps = [] if near is None else [mlp_line]
    kept, class_own = (), zeros
    for first, count in parts:
        outs = call(
            functools.partial(attention_kernel, places_here), (count // group,),
            [
                (smem(), info), frames_in(tokens, first), vec_in, frames_in(queries, first),
                (whole(all_shape), key_rows), (whole(all_shape), value_rows), (whole((8, width)), class_own),
            ]
            + pair(space_w),
            [
                low_out(prob_shape, first), low_out(frame_shape, first), wide_out(frame_shape, first),
                low_out(frame_shape, first), low_out(mixed_shape, first), low_out(sprob_shape, first),
                low_out(frame_shape, first), wide_out(frame_shape, first), sum_out,
            ],
            space_held, micros=27 * count / own, deps=deps, previous=kept,
        )
        kept, class_own = tuple(outs[:-1]), outs[-1]
        if near is not None and first == 0:
            mlp_planes = near.plane_step(mlp_line, [class_own])
            deps = list(mlp_planes[2:])
    time_prob, time_att, after, space_low, space_mixed, space_prob, space_att, places = kept

    if near is not None:
        rx, ry, sx, sy = mlp_planes
        mlp_first = tuple(gate(v, [sx, sy]) for v in (mlp_line, rx, ry))
        mlp_last = (near.swap(sx, 2), near.swap(sy, 1))
        mlp_w = (mlp_first + mlp_last, tuple(core_swap(v) for v in mlp_first) + tuple(core_swap(v) for v in mlp_last))
        class_far = core_swap(class_own)
    else:
        class_far = lax.psum(class_own, "frame") - class_own
    class_row = jnp.broadcast_to(clip_class.astype(FLOAT), (8, width))
    small = whole((8, width))
    result, class_result, mlp_low, hidden, feed_grad, before_grad, rows_grad, mlp_sums = call(
        functools.partial(mlp_kernel, places_here, frames, len(mlp_w[0])), (own // group,),
        [
            (smem(), info), (smem(), alive), frames_in(places), frames_in(grads),
            (small, class_row), (small, class_own), (small, class_far), vec_in, (whole(bias.shape), bias),
        ]
        + [(hbm(), v) for v in mlp_w[0] + mlp_w[1]],
        [
            low_out(out_shape), sum_out, low_out(frame_shape), low_out(hidden_shape), low_out(frame_shape),
            low_out(hidden_shape), wide_out(frame_shape), sum_out,
        ],
        [pltpu.VMEM((wide // width, group * rows, width), FLOAT)] + mlp_held,
        micros=25,
    )

    mlp_mine, mlp_far = mlp_outer(my_slot, flat(mlp_low), flat(before_grad), flat(hidden), flat(feed_grad))
    class_block_at = places_here // 16
    class_spec = pl.BlockSpec((1, 16, width), lambda s: (own - 1, class_block_at, 0))

    def space_back(first, count, sums, deps, previous):
        return call(
            functools.partial(space_back_kernel, places_here, frames), (count // group,),
            [
                (smem(), info), frames_in(rows_grad, first), (class_spec, rows_grad), frames_in(after, first),
                frames_in(space_mixed, first), frames_in(space_prob, first), frames_in(space_att, first),
                vec_in, (small, sums),
            ]
            + pair(space_w),
            [
                low_out(frame_shape, first), low_out(mixed_shape, first), wide_out(frame_shape, first),
                low_out(frame_shape, first), low_out(frame_shape, first), sum_out,
            ],
            space_held, micros=30 * count / own, deps=deps, previous=previous,
        )

    half = own // 2
    if near is not None:
        outs = space_back(0, half, zeros, [mlp_far], ())
        mlp_a, mlp_b, mlp_x, mlp_y, mlp_own = near.reduce_first(mlp_mine, core_swap(mlp_far), [outs[0]])
        outs = space_back(half, own - half, outs[-1], [mlp_a, mlp_b], tuple(outs[:-1]))
        mlp_x, mlp_y = near.reduce_second(mlp_x, mlp_y, mlp_a, mlp_b, [outs[0]])
        time_deps = [mlp_x, mlp_y]
    else:
        outs = space_back(0, own, zeros, [], ())
        time_deps = []
    branch_grad, space_mixed_grad, after_grad, time_grad, time_att_grad, space_sums = outs

    space_mine, space_far = space_outer(
        my_slot, *[flat(v) for v in (space_low, space_mixed_grad, space_att, branch_grad, time_att, time_grad)],
        deps=time_deps,
    )
    time_deps = time_deps + [space_far]
    far_frames = frames - own
    lanes_of = lambda shape: pl.BlockSpec(shape[:-1] + (2 * LANES,), lambda s: (0,) * (len(shape) - 1) + (s,))
    lanes_in = lambda v: (lanes_of(v.shape), v)
    q_grad, own_grad, far_grad = call(
        time_back_kernel, (width // LANES // 2,),
        [
            lanes_in(queries), lanes_in(key_rows), lanes_in(value_rows), (whole(prob_shape), time_prob),
            lanes_in(time_att_grad),
        ],
        [
            (lanes_of(shape), sds(shape, BRAIN))
            for shape in (frame_shape, (2,) + frame_shape, (2, far_frames, rows, width))
        ],
        micros=19, deps=time_deps,
    )
    if near is not None:
        from_far = core_swap(far_grad)
        mlp_first, mlp_second, *mlp_others = near.reduce_third(mlp_own, mlp_x, mlp_y, [q_grad])
        space_a, space_b, space_x, space_y, space_own = near.reduce_first(space_mine, core_swap(space_far), [mlp_second])
        mixed_deps = [space_own]
    else:
        mixed_deps = []
        padded = jnp.concatenate([jnp.zeros_like(own_grad), far_grad], axis=1)
        padded = jnp.roll(padded, core * own, axis=1)
        from_far = lax.psum_scatter(padded, "frame", scatter_dimension=1, tiled=True)
    pair_in = lambda v: (pl.BlockSpec((2, group, rows, width), lambda s: (0, s, 0, 0)), v)
    time_mixed_grad = call(
        mixed_grad_kernel, (own // group,), [frames_in(q_grad), pair_in(own_grad), pair_in(from_far)],
        [low_out(mixed_shape)], micros=3, deps=mixed_deps,
    )[0]
    outer = (flat(time_low), flat(time_mixed_grad))

    back_deps = []
    if near is not None:
        space_x, space_y = near.reduce_second(space_x, space_y, space_a, space_b, [time_mixed_grad])
        back_deps = [mlp_second, space_x, space_y]
    token_grad, time_sums = call(
        time_mix_back_kernel, (own // group,),
        [(smem(), info), frames_in(tokens), vec_in, frames_in(time_mixed_grad), frames_in(after_grad)]
        + pair(time_w),
        [wide_out(out_shape), sum_out],
        time_held, micros=4, deps=back_deps,
    )
    bias_grad = mlp_sums[3 : 3 + bias_rows].reshape(width, bias_rows)
    n_sums = 13
    sums = call(
        sums_kernel, (1,), [(small, time_sums), (small, space_sums), (small, mlp_sums), (whole(bias_grad.shape), bias_grad)],
        [(whole((width, LANES)), sds((width, LANES), FLOAT))], [pltpu.VMEM((LANES, width), FLOAT)],
    )[0]

    if near is not None:
        up_rows, grad_mlp_down = near.reduce_direct(
            mlp_first, mlp_second, *mlp_others, [(cut, 2 * width), (2 * cut, width)], final_mlp_kernel, [token_grad]
        )
        space_parts = near.reduce_third(space_own, space_x, space_y, [up_rows])
        time_mine, time_far = time_outer(my_slot, *outer, sums, deps=[space_parts[1]])
        time_a, time_b, time_x, time_y, time_own = near.reduce_first(time_mine, core_swap(time_far), [])
        time_x, time_y = near.reduce_second(time_x, time_y, time_a, time_b, [])
        time_parts = near.reduce_third(time_own, time_x, time_y, [])
        half = cut // 2
        space_grads = near.reduce_direct(*space_parts, [(half, 3 * width), (half, width), (half, width)])
        vec_shapes = [(v.shape[0], half) for v in (time_vec, space_vec, mlp_vec)]
        grad_time, grad_time_vec, grad_space_vec, grad_mlp_vec, bias_rows_grad = near.reduce_direct(
            *time_parts, [(half, 3 * width)] + vec_shapes + [(half, bias_rows)], final_time_kernel
        )
        grad_mlp_bias = bias_rows_grad.reshape(-1)
        grad_mlp_up = near.owner_rows(up_rows)
        class_total = space_sums[6:7] + core_swap(space_sums)[6:7]
    else:
        send = lambda v: lax.psum_scatter(v, AXES, scatter_dimension=0, tiled=True).astype(FLOAT)
        spread = lambda mine, far: jnp.stack([mine, far], axis=1).reshape(width, mine.shape[2])
        time_mine, time_far = time_outer(my_slot, *outer, sums)
        up = jnp.stack([v[:, : 2 * cut].reshape(BLOCKS, 2, cut, width) for v in (mlp_mine, mlp_far)])
        grad_mlp_up = send(jnp.transpose(up, (1, 3, 0, 2, 4)).reshape(width, wide))
        grad_mlp_down = send(jnp.stack([v[:, 2 * cut :] for v in (mlp_mine, mlp_far)], axis=1).reshape(wide, width))
        grad_space = send(spread(space_mine, space_far))
        space_grads = (grad_space[:, : 3 * width], grad_space[:, 3 * width : 4 * width], grad_space[:, 4 * width :])
        grad_time = send(spread(time_mine, time_far)[:, : 3 * width])
        class_total = lax.psum(space_sums[6:7], "frame")
        step = width // (clips * cores)
        sums = lax.dynamic_slice_in_dim(lax.psum(sums, AXES), shard * step, step, 0)
        lines = sums.T
        grad_time_vec, grad_space_vec, grad_mlp_vec = lines[:5], lines[5:10], lines[10:13]
        grad_mlp_bias = sums[:, n_sums : n_sums + bias_rows].reshape(-1)
    class_in_grad = rows_grad[own - 1, places_here][None] + class_total
    return (
        result[None],
        class_result[places_here % 8][None].astype(BRAIN),
        token_grad[None],
        class_in_grad,
        grad_time,
        space_grads[2],
        grad_time_vec,
        space_grads[0],
        space_grads[1],
        grad_space_vec,
        grad_mlp_up,
        grad_mlp_down,
        grad_mlp_vec,
        grad_mlp_bias,
    )


def solution(mesh):
    both = ("clip", "frame")
    rows = P(both, None)
    columns = P(None, both)
    weights = (rows, rows, columns, rows, rows, columns, rows, rows, columns, P(both))
    block = P("clip", "frame", None, None)
    classes = P("clip", None)
    return jax.shard_map(
        functools.partial(body, mesh.shape["clip"], mesh.shape["frame"]),
        mesh=mesh,
        in_specs=(block, classes, block, classes, P("clip")) + weights,
        out_specs=(block, classes, block, classes) + weights,
        check_vma=False,
    )
```
